32 devices in a mesh: crops: 8 (over z, x), rows: 4 (over y, core).
Axes of the slice: x: 2, y: 2, z: 4, core: 2. Of those that a mesh axis runs over, the one named last changes fastest.
Arguments:
- features: bfloat16 [640, 8, 8, 2048], P('crops', 'rows'), may hold values from -6 to 6
- pixel_mask: int32 [640, 8, 8], P('crops', 'rows'), may hold values from 0 to 1, as said below
- partners: int32 [640], P('crops'), may hold values from 0 to 639, as said below
- queued: float32 [3840, 128], P(('crops', 'rows')), as said below
- w_reduce: bfloat16 [2048, 512], P('crops'), may hold values from -0.125 to 0.125
- w_spatial: bfloat16 [4608, 512], P('crops'), may hold values from -0.09375 to 0.09375
- w_expand: bfloat16 [512, 2048], P('crops'), may hold values from -0.25 to 0.25
- w_hidden: bfloat16 [2048, 2048], P('crops'), may hold values from -0.125 to 0.125
- w_embed: bfloat16 [2048, 128], P('crops'), may hold values from -0.125 to 0.125
- prototypes: float32 [128, 3000], replicated, may hold values from -0.75 to 0.75
- gain_one: float32 [512], replicated, may hold values from 0.1 to 1.9
- bias_one: float32 [512], replicated, may hold values from -2.5 to 2.5
- gain_two: float32 [512], replicated, may hold values from 0.1 to 1.9
- bias_two: float32 [512], replicated, may hold values from -2.5 to 2.5
- gain_three: float32 [2048], replicated, may hold values from 0.1 to 1.9
- bias_three: float32 [2048], replicated, may hold values from -2.5 to 2.5
- gain_head: float32 [2048], replicated, may hold values from 0.1 to 1.9
- bias_head: float32 [2048], replicated, may hold values from -2.5 to 2.5
Outputs:
- swav_loss: float32 [], replicated
- grad_features: bfloat16 [640, 8, 8, 2048], P('crops', 'rows')
- grad_w_reduce: float32 [2048, 512], P('crops')
- grad_w_spatial: float32 [4608, 512], P('crops')
- grad_w_expand: float32 [512, 2048], P('crops')
- grad_w_hidden: float32 [2048, 2048], P('crops')
- grad_w_embed: float32 [2048, 128], P('crops')
- grad_prototypes: float32 [128, 3000], replicated
- grad_gain_one: float32 [512], replicated
- grad_bias_one: float32 [512], replicated
- grad_gain_two: float32 [512], replicated
- grad_bias_two: float32 [512], replicated
- grad_gain_three: float32 [2048], replicated
- grad_bias_three: float32 [2048], replicated
- grad_gain_head: float32 [2048], replicated
- grad_bias_head: float32 [2048], replicated
The draws below stay inside these ranges and needn't reach their ends.
Inputs may be any that keep to these rules, and one draw needn't show every extreme that they name: `pixel_mask`: each crop's valid pixels form one rectangle of 7 x 7 or 6 x 8 pixels inside its map. partners[n] != n, partners[partners[n]] == n, and n and partners[n] lie in the same aligned block of 80 crops. `queued`: every row has a nonzero entry.
All inputs are finite; a program needn't handle non-finite values.
Results may differ from the reference program's by a relative error of at most 0.012.
Values may be sent and summed in bfloat16 or wider, within the bound.
No kernel may reach another device: no remote copies, remote signals or barrier semaphores. Data moves between devices by JAX's collectives and lax.ppermute only.
A program may use at most 192 MiB of HBM per device.

```python
import math
import jax
import jax.numpy as jnp
from jax import lax

D = 2048
MID = 512
HID = 2048
PROJ = 128
PROTOS = 3000
QUEUE = 3840
SIDE = 8
C_DEV = 80
CROPS = 640


def draw_pixel_mask(key, part):
    subkeys = jax.random.split(key, 3)
    bucket = jax.random.randint(subkeys[0], (CROPS,), 0, 2)
    row_draw = jax.random.randint(subkeys[1], (CROPS,), 0, 6)
    col_draw = jax.random.randint(subkeys[2], (CROPS,), 0, 2)
    top_row = (row_draw % (2 + bucket))[:, None, None]
    left_col = (col_draw * (1 - bucket))[:, None, None]
    tall = (7 - bucket)[:, None, None]
    wide = (7 + bucket)[:, None, None]
    rows_at = jnp.arange(SIDE, dtype=jnp.int32)[None, :, None]
    cols_at = jnp.arange(SIDE, dtype=jnp.int32)[None, None, :]
    inside = (rows_at >= top_row) & (rows_at < top_row + tall) & (cols_at >= left_col) & (cols_at < left_col + wide)
    return inside.astype(jnp.int32)


def draw_partners(key, part):
    block_total = CROPS // C_DEV
    subkeys = jax.random.split(key, block_total)

    def match_block(block_key, start):
        shuffled = jax.random.permutation(block_key, C_DEV).astype(jnp.int32)
        swapped = shuffled.reshape(-1, 2)[:, ::-1].reshape(-1)
        return jnp.zeros((C_DEV,), jnp.int32).at[shuffled].set(swapped) + start
    starts = jnp.arange(block_total, dtype=jnp.int32) * C_DEV
    return jax.vmap(match_block)(subkeys, starts).reshape(-1)


def draw_queued(key, part):
    subkeys = jax.random.split(jax.random.fold_in(key, 17), 2)
    directions = jax.random.normal(subkeys[0], (16, PROJ), jnp.float32)
    along = jnp.repeat(directions, QUEUE // 16, axis=0)
    position = jnp.arange(QUEUE, dtype=jnp.float32) / QUEUE
    noise = jax.random.normal(subkeys[1], (QUEUE, PROJ), jnp.float32)
    strength = 0.3 + 2.7 * position
    return noise + strength[:, None] * along


def shard_levels(rng, extent, cuts, smallest, largest):
    level = 1.0
    for dim, parts in cuts:
        draws = jax.random.uniform(jax.random.fold_in(jax.random.fold_in(rng, 6), dim), (parts,), jnp.float32, smallest / len(cuts), largest / len(cuts))
        level = level * jnp.repeat(jnp.exp(draws), extent[dim] // parts).reshape((-1,) + (1,) * (len(extent) - 1 - dim))
    return level


def normal_values(stream_key, shape, deviation, reach, cuts=(), kind=jnp.bfloat16):
    factor_of = shard_levels(stream_key, shape, cuts, -0.22, 0.18) if cuts else 1.0
    values = jax.random.normal(stream_key, shape, jnp.float32) * deviation * factor_of
    return jnp.minimum(jnp.maximum(values, -reach), reach).astype(kind)


def setup_inputs(seed: int = 0) -> dict:
    arg_keys = jax.random.split(jax.random.key(seed), 19)
    return {
        "features": normal_values(arg_keys[0], (CROPS, SIDE, SIDE, D), 1.0, 6.0, ((0, 8), (1, 4))),
        "pixel_mask": draw_pixel_mask(jax.random.fold_in(arg_keys[18], 71), 0),
        "partners": draw_partners(jax.random.fold_in(arg_keys[18], 71), 0),
        "queued": draw_queued(jax.random.fold_in(arg_keys[18], 71), 0),
        "w_reduce": normal_values(arg_keys[4], (D, MID), D ** -0.5, 0.125, ((0, 8),)),
        "w_spatial": normal_values(arg_keys[5], (9 * MID, MID), (9 * MID) ** -0.5, 0.09375, ((0, 8),)),
        "w_expand": normal_values(arg_keys[6], (MID, D), MID ** -0.5, 0.25, ((0, 8),)),
        "w_hidden": normal_values(arg_keys[7], (D, HID), D ** -0.5, 0.125, ((0, 8),)),
        "w_embed": normal_values(arg_keys[8], (HID, PROJ), HID ** -0.5, 0.125, ((0, 8),)),
        "prototypes": normal_values(arg_keys[9], (PROJ, PROTOS), (PROJ // 2) ** -0.5, 0.75, (), jnp.float32),
        "gain_one": jnp.clip(1.0 + 0.18 * jax.random.normal(arg_keys[10], (MID,), jnp.float32), 0.1, 1.9),
        "bias_one": normal_values(arg_keys[11], (MID,), 0.5, 2.5, (), jnp.float32),
        "gain_two": jnp.clip(1.0 + 0.18 * jax.random.normal(arg_keys[12], (MID,), jnp.float32), 0.1, 1.9),
        "bias_two": normal_values(arg_keys[13], (MID,), 0.5, 2.5, (), jnp.float32),
        "gain_three": jnp.clip(1.0 + 0.18 * jax.random.normal(arg_keys[14], (D,), jnp.float32), 0.1, 1.9),
        "bias_three": normal_values(arg_keys[15], (D,), 0.5, 2.5, (), jnp.float32),
        "gain_head": jnp.clip(1.0 + 0.18 * jax.random.normal(arg_keys[16], (HID,), jnp.float32), 0.1, 1.9),
        "bias_head": normal_values(arg_keys[17], (HID,), 0.5, 2.5, (), jnp.float32),
    }


@jax.custom_vjp
def low(v):
    return lax.optimization_barrier(v.astype(jnp.bfloat16)).astype(jnp.float32)

@jax.custom_vjp
def low_back(v):
    return v

def low_keep(v):
    return (low(v), None)

def low_pass(kept, grad):
    return (grad,)

def back_keep(v):
    return (v, None)

def back_low(kept, grad):
    return (low(grad),)
low.defvjp(low_keep, low_pass)
low_back.defvjp(back_keep, back_low)
EPS_NORM = 1e-05
EPS_UNIT = 1e-06
SHARPNESS = 0.05
SOFTMAX_TEMPER = 0.1
PRECISE = lax.Precision.HIGHEST

def column_stats(value_entries, weights):
    valid_count = jnp.sum(weights)
    col_mean = lax.optimization_barrier(jnp.sum(value_entries * weights, axis=0)) / valid_count
    second_sum = lax.optimization_barrier(jnp.sum(value_entries * value_entries * weights, axis=0)) / valid_count
    return (col_mean, lax.rsqrt(second_sum - col_mean * col_mean + EPS_NORM))

def mapped_dot(value_entries, matrix, group_count):
    stacked = value_entries.reshape(group_count, -1, value_entries.shape[-1])
    result = lax.map(jax.checkpoint(lambda piece: jnp.dot(piece, matrix, precision=PRECISE)), stacked)
    return result.reshape(-1, matrix.shape[1])

def spatial_group(hidden_grid, w_spatial):
    height, breadth = (hidden_grid.shape[1], hidden_grid.shape[2])
    padded = jnp.pad(hidden_grid, ((0, 0), (1, 1), (1, 1), (0, 0)))
    pieces = [padded[:, tap_row:tap_row + height, tap_col:tap_col + breadth, :] for tap_row in range(3) for tap_col in range(3)]
    columns = jnp.concatenate(pieces, axis=-1).reshape(-1, 9 * hidden_grid.shape[3])
    return jnp.dot(columns, w_spatial, precision=PRECISE)

def forward(inputs, valid, queued, w_reduce, w_spatial, w_expand, w_hidden, w_embed, prototypes, gain_one, bias_one, gain_two, bias_two, gain_three, bias_three, gain_head, bias_head):
    total_crops, height, breadth, channels = inputs.shape
    group_count = total_crops // math.gcd(total_crops, 64)
    weights = valid.reshape(-1, 1)
    flat_in = (inputs * valid[..., None]).reshape(-1, channels)
    pre_one = low_back(mapped_dot(flat_in, w_reduce, group_count))
    mean_one, spread_one = column_stats(pre_one, weights)
    hidden_one = low(jax.nn.gelu(gain_one * ((pre_one - mean_one) * spread_one) + bias_one) * weights)
    grid_one = hidden_one.reshape(group_count, -1, height, breadth, hidden_one.shape[1])
    pre_two = lax.map(jax.checkpoint(lambda piece: spatial_group(piece, w_spatial)), grid_one).reshape(-1, w_spatial.shape[1])
    pre_two = low_back(pre_two)
    mean_two, spread_two = column_stats(pre_two, weights)
    hidden_two = low(jax.nn.gelu(gain_two * ((pre_two - mean_two) * spread_two) + bias_two) * weights)
    pre_three = low_back(mapped_dot(hidden_two, w_expand, group_count))
    mean_three, spread_three = column_stats(pre_three, weights)

    def pool_group(pieces):
        value_entries, residual, piece_weights = pieces
        summed = gain_three * ((value_entries - mean_three) * spread_three) + bias_three + residual
        output = jax.nn.gelu(summed) * piece_weights
        return lax.optimization_barrier(jnp.sum(output.reshape(-1, height * breadth, channels), axis=1))
    stacked = (pre_three.reshape(group_count, -1, channels), flat_in.reshape(group_count, -1, channels), weights.reshape(group_count, -1, 1))
    pooled_sum = lax.map(jax.checkpoint(pool_group), stacked).reshape(total_crops, channels)
    crop_count = lax.optimization_barrier(jnp.sum(valid.reshape(total_crops, -1), axis=1))
    pooled = pooled_sum / crop_count[:, None]
    pre_head = jnp.dot(pooled, w_hidden, precision=PRECISE)
    mean_head, spread_head = column_stats(pre_head, jnp.ones((total_crops, 1), pre_head.dtype))
    hidden_head = jax.nn.gelu(gain_head * ((pre_head - mean_head) * spread_head) + bias_head)
    embedding = jnp.dot(hidden_head, w_embed, precision=PRECISE)
    unit_embed = embedding * lax.rsqrt(lax.optimization_barrier(jnp.sum(embedding * embedding, axis=1, keepdims=True)) + EPS_UNIT)
    centroid_similarity = jnp.dot(unit_embed, prototypes, precision=PRECISE)
    queue_unit = queued * lax.rsqrt(lax.optimization_barrier(jnp.sum(queued * queued, axis=1, keepdims=True)) + EPS_UNIT)
    stored_similarity = jnp.dot(queue_unit, prototypes, precision=PRECISE)
    return (centroid_similarity, stored_similarity)

def balanced_transport_solver(centroid_similarity, stored_similarity):
    plan_mass = jnp.exp(centroid_similarity / SHARPNESS)
    queue_mass = jnp.exp(stored_similarity / SHARPNESS)
    row_total = centroid_similarity.shape[0] + stored_similarity.shape[0]
    proto_total = centroid_similarity.shape[1]
    for iteration in range(3):
        column = lax.optimization_barrier(jnp.sum(plan_mass, axis=0)) + lax.optimization_barrier(jnp.sum(queue_mass, axis=0))
        plan_mass = plan_mass / (proto_total * column)
        queue_mass = queue_mass / (proto_total * column)
        plan_mass = plan_mass / (row_total * lax.optimization_barrier(jnp.sum(plan_mass, axis=1, keepdims=True)))
        queue_mass = queue_mass / (row_total * lax.optimization_barrier(jnp.sum(queue_mass, axis=1, keepdims=True)))
    return row_total * plan_mass

def reference(features, pixel_mask, partners, queued, w_reduce, w_spatial, w_expand, w_hidden, w_embed, prototypes, gain_one, bias_one, gain_two, bias_two, gain_three, bias_three, gain_head, bias_head):
    valid = pixel_mask.astype(jnp.float32)
    floats = (features.astype(jnp.float32), w_reduce.astype(jnp.float32), w_spatial.astype(jnp.float32), w_expand.astype(jnp.float32), w_hidden.astype(jnp.float32), w_embed.astype(jnp.float32), prototypes, gain_one, bias_one, gain_two, bias_two, gain_three, bias_three, gain_head, bias_head)

    def objective(*pieces):
        return forward(pieces[0], valid, queued, *pieces[1:])
    (centroid_similarity, stored_similarity), pull_back = jax.vjp(objective, *floats)
    balanced_cluster_labels = balanced_transport_solver(centroid_similarity, stored_similarity)
    swapped_cluster_labels = jnp.take(balanced_cluster_labels, partners, axis=0)

    def objective_loss(value_entries):
        return -jnp.sum(swapped_cluster_labels * jax.nn.log_softmax(value_entries / SOFTMAX_TEMPER, axis=1)) / value_entries.shape[0]
    swav_loss, loss_back = jax.vjp(objective_loss, centroid_similarity)
    derivs = pull_back((loss_back(jnp.ones_like(swav_loss))[0], jnp.zeros_like(stored_similarity)))
    return (swav_loss, derivs[0].astype(jnp.bfloat16), derivs[1], derivs[2], derivs[3], derivs[4], derivs[5], derivs[6], derivs[7], derivs[8], derivs[9], derivs[10], derivs[11], derivs[12], derivs[13], derivs[14])
```

```python
import functools
import math

import jax
import jax.numpy as jnp
from jax import lax
from jax.experimental import pallas as pl
from jax.experimental.pallas import tpu as pltpu
from jax.sharding import PartitionSpec as P

EPS_NORM = 1e-05
EPS_UNIT = 1e-06
SHARPNESS = 0.05
SOFTMAX_TEMPER = 0.1
PRECISE = lax.Precision.HIGHEST
BOTH = ("crops", "rows")
GELU_SCALE = 0.7978845608028654
GELU_CUBE = 0.044715
F32 = jnp.float32
BF16 = jnp.bfloat16


def bits_of(axis):
    return [1 << k for k in range(lax.axis_size(axis).bit_length() - 1)]


def xor_permute(values, crop_xor, row_xor):
    crop_total, row_total = lax.axis_size("crops"), lax.axis_size("rows")
    pairs = [
        (c * row_total + r, (c ^ crop_xor) * row_total + (r ^ row_xor))
        for c in range(crop_total)
        for r in range(row_total)
    ]
    return lax.ppermute(values, BOTH, pairs)


def all_bits():
    return [(0, b) for b in bits_of("rows")] + [(b, 0) for b in bits_of("crops")]


def total_wide(values):
    steps = all_bits()
    groups = [steps[:1]] + [steps[k : k + 2] for k in range(1, len(steps), 2)]
    for group in groups:
        if len(group) == 1:
            values = values + xor_permute(values, *group[0])
        else:
            (a, b), (c, d) = group
            near = xor_permute(values, a, b)
            far = xor_permute(values, c, d)
            both = xor_permute(values, a ^ c, b ^ d)
            values = (values + near) + (far + both)
    return values


def total_carrying(values, rows_extra):
    width, own = values.shape[1], rows_extra.reshape(1, -1)
    slots = {0: own}
    steps = all_bits()
    groups = [steps[:1]] + [steps[k : k + 2] for k in range(1, len(steps), 2)]

    def send(step, current):
        if step[0]:
            return xor_permute(current, *step), {}
        keys = sorted(slots)
        got = xor_permute(jnp.concatenate([current] + [slots[k] for k in keys], axis=1), *step)
        parts = jnp.split(got[:, width:], len(keys), axis=1)
        return got[:, :width], {k ^ step[1]: part for k, part in zip(keys, parts)}

    for group in groups:
        if len(group) == 1:
            other, more = send(group[0], values)
            values = values + other
            slots.update(more)
        else:
            (a, b), (c, d) = group
            near, near_slots = send((a, b), values)
            far, far_slots = send((c, d), values)
            both, both_slots = send((a ^ c, b ^ d), values)
            values = (values + near) + (far + both)
            for more in (near_slots, far_slots, both_slots):
                slots.update(more)
    stacked = jnp.concatenate([slots[k] for k in sorted(slots)], axis=0)
    return values, stacked.reshape(-1, rows_extra.shape[1])


def after(values, *earlier):
    return lax.optimization_barrier((values,) + earlier)[0]


def total_narrow(values):
    count = lax.axis_size("crops") * lax.axis_size("rows")
    copies = jnp.broadcast_to(values[None], (count,) + values.shape)
    return jnp.sum(lax.all_to_all(copies, BOTH, 0, 0, tiled=True), axis=0)


def my_bit(step):
    crop_xor, row_xor = step
    if crop_xor:
        return (lax.axis_index("crops") // crop_xor) % 2
    return (lax.axis_index("rows") // row_xor) % 2


def halve(values, dim, step, narrow):
    bit = my_bit(step)
    kept = lax.dynamic_index_in_dim(values, bit, dim, keepdims=False)
    sent = lax.dynamic_index_in_dim(values, 1 - bit, dim, keepdims=False)
    if narrow:
        sent = sent.astype(BF16)
    return kept.astype(F32) + xor_permute(sent, *step).astype(F32)


def double(values, step):
    other = xor_permute(values, *step)
    low = my_bit(step) == 0
    return jnp.stack([jnp.where(low, values, other), jnp.where(low, other, values)])


def swap_sum(values, dims, bits):
    crop_total, row_total = lax.axis_size("crops"), lax.axis_size("rows")
    crop_mask, row_mask = sum(b for b, _ in bits), sum(b for _, b in bits)
    groups = {}
    for c in range(crop_total):
        for r in range(row_total):
            groups.setdefault((c & ~crop_mask, r & ~row_mask), []).append(c * row_total + r)
    front = [k for k, step in enumerate(dims) if step in bits]
    rest = [k for k in range(values.ndim) if k not in front]
    values = values.transpose(front + rest)
    values = values.reshape((2 ** len(bits),) + values.shape[len(bits) :]).astype(BF16)
    values = lax.all_to_all(
        values, BOTH, 0, 0, axis_index_groups=list(groups.values()), tiled=True
    )
    return jnp.sum(values.astype(F32), axis=0), [step for step in dims if step not in bits]


def gather_rows(values):
    row_bits = [(0, b) for b in bits_of("rows")]
    count = len(row_bits)
    rows, cols = values.shape
    for step in reversed(row_bits):
        values = double(values, step)
    values = values.transpose(tuple(range(count - 1, -1, -1)) + (count, count + 1))
    return values.reshape(-1, cols)


def reduce_stages(values):
    row_bits = [(0, b) for b in reversed(bits_of("rows"))]
    crop_bits = [(b, 0) for b in reversed(bits_of("crops"))]
    dims = crop_bits + row_bits
    rows, cols = values.shape
    values = values.reshape((2,) * len(dims) + (rows >> len(dims), cols))
    values = halve(values, len(dims) - 1, dims[-1], True)
    yield values
    values, dims = swap_sum(values, dims[:-1], row_bits[:-1] + crop_bits[-1:])
    yield values
    values, dims = swap_sum(values, dims, list(dims))
    yield values
    yield gather_rows(values.astype(BF16)).astype(F32)


def row_quarter(weight):
    size = weight.shape[0] // lax.axis_size("rows")
    return lax.dynamic_slice_in_dim(weight, lax.axis_index("rows") * size, size)


def gather_first(weight):
    crop_total = lax.axis_size("crops")
    size, cols = weight.shape[0] // 2, weight.shape[1]
    bit = lax.axis_index("rows") % 2
    mine = lax.dynamic_slice_in_dim(weight, bit * size, size)
    mine = lax.all_to_all(
        jnp.broadcast_to(mine[None], (crop_total, size, cols)), "crops", 0, 0, tiled=True
    )
    other = xor_permute(mine, 0, 1)
    low = bit == 0
    both = jnp.stack([jnp.where(low, mine, other), jnp.where(low, other, mine)], axis=1)
    return both.reshape(2 * crop_total * size, cols)


def gather_pair(first, second):
    quarter_one, quarter_two = row_quarter(first), row_quarter(second)
    cols = first.shape[1]
    blocks = second.shape[1] // cols
    size, short = quarter_one.shape[0], quarter_two.shape[0]
    flat_two = quarter_two.reshape(short, blocks, cols).transpose(1, 0, 2).reshape(-1, cols)
    whole = lax.all_gather(jnp.concatenate([quarter_one, flat_two], axis=0), BOTH, axis=0, tiled=False)
    count = whole.shape[0]
    second_blocks = whole[:, size:].reshape(count, blocks, short, cols).transpose(1, 0, 2, 3)
    if size % 16:
        whole, size = whole[:, :size].reshape(1, -1, cols), count * size
    return (whole, size), second_blocks.reshape(blocks, -1, cols)


def gather_products(left, right):
    mean = jnp.mean(left, axis=0, keepdims=True)
    total = jnp.sum(right, axis=0, keepdims=True)
    mean_high, total_high = lax.reduce_precision(mean, 8, 7), lax.reduce_precision(total, 8, 7)
    mean_low, total_low = mean - mean_high, total - total_high
    left = jnp.concatenate([left - mean, mean_high, mean_high, mean_low, mean_low], axis=0)
    right = jnp.concatenate([right, total_high, total_low, total_high, total_low], axis=0)
    return (
        lax.all_gather(left.astype(BF16), BOTH, axis=0, tiled=True),
        lax.all_gather(right.astype(BF16), BOTH, axis=0, tiled=True),
    )


def spread_of(sums, count):
    mean = sums[0] / count
    return mean, lax.rsqrt(sums[1] / count - mean * mean + EPS_NORM)


def gelu_both(x, mask=None):
    square = x * x
    half = 0.5 * jnp.tanh(x * (GELU_SCALE + GELU_SCALE * GELU_CUBE * square)) + 0.5
    inner = x * (2.0 * GELU_SCALE + 6.0 * GELU_SCALE * GELU_CUBE * square)
    kept = half if mask is None else half * mask
    return x * kept, kept * (1.0 + (1.0 - half) * inner)


def split_parts(x, parts):
    pieces = []
    for _ in range(parts - 1):
        piece = lax.reduce_precision(x, 8, 7)
        pieces.append(piece.astype(BF16))
        x = x - piece
    pieces.append(x.astype(BF16))
    return jnp.concatenate(pieces, axis=0)


def split_dot(x, matrix, dim, parts):
    count = x.shape[0]
    out = lax.dot_general(
        split_parts(x, parts), matrix, (((1,), (dim,)), ((), ())), preferred_element_type=F32
    )
    total = out[(parts - 1) * count :]
    for k in range(parts - 2, -1, -1):
        total = total + out[k * count : (k + 1) * count]
    return total


TN = (((0,), (0,)), ((), ()))
NT = (((1,), (1,)), ((), ()))
TILE = 16
UNROLL = 16


def kernel_call(body, grid, ins, outs, scratch, args, flops, transcendentals=0):
    moved = sum(a.size * a.dtype.itemsize for a in args) + sum(
        math.prod(s.shape) * s.dtype.itemsize for s, _ in outs
    )
    return pl.pallas_call(
        body,
        grid=(grid,),
        in_specs=ins,
        out_specs=[spec for _, spec in outs],
        out_shape=[shape for shape, _ in outs],
        scratch_shapes=scratch,
        compiler_params=pltpu.CompilerParams(vmem_limit_bytes=52 * 2**20),
        cost_estimate=pl.CostEstimate(
            flops=flops, bytes_accessed=moved, transcendentals=transcendentals
        ),
    )(*args)


def whole_block(array):
    zeros = (0,) * array.ndim
    return pl.BlockSpec(array.shape, lambda k: zeros)


def spatial_block(weight):
    array, size = weight
    return pl.BlockSpec((array.shape[0], size, array.shape[2]), lambda k: (0, 0, 0))


def sum_block(width):
    return jax.ShapeDtypeStruct((8, width), F32), pl.BlockSpec((8, width), lambda k: (0, 0))


def tall(row):
    return jnp.broadcast_to(row.reshape(1, -1), (TILE, row.size))


def fold(values):
    return values[:8] + values[8:]


def loop(count, step, start):
    return lax.fori_loop(0, count, step, start, unroll=math.gcd(count, UNROLL))


def clear_first(*refs):
    @pl.when(pl.program_id(0) == 0)
    def _():
        for ref in refs:
            ref[...] = jnp.zeros_like(ref)


def planes_of(height, width, rows):
    return pl.BlockSpec((height, rows, width), lambda k: (0, k, 0))


def gather_tile(ref, index, height):
    if height == 1:
        return ref[0, pl.ds(pl.multiple_of(index * TILE, TILE), TILE), :]
    return jnp.concatenate(
        [ref[i, pl.ds(pl.multiple_of(index * 8, 8), 8), :] for i in range(height)], axis=0
    )


def store_tile(ref, index, values, height):
    if height == 1:
        ref[0, pl.ds(pl.multiple_of(index * TILE, TILE), TILE), :] = values
    else:
        for i in range(height):
            ref[i, pl.ds(pl.multiple_of(index * 8, 8), 8), :] = values[8 * i : 8 * i + 8]


def tile_rows(index):
    return pl.ds(pl.multiple_of(index * TILE, TILE), TILE)


def first_body(height, x_ref, m_ref, c_ref, hidden_ref, slope_ref, sum_ref):
    clear_first(sum_ref)
    pairs = x_ref.shape[0] // 2
    width = x_ref.shape[3]
    for i in range(height):

        def step(k, carry):
            x = x_ref[pl.ds(pl.multiple_of(2 * k, 2), 2), i].reshape(TILE, width)
            m = m_ref[i, tile_rows(k), :]
            value, slope = gelu_both(c_ref[:TILE] * x + c_ref[TILE:], m)
            hidden = value.astype(BF16)
            hidden_ref[i, tile_rows(k), :] = hidden
            slope_ref[i, tile_rows(k), :] = slope
            return carry + fold(hidden.astype(F32))

        sum_ref[...] += loop(pairs, step, jnp.zeros(sum_ref.shape, F32))


def first_hidden(pre_one, mask_planes, scale, shift):
    crops, height, breadth, width = pre_one.shape
    tile = 16
    consts = jnp.concatenate([tall(scale), tall(shift)], axis=0)
    planes = planes_of(height, width, tile * 8)
    hidden, slope, sums = kernel_call(
        functools.partial(first_body, height),
        crops // tile,
        [
            pl.BlockSpec((tile, height, 8, width), lambda k: (k, 0, 0, 0)),
            planes_of(height, 1, tile * 8),
            whole_block(consts),
        ],
        [
            (jax.ShapeDtypeStruct((height, crops * 8, width), BF16), planes),
            (jax.ShapeDtypeStruct((height, crops * 8, width), F32), planes),
            sum_block(width),
        ],
        [],
        (pre_one, mask_planes, consts),
        40 * pre_one.size,
        pre_one.size,
    )
    return hidden, slope, jnp.sum(sums, axis=0)


def shifted(values, back):
    wide = values.astype(F32).reshape(2, 8, values.shape[1])
    place = lax.broadcasted_iota(jnp.int32, wide.shape, 1)
    before = jnp.where(place == 0, 0.0, pltpu.roll(wide, 1, 1)).reshape(values.shape).astype(BF16)
    after = jnp.where(place == 7, 0.0, pltpu.roll(wide, 7, 1)).reshape(values.shape).astype(BF16)
    return (after, before) if back else (before, after)


def fill_taps(read, out_ref, back):
    width = out_ref.shape[1] // 3

    def step(k, carry):
        values = read(k)
        low, high = shifted(values, back)
        out_ref[tile_rows(k), :width] = low
        out_ref[tile_rows(k), width : 2 * width] = values
        out_ref[tile_rows(k), 2 * width :] = high
        return carry

    loop(out_ref.shape[0] // TILE, step, 0)


def tap_dot(taps, w_ref, tap_row, back):
    width = taps.shape[1] // 3
    w_ref = w_ref.reshape(w_ref.shape[0] * w_ref.shape[1], w_ref.shape[2])
    if not back:
        return jnp.dot(
            taps, w_ref[3 * width * tap_row : 3 * width * (tap_row + 1), :], preferred_element_type=F32
        )
    total = None
    for b in range(3):
        at = (3 * tap_row + b) * width
        part = lax.dot_general(
            taps[:, b * width : (b + 1) * width],
            w_ref[at : at + width, :],
            NT,
            preferred_element_type=F32,
        )
        total = part if total is None else total + part
    return total


def local_body(height, back, x_ref, w_ref, out_ref, taps_ref):
    for p in range(height):
        fill_taps(lambda k, p=p: x_ref[p, tile_rows(k), :], taps_ref.at[p], back)
    for i in range(height):
        total = None
        for p in range(height):
            tap_row = i - p + 1 if back else p - i + 1
            if 0 <= tap_row <= 2:
                part = tap_dot(taps_ref[p], w_ref, tap_row, back)
                total = part if total is None else total + part
        out_ref[i] = total


def conv_local(planes, weight, back):
    height, rows, width = planes.shape
    parts = 2 if rows % 32 == 0 else 1
    block = planes_of(height, width, rows // parts)
    (out,) = kernel_call(
        functools.partial(local_body, height, back),
        parts,
        [block, spatial_block(weight)],
        [(jax.ShapeDtypeStruct(planes.shape, F32), block)],
        [pltpu.VMEM((height, rows // parts, 3 * width), BF16)],
        (planes, weight[0]),
        2 * rows * (3 * height - 2) * 3 * width * width,
    )
    return out


def add_halo(height, back, part_ref, above_ref, below_ref, w_ref, taps_ref):
    fill_taps(lambda k: above_ref[tile_rows(k), :], taps_ref.at[0], back)
    fill_taps(lambda k: below_ref[tile_rows(k), :], taps_ref.at[1], back)
    upper = tap_dot(taps_ref[0], w_ref, 2 if back else 0, back)
    lower = tap_dot(taps_ref[1], w_ref, 0 if back else 2, back)
    if height == 1:
        return [part_ref[0] + (upper + lower)]
    middle = [part_ref[i] for i in range(1, height - 1)]
    return [part_ref[0] + upper] + middle + [part_ref[height - 1] + lower]


def halo_body(height, part_ref, above_ref, below_ref, w_ref, m_ref, out_ref, sum_ref, square_ref, taps_ref):
    clear_first(sum_ref, square_ref)
    rows = add_halo(height, False, part_ref, above_ref, below_ref, w_ref, taps_ref)
    for i in range(height):
        out_ref[i] = rows[i]
    for i in range(height):

        def step(k, carry):
            x = out_ref[i, tile_rows(k), :]
            first = x * m_ref[i, tile_rows(k), :]
            return carry[0] + fold(first), carry[1] + fold(first * x)

        zero = jnp.zeros(sum_ref.shape, F32)
        first, second = loop(out_ref.shape[1] // TILE, step, (zero, zero))
        sum_ref[...] += first
        square_ref[...] += second


def conv_halo(part, above, below, weight, mask_planes):
    height, rows, width = part.shape
    parts = 2 if rows % 32 == 0 else 1
    size = rows // parts
    block = planes_of(height, width, size)
    edge = pl.BlockSpec((size, width), lambda k: (k, 0))
    out, first, second = kernel_call(
        functools.partial(halo_body, height),
        parts,
        [block, edge, edge, spatial_block(weight), planes_of(height, 1, size)],
        [(jax.ShapeDtypeStruct(part.shape, F32), block), sum_block(width), sum_block(width)],
        [pltpu.VMEM((2, size, 3 * width), BF16)],
        (part, above, below, weight[0], mask_planes),
        2 * rows * 2 * 3 * width * width,
    )
    return out, jnp.sum(first, axis=0), jnp.sum(second, axis=0)


def halo_back_body(
    height, part_ref, above_ref, below_ref, w_ref, slope_ref, x_ref, out_ref, sum_ref, dot_ref, taps_ref
):
    clear_first(sum_ref, dot_ref)
    rows = add_halo(height, True, part_ref, above_ref, below_ref, w_ref, taps_ref)
    for i in range(height):
        out_ref[i] = rows[i]
    width = out_ref.shape[2]
    for i in range(height):

        def step(k, carry):
            g = out_ref[i, tile_rows(k), :] * slope_ref[i, tile_rows(k), :]
            out_ref[i, tile_rows(k), :] = g
            x = x_ref[pl.ds(pl.multiple_of(2 * k, 2), 2), i].reshape(TILE, width)
            return carry[0] + fold(g), carry[1] + fold(g * x)

        zero = jnp.zeros(sum_ref.shape, F32)
        first, second = loop(out_ref.shape[1] // TILE, step, (zero, zero))
        sum_ref[...] += first
        dot_ref[...] += second


def conv_back_halo(part, above, below, weight, slope, pre_one):
    height, rows, width = part.shape
    parts = 2 if rows % 32 == 0 else 1
    size = rows // parts
    block = planes_of(height, width, size)
    edge = pl.BlockSpec((size, width), lambda k: (k, 0))
    out, first, second = kernel_call(
        functools.partial(halo_back_body, height),
        parts,
        [
            block,
            edge,
            edge,
            spatial_block(weight),
            block,
            pl.BlockSpec((size // 8, height, 8, width), lambda k: (k, 0, 0, 0)),
        ],
        [(jax.ShapeDtypeStruct(part.shape, F32), block), sum_block(width), sum_block(width)],
        [pltpu.VMEM((2, size, 3 * width), BF16)],
        (part, above, below, weight[0], slope, pre_one),
        2 * rows * 2 * 3 * width * width,
    )
    return out, jnp.sum(first, axis=0), jnp.sum(second, axis=0)


def spatial_grad_body(height, x_ref, above_ref, below_ref, g_ref, mean_ref, total_ref, out_ref, taps_ref):
    rows = g_ref.shape[1]
    reads = [lambda k: above_ref[tile_rows(k), :]]
    reads += [lambda k, p=p: x_ref[p, tile_rows(k), :] for p in range(height)]
    reads += [lambda k: below_ref[tile_rows(k), :]]
    for b in range(3):

        @pl.when(pl.program_id(0) == b)
        def _(b=b):
            for p in range(height + 2):

                def step(k, carry, p=p):
                    values = reads[p](k)
                    if b != 1:
                        values = shifted(values, False)[b // 2]
                    taps_ref[p, tile_rows(k), :] = values
                    return carry

                loop(rows // TILE, step, 0)

    for a in range(3):
        total = None
        for i in range(height):
            part = lax.dot_general(taps_ref[i + a], g_ref[i], TN, preferred_element_type=F32)
            total = part if total is None else total + part
        out_ref[a, 0] = (total - mean_ref[...] * total_ref[...]).astype(BF16)


def spatial_grad(hidden, above, below, grads, hidden_mean, grad_total):
    height, rows, width = hidden.shape
    mean, total = hidden_mean.reshape(width, 1), grad_total.reshape(1, width)
    (out,) = kernel_call(
        functools.partial(spatial_grad_body, height),
        3,
        [whole_block(a) for a in (hidden, above, below, grads, mean, total)],
        [
            (
                jax.ShapeDtypeStruct((3, 3, width, width), BF16),
                pl.BlockSpec((3, 1, width, width), lambda k: (0, k, 0, 0)),
            )
        ],
        [pltpu.VMEM((height + 2, rows, width), BF16)],
        (hidden, above, below, grads, mean, total),
        2 * 9 * height * rows * width * width,
    )
    return out.reshape(9 * width, width)


def second_body(height, x_ref, m_ref, c_ref, w_ref, hidden_ref, slope_ref, sum_ref, square_ref, mean_ref, y_ref):
    clear_first(sum_ref, square_ref, mean_ref)
    tiles = hidden_ref.shape[0] // TILE

    def step(k, carry):
        x = gather_tile(x_ref, k, height)
        m = m_ref[tile_rows(k), :]
        value, slope = gelu_both(c_ref[:TILE] * x + c_ref[TILE:], m)
        hidden = value.astype(BF16)
        hidden_ref[tile_rows(k), :] = hidden
        store_tile(slope_ref, k, slope, height)
        return carry + fold(hidden.astype(F32))

    mean_ref[...] += loop(tiles, step, jnp.zeros(mean_ref.shape, F32))
    half = w_ref.shape[2]
    for part in range(w_ref.shape[0]):
        cols = slice(part * half, (part + 1) * half)
        y_ref[:, cols] = jnp.dot(hidden_ref[...], w_ref[part], preferred_element_type=F32)

        def add(k, carry):
            y = y_ref[tile_rows(k), cols]
            return carry[0] + fold(y), carry[1] + fold(y * y)

        zero = jnp.zeros((8, half), F32)
        first, second = loop(tiles, add, (zero, zero))
        sum_ref[:, cols] += first
        square_ref[:, cols] += second


def second_hidden(pre_two, mask_flat, scale, shift, weight):
    height, rows, width = pre_two.shape
    channels = weight.shape[0] * weight.shape[2]
    crops = rows // 8
    tile = 16
    flat = tile * height * 8
    consts = jnp.concatenate([tall(scale), tall(shift)], axis=0)
    hidden, slope, first, second, mean = kernel_call(
        functools.partial(second_body, height),
        crops // tile,
        [
            planes_of(height, width, tile * 8),
            pl.BlockSpec((flat, 1), lambda k: (k, 0)),
            whole_block(consts),
            whole_block(weight),
        ],
        [
            (jax.ShapeDtypeStruct((height * rows, width), BF16), pl.BlockSpec((flat, width), lambda k: (k, 0))),
            (jax.ShapeDtypeStruct(pre_two.shape, F32), planes_of(height, width, tile * 8)),
            sum_block(channels),
            sum_block(channels),
            sum_block(width),
        ],
        [pltpu.VMEM((flat, channels), F32)],
        (pre_two, mask_flat, consts, weight),
        2 * height * rows * width * channels,
        pre_two.size,
    )
    return hidden, slope, jnp.sum(first, axis=0), jnp.sum(second, axis=0), jnp.sum(mean, axis=0)


def third_body(height, h_ref, w_ref, f_ref, m_ref, c_ref, slope_ref, pool_ref, first_ref, second_ref, y_ref):
    crops = pool_ref.shape[0]
    pixels = height * 8
    step_rows = max(pixels, TILE)
    per_step = step_rows // pixels
    chunk = w_ref.shape[2]
    for part in range(w_ref.shape[0]):
        cols = slice(part * chunk, (part + 1) * chunk)
        y_ref[:, cols] = jnp.dot(h_ref[...], w_ref[part], preferred_element_type=F32)

        def step(k, carry):
            at = pl.ds(pl.multiple_of(k * step_rows, TILE), step_rows)
            y = y_ref[at, cols]
            m = m_ref[at, :]
            s = y.reshape(-1, TILE, chunk) * c_ref[:TILE, cols] + c_ref[TILE:, cols]
            s = s.reshape(step_rows, chunk) + f_ref[at, cols].astype(F32)
            value, slope = gelu_both(s, m)
            slope_ref[at, cols] = slope.astype(BF16)
            for j in range(per_step):
                rows = slice(j * pixels, (j + 1) * pixels)
                crop = pl.ds(k * per_step + j, 1)
                pool_ref[crop, cols] = jnp.sum(value[rows], axis=0, keepdims=True)
                first_ref[crop, cols] = jnp.sum(slope[rows], axis=0, keepdims=True)
                second_ref[crop, cols] = jnp.sum(slope[rows] * y[rows], axis=0, keepdims=True)
            return carry

        loop(crops // per_step, step, 0)


def third_output(hidden, weight, features, mask_flat, scale, shift, height):
    total, width = hidden.shape
    channels = weight.shape[0] * weight.shape[2]
    tile = 16
    flat = tile * height * 8
    crops = total // (height * 8)
    consts = jnp.concatenate([tall(scale), tall(shift)], axis=0)
    rows_of = lambda n: pl.BlockSpec((flat, n), lambda k: (k, 0))
    crop_rows = (jax.ShapeDtypeStruct((crops, channels), F32), pl.BlockSpec((tile, channels), lambda k: (k, 0)))
    return kernel_call(
        functools.partial(third_body, height),
        crops // tile,
        [rows_of(width), whole_block(weight), rows_of(channels), rows_of(1), whole_block(consts)],
        [(jax.ShapeDtypeStruct((total, channels), BF16), rows_of(channels)), crop_rows, crop_rows, crop_rows],
        [pltpu.VMEM((flat, channels), F32)],
        (hidden, weight, features, mask_flat, consts),
        2 * total * width * channels + 40 * total * channels,
        total * channels,
    )


def third_back_body(
    height,
    h_ref,
    w_ref,
    d_ref,
    m_ref,
    s_ref,
    c_ref,
    slope_ref,
    x_ref,
    mean_ref,
    centred_ref,
    total_ref,
    out_ref,
    sum_ref,
    dot_ref,
    y_ref,
    g_ref,
    back_ref,
    grad_ref,
):
    clear_first(grad_ref, total_ref, sum_ref, dot_ref)
    crops = s_ref.shape[0]
    pixels = height * 8
    step_rows = max(pixels, TILE)
    per_step = step_rows // pixels
    chunk = w_ref.shape[2]
    for part in range(w_ref.shape[0]):
        cols = slice(part * chunk, (part + 1) * chunk)
        y_ref[:, cols] = jnp.dot(h_ref[...], w_ref[part], preferred_element_type=F32)

        def step(k, carry):
            at = pl.ds(pl.multiple_of(k * step_rows, TILE), step_rows)
            scales = [
                jnp.broadcast_to(s_ref[pl.ds(k * per_step + j, 1), cols], (pixels, chunk))
                for j in range(per_step)
            ]
            scale = scales[0] if per_step == 1 else jnp.concatenate(scales, axis=0)
            line = y_ref[at, cols].reshape(-1, TILE, chunk) * c_ref[TILE:, cols] + c_ref[:TILE, cols]
            g = d_ref[at, cols].astype(F32) * scale + m_ref[at, :] * line.reshape(step_rows, chunk)
            g = g.astype(BF16)
            g_ref[at, cols] = g
            g = g.astype(F32)
            return carry + jnp.sum(g.reshape(-1, 8, chunk), axis=0)

        total_ref[:, cols] += loop(crops // per_step, step, jnp.zeros((8, chunk), F32))
    grad_ref[...] += lax.dot_general(h_ref[...], g_ref[...], TN, preferred_element_type=F32)
    back = None
    for part in range(w_ref.shape[0]):
        cols = slice(part * chunk, (part + 1) * chunk)
        term = lax.dot_general(g_ref[:, cols], w_ref[part], NT, preferred_element_type=F32)
        back = term if back is None else back + term
    back_ref[...] = back

    def finish(k, carry):
        g = back_ref[tile_rows(k), :] * gather_tile(slope_ref, k, height)
        store_tile(out_ref, k, g, height)
        return carry[0] + fold(g), carry[1] + fold(g * gather_tile(x_ref, k, height))

    zero = jnp.zeros(sum_ref.shape, F32)
    first, second = loop(h_ref.shape[0] // TILE, finish, (zero, zero))
    sum_ref[...] += first
    dot_ref[...] += second

    @pl.when(pl.program_id(0) == pl.num_programs(0) - 1)
    def _():
        total = jnp.sum(total_ref[...], axis=0, keepdims=True)

        def centre(k, carry):
            at = tile_rows(k)
            centred_ref[at, :] = (grad_ref[at, :] - mean_ref[at, :] * total).astype(BF16)
            return carry

        lax.fori_loop(0, grad_ref.shape[0] // TILE, centre, 0, unroll=4)


def third_back(
    hidden, weight, slope_three, mask_flat, scale_rows, beta, gamma, slope_two, pre_two, hidden_mean
):
    height, rows, width = pre_two.shape
    total = height * rows
    channels = weight.shape[0] * weight.shape[2]
    mean = hidden_mean.reshape(width, 1)
    tile = 16
    flat = tile * height * 8
    crops = rows // 8
    consts = jnp.concatenate([tall(beta), tall(gamma)], axis=0)
    rows_of = lambda n: pl.BlockSpec((flat, n), lambda k: (k, 0))
    planes = planes_of(height, width, tile * 8)
    grad, sums, out, first, second = kernel_call(
        functools.partial(third_back_body, height),
        crops // tile,
        [
            rows_of(width),
            whole_block(weight),
            rows_of(channels),
            rows_of(1),
            pl.BlockSpec((tile, channels), lambda k: (k, 0)),
            whole_block(consts),
            planes,
            planes,
            whole_block(mean),
        ],
        [
            (jax.ShapeDtypeStruct((width, channels), BF16), pl.BlockSpec((width, channels), lambda k: (0, 0))),
            sum_block(channels),
            (jax.ShapeDtypeStruct(pre_two.shape, F32), planes),
            sum_block(width),
            sum_block(width),
        ],
        [
            pltpu.VMEM((flat, channels), F32),
            pltpu.VMEM((flat, channels), BF16),
            pltpu.VMEM((flat, width), F32),
            pltpu.VMEM((width, channels), F32),
        ],
        (hidden, weight, slope_three, mask_flat, scale_rows, consts, slope_two, pre_two, mean),
        6 * total * width * channels,
    )
    return grad, jnp.sum(sums, axis=0), out, jnp.sum(first, axis=0), jnp.sum(second, axis=0)


def second_back_body(height, g_ref, x_ref, m_ref, c_ref, out_ref, sum_ref):
    clear_first(sum_ref)
    for i in range(height):

        def step(k, carry):
            at = tile_rows(k)
            line = c_ref[TILE : 2 * TILE] + c_ref[2 * TILE :] * x_ref[i, at, :]
            g = (c_ref[:TILE] * g_ref[i, at, :] + m_ref[i, at, :] * line).astype(BF16)
            out_ref[i, at, :] = g
            return carry + fold(g.astype(F32))

        sum_ref[...] += loop(g_ref.shape[1] // TILE, step, jnp.zeros(sum_ref.shape, F32))


def second_back(grads, pre_two, mask_planes, alpha, beta, gamma):
    height, rows, width = pre_two.shape
    size = 128
    consts = jnp.concatenate([tall(alpha), tall(beta), tall(gamma)], axis=0)
    block = planes_of(height, width, size)
    out, sums = kernel_call(
        functools.partial(second_back_body, height),
        rows // size,
        [block, block, planes_of(height, 1, size), whole_block(consts)],
        [(jax.ShapeDtypeStruct(pre_two.shape, BF16), block), sum_block(width)],
        [],
        (grads, pre_two, mask_planes, consts),
        10 * pre_two.size,
    )
    return out, jnp.sum(sums, axis=0)


def first_back_body(height, g_ref, x_ref, m_ref, c_ref, out_ref):
    width = out_ref.shape[1]
    per_step = max(1, 2 // height)

    def step(k, carry):
        g = gather_tile(g_ref, k, height)
        x = x_ref[pl.ds(k * per_step, per_step)].reshape(-1, width)
        line = c_ref[TILE : 2 * TILE] + c_ref[2 * TILE :] * x
        out_ref[tile_rows(k), :] = (c_ref[:TILE] * g + m_ref[tile_rows(k), :] * line).astype(BF16)
        return carry

    loop(out_ref.shape[0] // TILE, step, 0)


def first_back(grads, pre_one, mask_flat, alpha, beta, gamma):
    crops, height, breadth, width = pre_one.shape
    tile = 16
    flat = tile * height * 8
    consts = jnp.concatenate([tall(alpha), tall(beta), tall(gamma)], axis=0)
    (out,) = kernel_call(
        functools.partial(first_back_body, height),
        crops // tile,
        [
            planes_of(height, width, tile * 8),
            pl.BlockSpec((tile, height, 8, width), lambda k: (k, 0, 0, 0)),
            pl.BlockSpec((flat, 1), lambda k: (k, 0)),
            whole_block(consts),
        ],
        [
            (
                jax.ShapeDtypeStruct((crops * height * 8, width), BF16),
                pl.BlockSpec((flat, width), lambda k: (k, 0)),
            )
        ],
        [],
        (grads, pre_one, mask_flat, consts),
        10 * pre_one.size,
    )
    return out


def last_body(height, g_ref, w_ref, d_ref, s_ref, out_ref, y_ref):
    y_ref[...] = lax.dot_general(g_ref[...], w_ref[...], NT, preferred_element_type=F32)
    pixels = height * 8
    step_rows = max(pixels, TILE)
    per_step = step_rows // pixels
    chunk = 1024
    for part in range(y_ref.shape[1] // chunk):
        cols = slice(part * chunk, (part + 1) * chunk)

        def step(k, carry):
            at = pl.ds(pl.multiple_of(k * step_rows, TILE), step_rows)
            scales = [
                jnp.broadcast_to(s_ref[pl.ds(k * per_step + j, 1), cols], (pixels, chunk))
                for j in range(per_step)
            ]
            scale = scales[0] if per_step == 1 else jnp.concatenate(scales, axis=0)
            out_ref[at, cols] = (y_ref[at, cols] + d_ref[at, cols].astype(F32) * scale).astype(BF16)
            return carry

        loop(s_ref.shape[0] // per_step, step, 0)


def last_grads(grads, weight, slope_three, scale_rows, height):
    total, width = grads.shape
    channels = weight.shape[0]
    tile = 16
    flat = tile * height * 8
    crops = total // (height * 8)
    rows_of = lambda n: pl.BlockSpec((flat, n), lambda k: (k, 0))
    (out,) = kernel_call(
        functools.partial(last_body, height),
        crops // tile,
        [
            rows_of(width),
            whole_block(weight),
            rows_of(channels),
            pl.BlockSpec((tile, channels), lambda k: (k, 0)),
        ],
        [(jax.ShapeDtypeStruct((total, channels), BF16), rows_of(channels))],
        [pltpu.VMEM((flat, channels), F32)],
        (grads, weight, slope_three, scale_rows),
        2 * total * width * channels,
    )
    return out


def edge_rows(planes):
    ends = lax.axis_size("rows") - 1
    above = lax.ppermute(planes[-1], "rows", [(i, i + 1) for i in range(ends)])
    below = lax.ppermute(planes[0], "rows", [(i + 1, i) for i in range(ends)])
    return above, below


def back_consts(gain, mean, spread, count, grad_sum, grad_dot):
    grad_gain = spread * (grad_dot - mean * grad_sum)
    alpha = gain * spread
    gamma = -alpha * spread * grad_gain / count
    beta = -alpha * grad_sum / count - gamma * mean
    return alpha, beta, gamma, grad_gain


def shards(
    features,
    pixel_mask,
    partners,
    queued,
    w_reduce,
    w_spatial,
    w_expand,
    w_hidden,
    w_embed,
    prototypes,
    gain_one,
    bias_one,
    gain_two,
    bias_two,
    gain_three,
    bias_three,
    gain_head,
    bias_head,
):
    local_crops, height, breadth, channels = features.shape
    pixels = height * breadth
    narrow = w_reduce.shape[1]
    row_count = lax.axis_size("rows")
    share = local_crops // row_count
    total_crops = local_crops * lax.axis_size("crops")
    full_reduce = gather_first(w_reduce)
    full_spatial, full_expand = gather_pair(w_spatial, w_expand)
    head_whole = lax.all_gather(
        jnp.concatenate([row_quarter(w_hidden), row_quarter(w_embed)], axis=1), BOTH, axis=0, tiled=True
    )
    hidden_cols = w_hidden.shape[1]
    full_hidden, full_embed = head_whole[:, :hidden_cols], head_whole[:, hidden_cols:]

    flat_in = features.reshape(-1, channels)
    weight_col = pixel_mask.reshape(-1, 1).astype(F32)
    mask_planes = (
        pixel_mask.transpose(1, 0, 2).reshape(height, local_crops * breadth, 1).astype(F32)
    )

    pre_one = jnp.dot(flat_in, full_reduce, preferred_element_type=F32)
    masked_one = pre_one * weight_col
    sums_one = total_narrow(
        jnp.stack(
            [
                jnp.sum(masked_one, axis=0),
                jnp.sum(masked_one * pre_one, axis=0),
                jnp.full((narrow,), jnp.sum(weight_col)),
            ]
        )
    )
    valid_count = sums_one[2, :1]
    mean_one, spread_one = spread_of(sums_one, valid_count)
    pre_one = pre_one.reshape(local_crops, height, breadth, narrow)
    scale_one = gain_one * spread_one
    hidden_one, slope_one, hidden_sum_one = first_hidden(
        pre_one, mask_planes, scale_one, bias_one - mean_one * scale_one
    )
    above_one, below_one = edge_rows(hidden_one)
    part_two = conv_local(hidden_one, full_spatial, False)
    pre_two, sum_two, square_two = conv_halo(part_two, above_one, below_one, full_spatial, mask_planes)
    sums_two = total_narrow(jnp.stack([sum_two, square_two, hidden_sum_one]))
    mean_two, spread_two = spread_of(sums_two, valid_count)
    hidden_mean_one = sums_two[2] / valid_count
    scale_two = gain_two * spread_two
    hidden_two, slope_two, sum_three, square_three, hidden_sum_two = second_hidden(
        pre_two, weight_col, scale_two, bias_two - mean_two * scale_two, full_expand
    )
    sums_three = total_wide(jnp.concatenate([sum_three, square_three, hidden_sum_two])[None])[0]
    hidden_mean_two = sums_three[2 * channels :] / valid_count
    mean_three, spread_three = spread_of(sums_three[: 2 * channels].reshape(2, -1), valid_count)
    scale_three = gain_three * spread_three
    slope_three, crop_sums, slope_sums, slope_dots = third_output(
        hidden_two, full_expand, flat_in, weight_col, scale_three, bias_three - mean_three * scale_three, height
    )
    crop_valid = jnp.sum(pixel_mask.reshape(local_crops, -1), axis=1).astype(F32)

    row_bits = [(0, b) for b in bits_of("rows")]
    pooled = jnp.concatenate(
        [crop_sums, jnp.broadcast_to(crop_valid[:, None], (local_crops, 128))], axis=1
    )
    pooled = pooled.reshape((2,) * len(row_bits) + (share, channels + 128))
    for k, step in enumerate(row_bits):
        pooled = halve(pooled, len(row_bits) - 1 - k, step, False)
    crop_count = pooled[:, channels : channels + 1]
    pooled = pooled[:, :channels] / crop_count

    pre_head = split_dot(pooled, full_hidden, 0, 3)
    sums_head = total_wide(jnp.stack([jnp.sum(pre_head, axis=0), jnp.sum(pre_head * pre_head, axis=0)]))
    mean_head, spread_head = spread_of(sums_head, F32(total_crops))
    norm_head = (pre_head - mean_head) * spread_head
    hidden_head, slope_head = gelu_both(gain_head * norm_head + bias_head)
    embedding = split_dot(hidden_head, full_embed, 0, 3)
    inverse = lax.rsqrt(jnp.sum(embedding * embedding, axis=1, keepdims=True) + EPS_UNIT)
    unit_embed = embedding * inverse

    partner_rows = (
        lax.dynamic_slice_in_dim(partners, lax.axis_index("rows") * share, share)
        - lax.axis_index("crops") * local_crops
    )
    partner_at = (partner_rows // share ^ lax.axis_index("rows")) * share + partner_rows % share
    queue_unit = queued * lax.rsqrt(jnp.sum(queued * queued, axis=1, keepdims=True) + EPS_UNIT)
    row_total = total_crops + queued.shape[0] * lax.axis_size("crops") * row_count
    proto_total = prototypes.shape[1]
    scores = jnp.dot(unit_embed, prototypes, precision=PRECISE)
    queue_scores = jnp.dot(queue_unit, prototypes, precision=PRECISE)
    plan_mass = jnp.exp(scores / SHARPNESS)
    queue_mass = jnp.exp(queue_scores / SHARPNESS)
    for iteration in range(3):
        column = jnp.sum(plan_mass, axis=0, keepdims=True) + jnp.sum(queue_mass, axis=0, keepdims=True)
        if iteration == 0:
            column, everyone = total_carrying(column, unit_embed)
            partner_embed = jnp.take(everyone, partner_at, axis=0)
            partner_scores = jnp.dot(partner_embed, prototypes, precision=PRECISE)
            partner_mass = jnp.exp(partner_scores / SHARPNESS)
        else:
            column = total_wide(column)
        scale = 1.0 / (proto_total * column)
        partner_mass = partner_mass * scale
        partner_mass = partner_mass / (row_total * jnp.sum(partner_mass, axis=1, keepdims=True))
        if iteration < 2:
            plan_mass = plan_mass * scale
            queue_mass = queue_mass * scale
            plan_mass = plan_mass / (row_total * jnp.sum(plan_mass, axis=1, keepdims=True))
            queue_mass = queue_mass / (row_total * jnp.sum(queue_mass, axis=1, keepdims=True))
    target = row_total * partner_mass
    log_probability = jax.nn.log_softmax(scores / SOFTMAX_TEMPER, axis=1)
    loss_part = -jnp.sum(target * log_probability) / total_crops
    grad_scores = (
        jnp.exp(log_probability) * jnp.sum(target, axis=1, keepdims=True) - target
    ) / (SOFTMAX_TEMPER * total_crops)
    grad_unit = jnp.dot(grad_scores, prototypes.T, precision=PRECISE)
    grad_embedding = inverse * (
        grad_unit - unit_embed * jnp.sum(unit_embed * grad_unit, axis=1, keepdims=True)
    )
    grad_hidden_head = split_dot(grad_embedding, full_embed, 1, 3)
    grad_act_head = grad_hidden_head * slope_head
    sums_back = total_wide(
        jnp.stack(
            [
                jnp.sum(grad_act_head * norm_head, axis=0),
                jnp.sum(grad_act_head, axis=0),
                jnp.full((channels,), loss_part),
            ]
        )
    )
    grad_gain_head, grad_bias_head, swav_loss = sums_back[0], sums_back[1], sums_back[2, 0]
    grad_pre_head = (
        gain_head
        * spread_head
        * (grad_act_head - (grad_bias_head + norm_head * grad_gain_head) / total_crops)
    )
    grad_pooled = split_dot(grad_pre_head, full_hidden, 1, 2)
    per_pixel = grad_pooled / crop_count
    scale_rows = lax.all_gather(per_pixel, "rows", axis=0, tiled=True)

    crop_index = lax.axis_index("crops")
    forward_all, backward_all = gather_products(
        jnp.concatenate([pooled, hidden_head, unit_embed], axis=1),
        jnp.concatenate([grad_pre_head, grad_embedding, grad_scores], axis=1),
    )
    shard_hidden, shard_embed = w_hidden.shape[0], w_embed.shape[0]
    score_at = hidden_cols + w_embed.shape[1]
    pooled_part = lax.dynamic_slice_in_dim(forward_all, crop_index * shard_hidden, shard_hidden, 1)
    hidden_part = lax.dynamic_slice_in_dim(
        forward_all, channels + crop_index * shard_embed, shard_embed, 1
    )
    out_hidden = jnp.dot(pooled_part.T, backward_all[:, :hidden_cols], preferred_element_type=F32)
    out_embed = jnp.dot(hidden_part.T, backward_all[:, hidden_cols:score_at], preferred_element_type=F32)
    grad_prototypes = jnp.dot(
        forward_all[:, channels + hidden_cols :].T, backward_all[:, score_at:], preferred_element_type=F32
    )

    sums_three_back = jnp.concatenate(
        [jnp.sum(scale_rows * slope_sums, axis=0), jnp.sum(scale_rows * slope_dots, axis=0)]
    )
    sums_three_back = total_wide(after(sums_three_back, forward_all)[None])[0]
    grad_bias_three = sums_three_back[:channels]
    alpha, beta, gamma, grad_gain_three = back_consts(
        gain_three, mean_three, spread_three, valid_count, grad_bias_three, sums_three_back[channels:]
    )
    grad_w_expand, total_three, grad_act_two, sum_back, dot_back = third_back(
        hidden_two,
        full_expand,
        slope_three,
        weight_col,
        scale_rows * alpha,
        beta,
        gamma,
        slope_two,
        pre_two,
        hidden_mean_two,
    )
    expand_stages = reduce_stages(grad_w_expand)
    sums_two_back = total_narrow(jnp.stack([sum_back, dot_back]))
    grad_bias_two = sums_two_back[0]
    alpha, beta, gamma, grad_gain_two = back_consts(
        gain_two, mean_two, spread_two, valid_count, grad_bias_two, sums_two_back[1]
    )
    alpha = after(alpha, next(expand_stages))
    grad_pre_two, total_two = second_back(grad_act_two, pre_two, mask_planes, alpha, beta, gamma)
    above_two, below_two = edge_rows(grad_pre_two)
    part_one = conv_local(grad_pre_two, full_spatial, True)
    grad_w_spatial = spatial_grad(
        hidden_one,
        above_one,
        below_one,
        grad_pre_two,
        hidden_mean_one,
        after(total_two, next(expand_stages), part_one),
    )
    spatial_stages = reduce_stages(grad_w_spatial)
    grad_act_one, sum_back, dot_back = conv_back_halo(
        part_one, after(above_two, next(expand_stages)), below_two, full_spatial, slope_one, pre_one
    )
    next(spatial_stages)
    sums_one_back = total_narrow(jnp.stack([sum_back, dot_back]))
    grad_bias_one = sums_one_back[0]
    alpha, beta, gamma, grad_gain_one = back_consts(
        gain_one, mean_one, spread_one, valid_count, grad_bias_one, sums_one_back[1]
    )
    out_expand = next(expand_stages)
    grad_pre_one = first_back(grad_act_one, pre_one, weight_col, alpha, beta, gamma)
    grad_w_reduce = lax.dot_general(
        flat_in, after(grad_pre_one, next(spatial_stages)), TN, preferred_element_type=F32
    ).astype(BF16)
    *_, out_reduce = reduce_stages(grad_w_reduce)
    *_, out_spatial = spatial_stages
    grad_features = last_grads(
        grad_pre_one, full_reduce, slope_three, scale_rows, height
    ).reshape(features.shape)

    totals = total_wide(jnp.concatenate([total_three, total_two])[None])[0]
    tap_means = jnp.tile(hidden_mean_one, 9)
    shard_expand, shard_spatial = w_expand.shape[0], w_spatial.shape[0]
    means = lax.dynamic_slice_in_dim(hidden_mean_two, crop_index * shard_expand, shard_expand)
    out_expand = out_expand + means[:, None] * totals[:channels]
    means = lax.dynamic_slice_in_dim(tap_means, crop_index * shard_spatial, shard_spatial)
    out_spatial = out_spatial + means[:, None] * totals[channels:]
    return (
        swav_loss,
        grad_features,
        out_reduce,
        out_spatial,
        out_expand,
        out_hidden,
        out_embed,
        grad_prototypes,
        grad_gain_one,
        grad_bias_one,
        grad_gain_two,
        grad_bias_two,
        grad_gain_three,
        grad_bias_three,
        grad_gain_head,
        grad_bias_head,
    )


def solution(mesh):
    split = P("crops", None)
    map_spec = P("crops", "rows", None, None)
    in_specs = (
        (map_spec, P("crops", "rows", None), P("crops"), P(BOTH, None)) + (split,) * 5 + (P(),) * 9
    )
    out_specs = (P(), map_spec) + (split,) * 5 + (P(),) * 9
    return jax.shard_map(shards, mesh=mesh, in_specs=in_specs, out_specs=out_specs, check_vma=False)
```

```python
import functools
import itertools
import math

import jax
import jax.numpy as jnp
from jax import lax
from jax.experimental import pallas as pl
from jax.experimental.pallas import tpu as pltpu
from jax.sharding import PartitionSpec as P

EPS_NORM = 1e-05
EPS_UNIT = 1e-06
SHARPNESS = 0.05
SOFTMAX_TEMPER = 0.1
PRECISE = lax.Precision.HIGHEST
BOTH = ("crops", "rows")
GELU_SCALE = 0.7978845608028654
GELU_CUBE = 0.044715
F32 = jnp.float32
BF16 = jnp.bfloat16


def bits_of(axis):
    return [1 << k for k in range(lax.axis_size(axis).bit_length() - 1)]


def xor_permute(values, crop_xor, row_xor):
    crop_total, row_total = lax.axis_size("crops"), lax.axis_size("rows")
    pairs = [
        (c * row_total + r, (c ^ crop_xor) * row_total + (r ^ row_xor))
        for c in range(crop_total)
        for r in range(row_total)
    ]
    return lax.ppermute(values, BOTH, pairs)


def all_bits():
    return [(0, b) for b in bits_of("rows")] + [(b, 0) for b in bits_of("crops")]


def total_wide(values):
    steps = all_bits()
    groups = [steps[:1]] + [steps[k : k + 2] for k in range(1, len(steps), 2)]
    for group in groups:
        if len(group) == 1:
            values = values + xor_permute(values, *group[0])
        else:
            (a, b), (c, d) = group
            near = xor_permute(values, a, b)
            far = xor_permute(values, c, d)
            both = xor_permute(values, a ^ c, b ^ d)
            values = (values + near) + (far + both)
    return values


def total_carrying(values, rows_extra):
    width, own = values.shape[1], rows_extra.reshape(1, -1)
    slots = {0: own}
    steps = all_bits()
    groups = [steps[:1]] + [steps[k : k + 2] for k in range(1, len(steps), 2)]

    def send(step, current):
        if step[0]:
            return xor_permute(current, *step), {}
        keys = sorted(slots)
        got = xor_permute(jnp.concatenate([current] + [slots[k] for k in keys], axis=1), *step)
        parts = jnp.split(got[:, width:], len(keys), axis=1)
        return got[:, :width], {k ^ step[1]: part for k, part in zip(keys, parts)}

    for group in groups:
        if len(group) == 1:
            other, more = send(group[0], values)
            values = values + other
            slots.update(more)
        else:
            (a, b), (c, d) = group
            near, near_slots = send((a, b), values)
            far, far_slots = send((c, d), values)
            both, both_slots = send((a ^ c, b ^ d), values)
            values = (values + near) + (far + both)
            for more in (near_slots, far_slots, both_slots):
                slots.update(more)
    stacked = jnp.concatenate([slots[k] for k in sorted(slots)], axis=0)
    return values, stacked.reshape(-1, rows_extra.shape[1])


def total_narrow(values):
    count = lax.axis_size("crops") * lax.axis_size("rows")
    copies = jnp.broadcast_to(values[None], (count,) + values.shape)
    return jnp.sum(lax.all_to_all(copies, BOTH, 0, 0, tiled=True), axis=0)


def my_bit(step):
    crop_xor, row_xor = step
    if crop_xor:
        return (lax.axis_index("crops") // crop_xor) % 2
    return (lax.axis_index("rows") // row_xor) % 2


def halve(values, dim, step, narrow):
    bit = my_bit(step)
    kept = lax.dynamic_index_in_dim(values, bit, dim, keepdims=False)
    sent = lax.dynamic_index_in_dim(values, 1 - bit, dim, keepdims=False)
    if narrow:
        sent = sent.astype(BF16)
    return kept.astype(F32) + xor_permute(sent, *step).astype(F32)


def double(values, step):
    other = xor_permute(values, *step)
    low = my_bit(step) == 0
    return jnp.stack([jnp.where(low, values, other), jnp.where(low, other, values)])


def gather_rows(values):
    row_bits = [(0, b) for b in bits_of("rows")]
    count = len(row_bits)
    rows, cols = values.shape
    for step in reversed(row_bits):
        values = double(values, step)
    values = values.transpose(tuple(range(count - 1, -1, -1)) + (count, count + 1))
    return values.reshape(-1, cols)


def row_quarter(weight):
    size = weight.shape[0] // lax.axis_size("rows")
    return lax.dynamic_slice_in_dim(weight, lax.axis_index("rows") * size, size)


def gather_first(weight):
    crop_total = lax.axis_size("crops")
    size, cols = weight.shape[0] // 2, weight.shape[1]
    bit = lax.axis_index("rows") % 2
    mine = lax.dynamic_slice_in_dim(weight, bit * size, size)
    mine = lax.all_to_all(
        jnp.broadcast_to(mine[None], (crop_total, size, cols)), "crops", 0, 0, tiled=True
    )
    other = xor_permute(mine, 0, 1)
    low = bit == 0
    both = jnp.stack([jnp.where(low, mine, other), jnp.where(low, other, mine)], axis=1)
    return both.reshape(2 * crop_total * size, cols)


def gather_pair(first, second):
    quarter_one, quarter_two = row_quarter(first), row_quarter(second)
    cols = first.shape[1]
    blocks = second.shape[1] // cols
    size, short = quarter_one.shape[0], quarter_two.shape[0]
    flat_two = quarter_two.reshape(short, blocks, cols).transpose(1, 0, 2).reshape(-1, cols)
    whole = lax.all_gather(jnp.concatenate([quarter_one, flat_two], axis=0), BOTH, axis=0, tiled=False)
    count = whole.shape[0]
    second_blocks = whole[:, size:].reshape(count, blocks, short, cols).transpose(1, 0, 2, 3)
    if size % 16:
        whole, size = whole[:, :size].reshape(1, -1, cols), count * size
    return (whole, size), second_blocks.reshape(blocks, -1, cols)


def spread_of(sums, count):
    mean = sums[0] / count
    return mean, lax.rsqrt(sums[1] / count - mean * mean + EPS_NORM)


def gelu_both(x, mask=None):
    square = x * x
    half = 0.5 * jnp.tanh(x * (GELU_SCALE + GELU_SCALE * GELU_CUBE * square)) + 0.5
    inner = x * (2.0 * GELU_SCALE + 6.0 * GELU_SCALE * GELU_CUBE * square)
    kept = half if mask is None else half * mask
    return x * kept, kept * (1.0 + (1.0 - half) * inner)


def split_parts(x, parts):
    pieces = []
    for _ in range(parts - 1):
        piece = lax.reduce_precision(x, 8, 7)
        pieces.append(piece.astype(BF16))
        x = x - piece
    pieces.append(x.astype(BF16))
    return jnp.concatenate(pieces, axis=0)


def split_dot(x, matrix, dim, parts):
    count = x.shape[0]
    out = lax.dot_general(
        split_parts(x, parts), matrix, (((1,), (dim,)), ((), ())), preferred_element_type=F32
    )
    total = out[(parts - 1) * count :]
    for k in range(parts - 2, -1, -1):
        total = total + out[k * count : (k + 1) * count]
    return total


TN = (((0,), (0,)), ((), ()))
NT = (((1,), (1,)), ((), ()))
TILE = 16
UNROLL = 16


def kernel_call(body, grid, ins, outs, scratch, args, flops, transcendentals=0, deps=()):
    moved = sum(a.size * a.dtype.itemsize for a in args) + sum(
        math.prod(s.shape) * s.dtype.itemsize for s, _ in outs
    )
    count = len(ins)

    def inner(*refs):
        body(*refs[:count], *refs[count + len(deps) :])

    return pl.pallas_call(
        inner,
        grid=(grid,),
        in_specs=ins + [pl.BlockSpec(memory_space=pl.ANY)] * len(deps),
        out_specs=[spec for _, spec in outs],
        out_shape=[shape for shape, _ in outs],
        scratch_shapes=scratch,
        compiler_params=pltpu.CompilerParams(vmem_limit_bytes=52 * 2**20),
        cost_estimate=pl.CostEstimate(
            flops=flops, bytes_accessed=moved, transcendentals=transcendentals
        ),
    )(*args, *deps)


def whole_block(array):
    zeros = (0,) * array.ndim
    return pl.BlockSpec(array.shape, lambda k: zeros)


def spatial_block(weight):
    array, size = weight
    return pl.BlockSpec((array.shape[0], size, array.shape[2]), lambda k: (0, 0, 0))


def sum_block(width):
    return jax.ShapeDtypeStruct((8, width), F32), pl.BlockSpec((8, width), lambda k: (0, 0))


def tall(row):
    return jnp.broadcast_to(row.reshape(1, -1), (TILE, row.size))


def fold(values):
    return values[:8] + values[8:]


def loop(count, step, start):
    return lax.fori_loop(0, count, step, start, unroll=math.gcd(count, UNROLL))


def clear_first(*refs):
    @pl.when(pl.program_id(0) == 0)
    def _():
        for ref in refs:
            ref[...] = jnp.zeros_like(ref)


def planes_of(height, width, rows):
    return pl.BlockSpec((height, rows, width), lambda k: (0, k, 0))


def rows_block(rows, width):
    return pl.BlockSpec((rows, width), lambda k: (k, 0))


def plane_out(total, width, rows):
    return jax.ShapeDtypeStruct((total, width), BF16), rows_block(rows, width)


def gather_tile(ref, index, height):
    if height == 1:
        return ref[0, pl.ds(pl.multiple_of(index * TILE, TILE), TILE), :]
    return jnp.concatenate(
        [ref[i, pl.ds(pl.multiple_of(index * 8, 8), 8), :] for i in range(height)], axis=0
    )


def store_tile(ref, index, values, height):
    if height == 1:
        ref[0, pl.ds(pl.multiple_of(index * TILE, TILE), TILE), :] = values
    else:
        for i in range(height):
            ref[i, pl.ds(pl.multiple_of(index * 8, 8), 8), :] = values[8 * i : 8 * i + 8]


def tile_rows(index):
    return pl.ds(pl.multiple_of(index * TILE, TILE), TILE)


def merge_body(counts, place_ref, *refs):
    step = pl.program_id(0)
    at, rows, totals = 0, 0, []
    for count in counts:
        total = refs[at][...].astype(F32)
        for ref in refs[at + 1 : at + count]:
            total = total + ref[...].astype(F32)
        lead, _, inner, cols = total.shape
        totals.append((rows, inner, total.astype(BF16).reshape(lead, inner, cols)))
        at, rows = at + count, rows + inner
    for k, out_ref in enumerate(refs[at:]):

        @pl.when(step == k)
        def _(out_ref=out_ref):
            for first, inner, total in totals:
                out_ref[:, first : first + inner, :] = total


def merge_split(groups, place, deps):
    lead, split, _, cols = groups[0][0].shape
    counts = [len(parts) for parts in groups]
    inner = sum(parts[0].shape[2] for parts in groups)
    args = [part for parts in groups for part in parts]

    def body(place_ref, *refs):
        merge_body(counts, place_ref, *refs[: len(args)], *refs[len(args) + len(deps) :])

    return pl.pallas_call(
        body,
        grid_spec=pltpu.PrefetchScalarGridSpec(
            num_scalar_prefetch=1,
            grid=(split,),
            in_specs=[
                pl.BlockSpec(
                    (lead, 1, part.shape[2], cols), lambda k, at: (0, jnp.bitwise_xor(at[0], k), 0, 0)
                )
                for part in args
            ]
            + [pl.BlockSpec(memory_space=pl.ANY)] * len(deps),
            out_specs=[pl.BlockSpec((lead, inner, cols), lambda k, at: (0, 0, 0))] * split,
        ),
        out_shape=[jax.ShapeDtypeStruct((lead, inner, cols), BF16)] * split,
        compiler_params=pltpu.CompilerParams(vmem_limit_bytes=52 * 2**20),
        cost_estimate=pl.CostEstimate(
            flops=sum(a.size for a in args), bytes_accessed=3 * sum(a.size for a in args), transcendentals=0
        ),
    )(jnp.reshape(place, (1,)).astype(jnp.int32), *args, *deps)


def reduce_steps():
    row_bits = [(0, b) for b in reversed(bits_of("rows"))]
    crop_bits = [(b, 0) for b in reversed(bits_of("crops"))]
    return [row_bits[-1:], crop_bits[-1:] + row_bits[:-1], crop_bits[:-1]]


def device_count():
    return lax.axis_size("crops") * lax.axis_size("rows")


def exchange(groups, bits, inner, deps=()):
    split = 2 ** len(bits)
    place = sum(my_bit(step) << k for k, step in enumerate(reversed(bits)))
    groups = [[p.reshape(-1, split, n, p.shape[-1]) for p in parts] for parts, n in zip(groups, inner)]
    pieces = merge_split(groups, place, deps)
    parts = [pieces[0]]
    for flips in range(1, split):
        chosen = [step for k, step in enumerate(reversed(bits)) if flips >> k & 1]
        parts.append(xor_permute(pieces[flips], sum(b for b, _ in chosen), sum(b for _, b in chosen)))
    return parts


def core_exchange(values, deps=()):
    inner = values.shape[0] // device_count()
    return exchange([[values]], reduce_steps()[0], [inner], deps)


def near_exchange(groups, inner, deps=()):
    return exchange(groups, reduce_steps()[1], inner, deps)


def far_exchange(parts, deps=()):
    return exchange([parts], reduce_steps()[2], [parts[0].shape[-2]], deps)


def line_exchange(parts, inner):
    _, near, far = reduce_steps()
    return exchange([parts], far[-1:], [inner * 2 ** len(near)])


def reduce_end(parts, deps=()):
    (total,) = merge_split([[p[:, None] for p in parts]], jnp.int32(0), deps)
    return gather_rows(total.reshape(total.shape[1:])).astype(F32)


def pack_body(count, *refs):
    *ins, out_ref, rows_ref = refs
    at = 0
    for k, ref in enumerate(ins):
        share, width = ref.shape
        cols = slice(at, at + width)
        at += width
        values = ref[...]
        extra = jnp.sum(values, axis=0, keepdims=True)
        if k < count:
            extra = extra * (1.0 / share)
            values = values - extra
        high = extra.astype(BF16).astype(F32)
        low = extra - high
        rows_ref[:share, cols] = values
        order = (high, high, low, low) if k < count else (high, low, high, low)
        for j, row in enumerate(order):
            rows_ref[share + j : share + j + 1, cols] = row
    out_ref[...] = rows_ref[...].astype(BF16)


def gather_products(left, right):
    arrays = left + right
    widths = [a.shape[1] for a in arrays]
    rows = arrays[0].shape[0] + 4
    (packed,) = kernel_call(
        functools.partial(pack_body, len(left)),
        1,
        [whole_block(a) for a in arrays],
        [
            (
                jax.ShapeDtypeStruct((rows, sum(widths)), BF16),
                pl.BlockSpec((rows, sum(widths)), lambda k: (0, 0)),
            )
        ],
        [pltpu.VMEM((rows, sum(widths)), F32)],
        tuple(arrays),
        6 * rows * sum(widths),
    )
    return lax.all_gather(packed, BOTH, axis=0, tiled=True)


def first_body(height, x_ref, m_ref, c_ref, *refs):
    hidden_refs, (slope_ref, sum_ref) = refs[:height], refs[height:]
    clear_first(sum_ref)
    pairs = x_ref.shape[0] // 2
    width = x_ref.shape[3]
    for i in range(height):

        def step(k, carry):
            x = x_ref[pl.ds(pl.multiple_of(2 * k, 2), 2), i].reshape(TILE, width)
            m = m_ref[i, tile_rows(k), :]
            value, slope = gelu_both(c_ref[:TILE] * x + c_ref[TILE:], m)
            hidden = value.astype(BF16)
            hidden_refs[i][tile_rows(k), :] = hidden
            slope_ref[i, tile_rows(k), :] = slope
            return carry + fold(hidden.astype(F32))

        sum_ref[...] += loop(pairs, step, jnp.zeros(sum_ref.shape, F32))


def first_hidden(pre_one, mask_planes, scale, shift, deps):
    crops, height, breadth, width = pre_one.shape
    tile = 16
    consts = jnp.concatenate([tall(scale), tall(shift)], axis=0)
    planes = planes_of(height, width, tile * 8)
    *hidden, slope, sums = kernel_call(
        functools.partial(first_body, height),
        crops // tile,
        [
            pl.BlockSpec((tile, height, 8, width), lambda k: (k, 0, 0, 0)),
            planes_of(height, 1, tile * 8),
            whole_block(consts),
        ],
        [
            *[plane_out(crops * 8, width, tile * 8)] * height,
            (jax.ShapeDtypeStruct((height, crops * 8, width), F32), planes),
            sum_block(width),
        ],
        [],
        (pre_one, mask_planes, consts),
        40 * pre_one.size,
        pre_one.size,
        deps,
    )
    return hidden, slope, jnp.sum(sums, axis=0)


def shifted(values, back):
    wide = values.astype(F32).reshape(2, 8, values.shape[1])
    place = lax.broadcasted_iota(jnp.int32, wide.shape, 1)
    before = jnp.where(place == 0, 0.0, pltpu.roll(wide, 1, 1)).reshape(values.shape).astype(BF16)
    after = jnp.where(place == 7, 0.0, pltpu.roll(wide, 7, 1)).reshape(values.shape).astype(BF16)
    return (after, before) if back else (before, after)


def fill_taps(read, out_ref, back):
    width = out_ref.shape[1] // 3

    def step(k, carry):
        values = read(k)
        low, high = shifted(values, back)
        out_ref[tile_rows(k), :width] = low
        out_ref[tile_rows(k), width : 2 * width] = values
        out_ref[tile_rows(k), 2 * width :] = high
        return carry

    loop(out_ref.shape[0] // TILE, step, 0)


def tap_dot(taps, w_ref, tap_row, back):
    width = taps.shape[1] // 3
    w_ref = w_ref.reshape(w_ref.shape[0] * w_ref.shape[1], w_ref.shape[2])
    if not back:
        return jnp.dot(
            taps, w_ref[3 * width * tap_row : 3 * width * (tap_row + 1), :], preferred_element_type=F32
        )
    total = None
    for b in range(3):
        at = (3 * tap_row + b) * width
        part = lax.dot_general(
            taps[:, b * width : (b + 1) * width],
            w_ref[at : at + width, :],
            NT,
            preferred_element_type=F32,
        )
        total = part if total is None else total + part
    return total


def local_body(height, back, *refs):
    w_ref, out_ref, taps_ref = refs[height:]
    for p in range(height):
        fill_taps(lambda k, p=p: refs[p][tile_rows(k), :], taps_ref.at[p], back)
    for i in range(height):
        total = None
        for p in range(height):
            tap_row = i - p + 1 if back else p - i + 1
            if 0 <= tap_row <= 2:
                part = tap_dot(taps_ref[p], w_ref, tap_row, back)
                total = part if total is None else total + part
        out_ref[i] = total


def conv_local(planes, weight, back):
    height = len(planes)
    rows, width = planes[0].shape
    parts = 2 if rows % 32 == 0 else 1
    (out,) = kernel_call(
        functools.partial(local_body, height, back),
        parts,
        [rows_block(rows // parts, width)] * height + [spatial_block(weight)],
        [(jax.ShapeDtypeStruct((height, rows, width), F32), planes_of(height, width, rows // parts))],
        [pltpu.VMEM((height, rows // parts, 3 * width), BF16)],
        (*planes, weight[0]),
        2 * rows * (3 * height - 2) * 3 * width * width,
    )
    return out


def add_halo(height, back, part_ref, above_ref, below_ref, w_ref, taps_ref):
    fill_taps(lambda k: above_ref[tile_rows(k), :], taps_ref.at[0], back)
    fill_taps(lambda k: below_ref[tile_rows(k), :], taps_ref.at[1], back)
    upper = tap_dot(taps_ref[0], w_ref, 2 if back else 0, back)
    lower = tap_dot(taps_ref[1], w_ref, 0 if back else 2, back)
    if height == 1:
        return [part_ref[0] + (upper + lower)]
    middle = [part_ref[i] for i in range(1, height - 1)]
    return [part_ref[0] + upper] + middle + [part_ref[height - 1] + lower]


def halo_body(height, part_ref, above_ref, below_ref, w_ref, m_ref, out_ref, sum_ref, square_ref, taps_ref):
    clear_first(sum_ref, square_ref)
    rows = add_halo(height, False, part_ref, above_ref, below_ref, w_ref, taps_ref)
    for i in range(height):
        out_ref[i] = rows[i]
    for i in range(height):

        def step(k, carry):
            x = out_ref[i, tile_rows(k), :]
            first = x * m_ref[i, tile_rows(k), :]
            return carry[0] + fold(first), carry[1] + fold(first * x)

        zero = jnp.zeros(sum_ref.shape, F32)
        first, second = loop(out_ref.shape[1] // TILE, step, (zero, zero))
        sum_ref[...] += first
        square_ref[...] += second


def conv_halo(part, above, below, weight, mask_planes):
    height, rows, width = part.shape
    parts = 2 if rows % 32 == 0 else 1
    size = rows // parts
    block = planes_of(height, width, size)
    edge = pl.BlockSpec((size, width), lambda k: (k, 0))
    out, first, second = kernel_call(
        functools.partial(halo_body, height),
        parts,
        [block, edge, edge, spatial_block(weight), planes_of(height, 1, size)],
        [(jax.ShapeDtypeStruct(part.shape, F32), block), sum_block(width), sum_block(width)],
        [pltpu.VMEM((2, size, 3 * width), BF16)],
        (part, above, below, weight[0], mask_planes),
        2 * rows * 2 * 3 * width * width,
    )
    return out, jnp.sum(first, axis=0), jnp.sum(second, axis=0)


def halo_back_body(
    height, part_ref, above_ref, below_ref, w_ref, slope_ref, x_ref, out_ref, sum_ref, dot_ref, taps_ref
):
    clear_first(sum_ref, dot_ref)
    rows = add_halo(height, True, part_ref, above_ref, below_ref, w_ref, taps_ref)
    for i in range(height):
        out_ref[i] = rows[i]
    width = out_ref.shape[2]
    for i in range(height):

        def step(k, carry):
            g = out_ref[i, tile_rows(k), :] * slope_ref[i, tile_rows(k), :]
            out_ref[i, tile_rows(k), :] = g
            x = x_ref[pl.ds(pl.multiple_of(2 * k, 2), 2), i].reshape(TILE, width)
            return carry[0] + fold(g), carry[1] + fold(g * x)

        zero = jnp.zeros(sum_ref.shape, F32)
        first, second = loop(out_ref.shape[1] // TILE, step, (zero, zero))
        sum_ref[...] += first
        dot_ref[...] += second


def conv_back_halo(part, above, below, weight, slope, pre_one, deps):
    height, rows, width = part.shape
    parts = 2 if rows % 32 == 0 else 1
    size = rows // parts
    block = planes_of(height, width, size)
    edge = pl.BlockSpec((size, width), lambda k: (k, 0))
    out, first, second = kernel_call(
        functools.partial(halo_back_body, height),
        parts,
        [
            block,
            edge,
            edge,
            spatial_block(weight),
            block,
            pl.BlockSpec((size // 8, height, 8, width), lambda k: (k, 0, 0, 0)),
        ],
        [(jax.ShapeDtypeStruct(part.shape, F32), block), sum_block(width), sum_block(width)],
        [pltpu.VMEM((2, size, 3 * width), BF16)],
        (part, above, below, weight[0], slope, pre_one),
        2 * rows * 2 * 3 * width * width,
        deps=deps,
    )
    return out, jnp.sum(first, axis=0), jnp.sum(second, axis=0)


def spatial_grad_body(height, *refs):
    x_refs, (above_ref, below_ref), g_refs = refs[:height], refs[height : height + 2], refs[height + 2 : -4]
    mean_ref, total_ref, out_ref, taps_ref = refs[-4:]
    rows = above_ref.shape[0]
    reads = [lambda k: above_ref[tile_rows(k), :]]
    reads += [lambda k, ref=ref: ref[tile_rows(k), :] for ref in x_refs]
    reads += [lambda k: below_ref[tile_rows(k), :]]
    for b in range(3):

        @pl.when(pl.program_id(0) == b)
        def _(b=b):
            for p in range(height + 2):

                def step(k, carry, p=p):
                    values = reads[p](k)
                    if b != 1:
                        values = shifted(values, False)[b // 2]
                    taps_ref[p, tile_rows(k), :] = values
                    return carry

                loop(rows // TILE, step, 0)

    for a in range(3):
        total = None
        for i in range(height):
            part = lax.dot_general(taps_ref[i + a], g_refs[i][...], TN, preferred_element_type=F32)
            total = part if total is None else total + part
        out_ref[a, 0] = (total - mean_ref[...] * total_ref[...]).astype(BF16)


def spatial_grad(hidden, above, below, grads, hidden_mean, grad_total, deps):
    height = len(hidden)
    rows, width = above.shape
    mean, total = hidden_mean.reshape(width, 1), grad_total.reshape(1, width)
    (out,) = kernel_call(
        functools.partial(spatial_grad_body, height),
        3,
        [whole_block(a) for a in (*hidden, above, below, *grads, mean, total)],
        [
            (
                jax.ShapeDtypeStruct((3, 3, width, width), BF16),
                pl.BlockSpec((3, 1, width, width), lambda k: (0, k, 0, 0)),
            )
        ],
        [pltpu.VMEM((height + 2, rows, width), BF16)],
        (*hidden, above, below, *grads, mean, total),
        2 * 9 * height * rows * width * width,
        deps=deps,
    )
    return out.reshape(9 * width, width)


def second_body(height, x_ref, m_ref, c_ref, w_ref, hidden_ref, slope_ref, sum_ref, square_ref, mean_ref, y_ref):
    clear_first(sum_ref, square_ref, mean_ref)
    tiles = hidden_ref.shape[0] // TILE

    def step(k, carry):
        x = gather_tile(x_ref, k, height)
        m = m_ref[tile_rows(k), :]
        value, slope = gelu_both(c_ref[:TILE] * x + c_ref[TILE:], m)
        hidden = value.astype(BF16)
        hidden_ref[tile_rows(k), :] = hidden
        store_tile(slope_ref, k, slope, height)
        return carry + fold(hidden.astype(F32))

    mean_ref[...] += loop(tiles, step, jnp.zeros(mean_ref.shape, F32))
    half = w_ref.shape[2]
    for part in range(w_ref.shape[0]):
        cols = slice(part * half, (part + 1) * half)
        y_ref[:, cols] = jnp.dot(hidden_ref[...], w_ref[part], preferred_element_type=F32)

        def add(k, carry):
            y = y_ref[tile_rows(k), cols]
            return carry[0] + fold(y), carry[1] + fold(y * y)

        zero = jnp.zeros((8, half), F32)
        first, second = loop(tiles, add, (zero, zero))
        sum_ref[:, cols] += first
        square_ref[:, cols] += second


def second_hidden(pre_two, mask_flat, scale, shift, weight):
    height, rows, width = pre_two.shape
    channels = weight.shape[0] * weight.shape[2]
    crops = rows // 8
    tile = 16
    flat = tile * height * 8
    consts = jnp.concatenate([tall(scale), tall(shift)], axis=0)
    hidden, slope, first, second, mean = kernel_call(
        functools.partial(second_body, height),
        crops // tile,
        [
            planes_of(height, width, tile * 8),
            pl.BlockSpec((flat, 1), lambda k: (k, 0)),
            whole_block(consts),
            whole_block(weight),
        ],
        [
            (jax.ShapeDtypeStruct((height * rows, width), BF16), pl.BlockSpec((flat, width), lambda k: (k, 0))),
            (jax.ShapeDtypeStruct(pre_two.shape, F32), planes_of(height, width, tile * 8)),
            sum_block(channels),
            sum_block(channels),
            sum_block(width),
        ],
        [pltpu.VMEM((flat, channels), F32)],
        (pre_two, mask_flat, consts, weight),
        2 * height * rows * width * channels,
        pre_two.size,
    )
    return hidden, slope, jnp.sum(first, axis=0), jnp.sum(second, axis=0), jnp.sum(mean, axis=0)


def third_body(
    height, share, h_ref, w_ref, f_ref, m_ref, c_ref, slope_ref, pool_ref, first_ref, second_ref, y_ref
):
    crops = first_ref.shape[0]
    start = pl.program_id(0) * crops
    padding = -share % 8
    pixels = height * 8
    step_rows = max(pixels, TILE)
    per_step = step_rows // pixels
    chunk = w_ref.shape[2]
    for part in range(w_ref.shape[0]):
        cols = slice(part * chunk, (part + 1) * chunk)
        y_ref[:, cols] = jnp.dot(h_ref[...], w_ref[part], preferred_element_type=F32)

        def step(k, carry):
            at = pl.ds(pl.multiple_of(k * step_rows, TILE), step_rows)
            y = y_ref[at, cols]
            m = m_ref[at, :]
            s = y.reshape(-1, TILE, chunk) * c_ref[:TILE, cols] + c_ref[TILE:, cols]
            s = s.reshape(step_rows, chunk) + f_ref[at, cols].astype(F32)
            value, slope = gelu_both(s, m)
            slope_ref[at, cols] = slope.astype(BF16)
            for j in range(per_step):
                rows = slice(j * pixels, (j + 1) * pixels)
                crop = pl.ds(k * per_step + j, 1)
                pooled_at = start + k * per_step + j
                pooled_at = pooled_at + pooled_at // share * padding
                pool_ref[pl.ds(pooled_at, 1), cols] = jnp.sum(value[rows], axis=0, keepdims=True)
                first_ref[crop, cols] = jnp.sum(slope[rows], axis=0, keepdims=True)
                second_ref[crop, cols] = jnp.sum(slope[rows] * y[rows], axis=0, keepdims=True)
            return carry

        loop(crops // per_step, step, 0)


def third_output(hidden, weight, features, mask_flat, scale, shift, height, share):
    total, width = hidden.shape
    channels = weight.shape[0] * weight.shape[2]
    tile = 16
    flat = tile * height * 8
    crops = total // (height * 8)
    consts = jnp.concatenate([tall(scale), tall(shift)], axis=0)
    rows_of = lambda n: pl.BlockSpec((flat, n), lambda k: (k, 0))
    padded = crops // share * (share + -share % 8)
    crop_rows = (jax.ShapeDtypeStruct((crops, channels), F32), pl.BlockSpec((tile, channels), lambda k: (k, 0)))
    return kernel_call(
        functools.partial(third_body, height, share),
        crops // tile,
        [rows_of(width), whole_block(weight), rows_of(channels), rows_of(1), whole_block(consts)],
        [
            (jax.ShapeDtypeStruct((total, channels), BF16), rows_of(channels)),
            (
                jax.ShapeDtypeStruct((padded, channels), F32),
                pl.BlockSpec((padded, channels), lambda k: (0, 0)),
            ),
            crop_rows,
            crop_rows,
        ],
        [pltpu.VMEM((flat, channels), F32)],
        (hidden, weight, features, mask_flat, consts),
        2 * total * width * channels + 40 * total * channels,
        total * channels,
    )


def third_back_body(
    height,
    inner,
    h_ref,
    w_ref,
    d_ref,
    m_ref,
    s_ref,
    c_ref,
    slope_ref,
    x_ref,
    mean_ref,
    centred_ref,
    total_ref,
    out_ref,
    sum_ref,
    dot_ref,
    y_ref,
    g_ref,
    back_ref,
    grad_ref,
):
    clear_first(grad_ref, total_ref, sum_ref, dot_ref)
    crops = s_ref.shape[0]
    pixels = height * 8
    step_rows = max(pixels, TILE)
    per_step = step_rows // pixels
    chunk = w_ref.shape[2]
    for part in range(w_ref.shape[0]):
        cols = slice(part * chunk, (part + 1) * chunk)
        y_ref[:, cols] = jnp.dot(h_ref[...], w_ref[part], preferred_element_type=F32)

        def step(k, carry):
            at = pl.ds(pl.multiple_of(k * step_rows, TILE), step_rows)
            scales = [
                jnp.broadcast_to(s_ref[pl.ds(k * per_step + j, 1), cols], (pixels, chunk))
                for j in range(per_step)
            ]
            scale = scales[0] if per_step == 1 else jnp.concatenate(scales, axis=0)
            line = y_ref[at, cols].reshape(-1, TILE, chunk) * c_ref[TILE:, cols] + c_ref[:TILE, cols]
            g = d_ref[at, cols].astype(F32) * scale + m_ref[at, :] * line.reshape(step_rows, chunk)
            g = g.astype(BF16)
            g_ref[at, cols] = g
            g = g.astype(F32)
            return carry + jnp.sum(g.reshape(-1, 8, chunk), axis=0)

        total_ref[:, cols] += loop(crops // per_step, step, jnp.zeros((8, chunk), F32))
    grad_ref[...] += lax.dot_general(h_ref[...], g_ref[...], TN, preferred_element_type=F32)
    back = None
    for part in range(w_ref.shape[0]):
        cols = slice(part * chunk, (part + 1) * chunk)
        term = lax.dot_general(g_ref[:, cols], w_ref[part], NT, preferred_element_type=F32)
        back = term if back is None else back + term
    back_ref[...] = back

    def finish(k, carry):
        g = back_ref[tile_rows(k), :] * gather_tile(slope_ref, k, height)
        store_tile(out_ref, k, g, height)
        return carry[0] + fold(g), carry[1] + fold(g * gather_tile(x_ref, k, height))

    zero = jnp.zeros(sum_ref.shape, F32)
    first, second = loop(h_ref.shape[0] // TILE, finish, (zero, zero))
    sum_ref[...] += first
    dot_ref[...] += second

    @pl.when(pl.program_id(0) == pl.num_programs(0) - 1)
    def _():
        total = jnp.sum(total_ref[...], axis=0, keepdims=True)
        width = centred_ref.shape[1]
        blocks, tiles = grad_ref.shape[1] // width, inner // TILE

        def centre(k, carry):
            at = tile_rows(k)
            centred = (grad_ref[at, :] - mean_ref[at, :] * total).astype(BF16)
            for part in range(centred.shape[1] // width):
                block = (k // tiles * blocks + part) * tiles + k % tiles
                centred_ref[tile_rows(block), :] = centred[:, part * width : (part + 1) * width]
            return carry

        lax.fori_loop(0, grad_ref.shape[0] // TILE, centre, 0, unroll=4)


def third_back(
    hidden, weight, slope_three, mask_flat, scale_rows, beta, gamma, slope_two, pre_two, hidden_mean
):
    height, rows, width = pre_two.shape
    total = height * rows
    channels = weight.shape[0] * weight.shape[2]
    mean = hidden_mean.reshape(width, 1)
    inner = max(TILE, width // device_count())
    tile = 16
    flat = tile * height * 8
    crops = rows // 8
    consts = jnp.concatenate([tall(beta), tall(gamma)], axis=0)
    rows_of = lambda n: pl.BlockSpec((flat, n), lambda k: (k, 0))
    planes = planes_of(height, width, tile * 8)
    grad, sums, out, first, second = kernel_call(
        functools.partial(third_back_body, height, inner),
        crops // tile,
        [
            rows_of(width),
            whole_block(weight),
            rows_of(channels),
            rows_of(1),
            pl.BlockSpec((tile, channels), lambda k: (k, 0)),
            whole_block(consts),
            planes,
            planes,
            whole_block(mean),
        ],
        [
            (jax.ShapeDtypeStruct((channels, width), BF16), pl.BlockSpec((channels, width), lambda k: (0, 0))),
            sum_block(channels),
            (jax.ShapeDtypeStruct(pre_two.shape, F32), planes),
            sum_block(width),
            sum_block(width),
        ],
        [
            pltpu.VMEM((flat, channels), F32),
            pltpu.VMEM((flat, channels), BF16),
            pltpu.VMEM((flat, width), F32),
            pltpu.VMEM((width, channels), F32),
        ],
        (hidden, weight, slope_three, mask_flat, scale_rows, consts, slope_two, pre_two, mean),
        6 * total * width * channels,
    )
    return grad, jnp.sum(sums, axis=0), out, jnp.sum(first, axis=0), jnp.sum(second, axis=0)


def second_back_body(height, g_ref, x_ref, m_ref, c_ref, *refs):
    out_refs, sum_ref = refs[:height], refs[height]
    clear_first(sum_ref)
    for i in range(height):

        def step(k, carry):
            at = tile_rows(k)
            line = c_ref[TILE : 2 * TILE] + c_ref[2 * TILE :] * x_ref[i, at, :]
            g = (c_ref[:TILE] * g_ref[i, at, :] + m_ref[i, at, :] * line).astype(BF16)
            out_refs[i][at, :] = g
            return carry + fold(g.astype(F32))

        sum_ref[...] += loop(g_ref.shape[1] // TILE, step, jnp.zeros(sum_ref.shape, F32))


def second_back(grads, pre_two, mask_planes, alpha, beta, gamma, deps):
    height, rows, width = pre_two.shape
    size = 128
    consts = jnp.concatenate([tall(alpha), tall(beta), tall(gamma)], axis=0)
    block = planes_of(height, width, size)
    *out, sums = kernel_call(
        functools.partial(second_back_body, height),
        rows // size,
        [block, block, planes_of(height, 1, size), whole_block(consts)],
        [plane_out(rows, width, size)] * height + [sum_block(width)],
        [],
        (grads, pre_two, mask_planes, consts),
        10 * pre_two.size,
        deps=deps,
    )
    return out, jnp.sum(sums, axis=0)


def first_back_body(height, g_ref, x_ref, m_ref, c_ref, f_ref, out_ref, grad_ref, total_ref):
    clear_first(total_ref)
    width = out_ref.shape[1]
    per_step = max(1, 2 // height)

    def step(k, carry):
        g = gather_tile(g_ref, k, height)
        x = x_ref[pl.ds(k * per_step, per_step)].reshape(-1, width)
        line = c_ref[TILE : 2 * TILE] + c_ref[2 * TILE :] * x
        out_ref[tile_rows(k), :] = (c_ref[:TILE] * g + m_ref[tile_rows(k), :] * line).astype(BF16)
        return carry

    loop(out_ref.shape[0] // TILE, step, 0)
    last = pl.program_id(0) == pl.num_programs(0) - 1
    for at in range(0, f_ref.shape[1], width):
        part = slice(at, at + width)
        total_ref[part, :] += lax.dot_general(
            f_ref[:, part], out_ref[...], TN, preferred_element_type=F32
        )

    @pl.when(last)
    def _():
        grad_ref[...] = total_ref[...].astype(BF16)


def first_back(grads, pre_one, mask_flat, alpha, beta, gamma, features, deps):
    crops, height, breadth, width = pre_one.shape
    channels = features.shape[1]
    tile = crops // 2
    flat = tile * height * 8
    consts = jnp.concatenate([tall(alpha), tall(beta), tall(gamma)], axis=0)
    return kernel_call(
        functools.partial(first_back_body, height),
        crops // tile,
        [
            planes_of(height, width, tile * 8),
            pl.BlockSpec((tile, height, 8, width), lambda k: (k, 0, 0, 0)),
            rows_block(flat, 1),
            whole_block(consts),
            rows_block(flat, channels),
        ],
        [
            plane_out(crops * height * 8, width, flat),
            (jax.ShapeDtypeStruct((channels, width), BF16), pl.BlockSpec((channels, width), lambda k: (0, 0))),
        ],
        [pltpu.VMEM((channels, width), F32)],
        (grads, pre_one, mask_flat, consts, features),
        2 * crops * height * 8 * width * channels,
        deps=deps,
    )


def last_body(height, g_ref, w_ref, d_ref, s_ref, out_ref, y_ref):
    y_ref[...] = lax.dot_general(g_ref[...], w_ref[...], NT, preferred_element_type=F32)
    pixels = height * 8
    step_rows = max(pixels, TILE)
    per_step = step_rows // pixels
    chunk = 1024
    for part in range(y_ref.shape[1] // chunk):
        cols = slice(part * chunk, (part + 1) * chunk)

        def step(k, carry):
            at = pl.ds(pl.multiple_of(k * step_rows, TILE), step_rows)
            scales = [
                jnp.broadcast_to(s_ref[pl.ds(k * per_step + j, 1), cols], (pixels, chunk))
                for j in range(per_step)
            ]
            scale = scales[0] if per_step == 1 else jnp.concatenate(scales, axis=0)
            out_ref[at, cols] = (y_ref[at, cols] + d_ref[at, cols].astype(F32) * scale).astype(BF16)
            return carry

        loop(s_ref.shape[0] // per_step, step, 0)


def last_grads(grads, weight, slope_three, scale_rows, height, deps):
    total, width = grads.shape
    channels = weight.shape[0]
    tile = 16
    flat = tile * height * 8
    crops = total // (height * 8)
    rows_of = lambda n: pl.BlockSpec((flat, n), lambda k: (k, 0))
    (out,) = kernel_call(
        functools.partial(last_body, height),
        crops // tile,
        [
            rows_of(width),
            whole_block(weight),
            rows_of(channels),
            pl.BlockSpec((tile, channels), lambda k: (k, 0)),
        ],
        [(jax.ShapeDtypeStruct((total, channels), BF16), rows_of(channels))],
        [pltpu.VMEM((flat, channels), F32)],
        (grads, weight, slope_three, scale_rows),
        2 * total * width * channels,
        deps=deps,
    )
    return out


def edge_rows(planes):
    ends = lax.axis_size("rows") - 1
    above = lax.ppermute(planes[-1], "rows", [(i, i + 1) for i in range(ends)])
    below = lax.ppermute(planes[0], "rows", [(i + 1, i) for i in range(ends)])
    return above, below


def back_consts(gain, mean, spread, count, grad_sum, grad_dot):
    grad_gain = spread * (grad_dot - mean * grad_sum)
    alpha = gain * spread
    gamma = -alpha * spread * grad_gain / count
    beta = -alpha * grad_sum / count - gamma * mean
    return alpha, beta, gamma, grad_gain


def shards(
    features,
    pixel_mask,
    partners,
    queued,
    w_reduce,
    w_spatial,
    w_expand,
    w_hidden,
    w_embed,
    prototypes,
    gain_one,
    bias_one,
    gain_two,
    bias_two,
    gain_three,
    bias_three,
    gain_head,
    bias_head,
):
    local_crops, height, breadth, channels = features.shape
    pixels = height * breadth
    narrow = w_reduce.shape[1]
    row_count = lax.axis_size("rows")
    share = local_crops // row_count
    total_crops = local_crops * lax.axis_size("crops")
    full_reduce = gather_first(w_reduce)
    full_spatial, full_expand = gather_pair(w_spatial, w_expand)
    head_whole = lax.all_gather(
        jnp.concatenate([row_quarter(w_hidden), row_quarter(w_embed)], axis=1), BOTH, axis=0, tiled=True
    )
    hidden_cols = w_hidden.shape[1]
    full_hidden, full_embed = head_whole[:, :hidden_cols], head_whole[:, hidden_cols:]

    row_bits = [(0, b) for b in bits_of("rows")]
    crop_count = jnp.sum(pixel_mask.reshape(local_crops, -1), axis=1).astype(F32)
    crop_count = jnp.broadcast_to(crop_count[:, None], (local_crops, 128))
    crop_count = crop_count.reshape((2,) * len(row_bits) + (share, 128))
    for k, step in enumerate(row_bits):
        crop_count = halve(crop_count, len(row_bits) - 1 - k, step, False)
    crop_count = crop_count[:, :1]

    flat_in = features.reshape(-1, channels)
    weight_col = pixel_mask.reshape(-1, 1).astype(F32)
    mask_planes = (
        pixel_mask.transpose(1, 0, 2).reshape(height, local_crops * breadth, 1).astype(F32)
    )

    queue_unit = queued * lax.rsqrt(jnp.sum(queued * queued, axis=1, keepdims=True) + EPS_UNIT)
    queue_scores = jnp.dot(queue_unit, prototypes, precision=PRECISE)
    pre_one = jnp.dot(flat_in, full_reduce, preferred_element_type=F32)
    masked_one = pre_one * weight_col
    sums_one = total_narrow(
        jnp.stack(
            [
                jnp.sum(masked_one, axis=0),
                jnp.sum(masked_one * pre_one, axis=0),
                jnp.full((narrow,), jnp.sum(weight_col)),
            ]
        )
    )
    valid_count = sums_one[2, :1]
    mean_one, spread_one = spread_of(sums_one, valid_count)
    pre_one = pre_one.reshape(local_crops, height, breadth, narrow)
    scale_one = gain_one * spread_one
    hidden_one, slope_one, hidden_sum_one = first_hidden(
        pre_one, mask_planes, scale_one, bias_one - mean_one * scale_one, (queue_scores,)
    )
    above_one, below_one = edge_rows(hidden_one)
    part_two = conv_local(hidden_one, full_spatial, False)
    pre_two, sum_two, square_two = conv_halo(part_two, above_one, below_one, full_spatial, mask_planes)
    sums_two = total_narrow(jnp.stack([sum_two, square_two, hidden_sum_one]))
    mean_two, spread_two = spread_of(sums_two, valid_count)
    hidden_mean_one = sums_two[2] / valid_count
    scale_two = gain_two * spread_two
    hidden_two, slope_two, sum_three, square_three, hidden_sum_two = second_hidden(
        pre_two, weight_col, scale_two, bias_two - mean_two * scale_two, full_expand
    )
    sums_three = total_wide(jnp.concatenate([sum_three, square_three, hidden_sum_two])[None])[0]
    hidden_mean_two = sums_three[2 * channels :] / valid_count
    mean_three, spread_three = spread_of(sums_three[: 2 * channels].reshape(2, -1), valid_count)
    scale_three = gain_three * spread_three
    slope_three, crop_sums, slope_sums, slope_dots = third_output(
        hidden_two, full_expand, flat_in, weight_col, scale_three, bias_three - mean_three * scale_three, height, share
    )
    pooled = crop_sums.reshape((2,) * len(row_bits) + (-1, channels))
    for k, step in enumerate(row_bits):
        pooled = halve(pooled, len(row_bits) - 1 - k, step, False)
    pooled = pooled[:share] / crop_count

    pre_head = split_dot(pooled, full_hidden, 0, 3)
    sums_head = total_wide(jnp.stack([jnp.sum(pre_head, axis=0), jnp.sum(pre_head * pre_head, axis=0)]))
    mean_head, spread_head = spread_of(sums_head, F32(total_crops))
    norm_head = (pre_head - mean_head) * spread_head
    hidden_head, slope_head = gelu_both(gain_head * norm_head + bias_head)
    embedding = split_dot(hidden_head, full_embed, 0, 3)
    inverse = lax.rsqrt(jnp.sum(embedding * embedding, axis=1, keepdims=True) + EPS_UNIT)
    unit_embed = embedding * inverse

    partner_rows = (
        lax.dynamic_slice_in_dim(partners, lax.axis_index("rows") * share, share)
        - lax.axis_index("crops") * local_crops
    )
    partner_at = (partner_rows // share ^ lax.axis_index("rows")) * share + partner_rows % share
    row_total = total_crops + queued.shape[0] * lax.axis_size("crops") * row_count
    proto_total = prototypes.shape[1]
    scores = jnp.dot(unit_embed, prototypes, precision=PRECISE)
    plan_mass = jnp.exp(scores / SHARPNESS)
    queue_mass = jnp.exp(queue_scores / SHARPNESS)
    for iteration in range(3):
        column = jnp.sum(plan_mass, axis=0, keepdims=True) + jnp.sum(queue_mass, axis=0, keepdims=True)
        if iteration == 0:
            column, everyone = total_carrying(column, unit_embed)
            partner_embed = jnp.take(everyone, partner_at, axis=0)
            partner_scores = jnp.dot(partner_embed, prototypes, precision=PRECISE)
            partner_mass = jnp.exp(partner_scores / SHARPNESS)
        else:
            column = total_wide(column)
        scale = 1.0 / (proto_total * column)
        partner_mass = partner_mass * scale
        partner_mass = partner_mass / (row_total * jnp.sum(partner_mass, axis=1, keepdims=True))
        if iteration < 2:
            plan_mass = plan_mass * scale
            queue_mass = queue_mass * scale
            plan_mass = plan_mass / (row_total * jnp.sum(plan_mass, axis=1, keepdims=True))
            queue_mass = queue_mass / (row_total * jnp.sum(queue_mass, axis=1, keepdims=True))
    target = row_total * partner_mass
    log_probability = jax.nn.log_softmax(scores / SOFTMAX_TEMPER, axis=1)
    loss_part = -jnp.sum(target * log_probability) / total_crops
    grad_scores = (
        jnp.exp(log_probability) * jnp.sum(target, axis=1, keepdims=True) - target
    ) / (SOFTMAX_TEMPER * total_crops)
    grad_unit = jnp.dot(grad_scores, prototypes.T, precision=PRECISE)
    grad_embedding = inverse * (
        grad_unit - unit_embed * jnp.sum(unit_embed * grad_unit, axis=1, keepdims=True)
    )
    grad_hidden_head = split_dot(grad_embedding, full_embed, 1, 3)
    grad_act_head = grad_hidden_head * slope_head
    sums_back = total_wide(
        jnp.stack(
            [
                jnp.sum(grad_act_head * norm_head, axis=0),
                jnp.sum(grad_act_head, axis=0),
                jnp.full((channels,), loss_part),
            ]
        )
    )
    grad_gain_head, grad_bias_head, swav_loss = sums_back[0], sums_back[1], sums_back[2, 0]
    grad_pre_head = (
        gain_head
        * spread_head
        * (grad_act_head - (grad_bias_head + norm_head * grad_gain_head) / total_crops)
    )
    grad_pooled = split_dot(grad_pre_head, full_hidden, 1, 2)
    per_pixel = grad_pooled / crop_count
    scale_rows = lax.all_gather(per_pixel, "rows", axis=0, tiled=True)

    crop_index = lax.axis_index("crops")
    proto_pad = -proto_total % 128
    products = gather_products(
        [pooled, hidden_head, unit_embed],
        [grad_pre_head, grad_embedding, jnp.pad(grad_scores, ((0, 0), (0, proto_pad)))],
    )
    shard_hidden, shard_embed, width = w_hidden.shape[0], w_embed.shape[0], w_embed.shape[1]
    right_at = channels + hidden_cols + width

    def product_of(at, size, to, count):
        return lax.dot_general(
            lax.dynamic_slice_in_dim(products, at, size, 1),
            lax.slice_in_dim(products, right_at + to, right_at + to + count, axis=1),
            TN,
            preferred_element_type=F32,
        )

    out_hidden = product_of(crop_index * shard_hidden, shard_hidden, 0, hidden_cols)
    out_embed = product_of(channels + crop_index * shard_embed, shard_embed, hidden_cols, width)
    grad_prototypes = product_of(channels + hidden_cols, width, hidden_cols + width, proto_total)

    sums_three_back = jnp.concatenate(
        [jnp.sum(scale_rows * slope_sums, axis=0), jnp.sum(scale_rows * slope_dots, axis=0)]
    )
    sums_three_back = total_wide(sums_three_back[None])[0]
    grad_bias_three = sums_three_back[:channels]
    alpha, beta, gamma, grad_gain_three = back_consts(
        gain_three, mean_three, spread_three, valid_count, grad_bias_three, sums_three_back[channels:]
    )
    grad_w_expand, total_three, grad_act_two, sum_back, dot_back = third_back(
        hidden_two,
        full_expand,
        slope_three,
        weight_col,
        scale_rows * alpha,
        beta,
        gamma,
        slope_two,
        pre_two,
        hidden_mean_two,
    )
    sums_two_back = total_narrow(jnp.stack([sum_back, dot_back]))
    grad_bias_two = sums_two_back[0]
    alpha, beta, gamma, grad_gain_two = back_consts(
        gain_two, mean_two, spread_two, valid_count, grad_bias_two, sums_two_back[1]
    )
    grad_pre_two, total_two = second_back(
        grad_act_two, pre_two, mask_planes, alpha, beta, gamma, ()
    )
    above_two, below_two = edge_rows(grad_pre_two)
    part_one = conv_local(grad_pre_two, full_spatial, True)
    grad_act_one, sum_back, dot_back = conv_back_halo(
        part_one, above_two, below_two, full_spatial, slope_one, pre_one, ()
    )
    sums_one_back = total_narrow(
        jnp.concatenate([sum_back, dot_back, total_two, total_three]).reshape(-1, narrow)
    )
    grad_w_spatial = spatial_grad(
        hidden_one,
        above_one,
        below_one,
        grad_pre_two,
        hidden_mean_one,
        total_two,
        (grad_act_one,),
    )
    grad_bias_one = sums_one_back[0]
    alpha, beta, gamma, grad_gain_one = back_consts(
        gain_one, mean_one, spread_one, valid_count, grad_bias_one, sums_one_back[1]
    )
    spatial_core = core_exchange(grad_w_spatial, (alpha,))
    blocks = channels // narrow
    spatial_rows, *lane_rows = [
        n // row_count for n in (w_spatial.shape[0], w_reduce.shape[0], blocks * w_expand.shape[0])
    ]
    grad_pre_one, grad_w_reduce = first_back(
        grad_act_one, pre_one, weight_col, alpha, beta, gamma, flat_in, (spatial_core[0],)
    )
    near = near_exchange([spatial_core], [spatial_rows])
    lines = [
        line_exchange(core_exchange(g), n) for g, n in zip((grad_w_reduce, grad_w_expand), lane_rows)
    ]
    grad_features = last_grads(
        grad_pre_one,
        full_reduce,
        slope_three,
        scale_rows,
        height,
        (out_hidden, out_embed, grad_prototypes, near[0], *[parts[0] for parts in lines]),
    )
    far = far_exchange(near, (grad_features,))
    lane = near_exchange(lines, lane_rows, (grad_features,))
    lane = exchange([lane], reduce_steps()[2][:-1], [sum(lane_rows)])
    out_spatial = reduce_end(far).reshape(w_spatial.shape)
    sums = reduce_end(lane).reshape(row_count, -1, narrow)
    out_reduce = sums[:, : lane_rows[0]].reshape(w_reduce.shape)
    out_expand = sums[:, lane_rows[0] :].reshape(row_count, blocks, -1, narrow)
    out_expand = out_expand.transpose(0, 2, 1, 3).reshape(w_expand.shape)
    grad_features = grad_features.reshape(features.shape)

    grad_totals = sums_one_back[2:].reshape(-1)
    tap_means = jnp.tile(hidden_mean_one, 9)
    shard_expand, shard_spatial = w_expand.shape[0], w_spatial.shape[0]
    means = lax.dynamic_slice_in_dim(hidden_mean_two, crop_index * shard_expand, shard_expand)
    out_expand = out_expand + means[:, None] * grad_totals[narrow:]
    means = lax.dynamic_slice_in_dim(tap_means, crop_index * shard_spatial, shard_spatial)
    out_spatial = out_spatial + means[:, None] * grad_totals[:narrow]
    return (
        swav_loss,
        grad_features,
        out_reduce,
        out_spatial,
        out_expand,
        out_hidden,
        out_embed,
        grad_prototypes,
        grad_gain_one,
        grad_bias_one,
        grad_gain_two,
        grad_bias_two,
        grad_gain_three,
        grad_bias_three,
        grad_gain_head,
        grad_bias_head,
    )


def solution(mesh):
    split = P("crops", None)
    map_spec = P("crops", "rows", None, None)
    in_specs = (
        (map_spec, P("crops", "rows", None), P("crops"), P(BOTH, None)) + (split,) * 5 + (P(),) * 9
    )
    out_specs = (P(), map_spec) + (split,) * 5 + (P(),) * 9
    return jax.shard_map(shards, mesh=mesh, in_specs=in_specs, out_specs=out_specs, check_vma=False)
```

```python
import functools
import itertools
import math

import jax
import jax.numpy as jnp
from jax import lax
from jax.experimental import pallas as pl
from jax.experimental.pallas import tpu as pltpu
from jax.sharding import PartitionSpec as P

EPS_NORM = 1e-05
EPS_UNIT = 1e-06
SHARPNESS = 0.05
SOFTMAX_TEMPER = 0.1
PRECISE = lax.Precision.HIGHEST
BOTH = ("crops", "rows")
GELU_SCALE = 0.7978845608028654
GELU_CUBE = 0.044715
F32 = jnp.float32
BF16 = jnp.bfloat16


def bits_of(axis):
    return [1 << k for k in range(lax.axis_size(axis).bit_length() - 1)]


def xor_permute(values, crop_xor, row_xor):
    crop_total, row_total = lax.axis_size("crops"), lax.axis_size("rows")
    pairs = [
        (c * row_total + r, (c ^ crop_xor) * row_total + (r ^ row_xor))
        for c in range(crop_total)
        for r in range(row_total)
    ]
    return lax.ppermute(values, BOTH, pairs)


def all_bits():
    return [(0, b) for b in bits_of("rows")] + [(b, 0) for b in bits_of("crops")]


def total_wide(values):
    steps = all_bits()
    groups = [steps[:1]] + [steps[k : k + 2] for k in range(1, len(steps), 2)]
    for group in groups:
        if len(group) == 1:
            values = values + xor_permute(values, *group[0])
        else:
            (a, b), (c, d) = group
            near = xor_permute(values, a, b)
            far = xor_permute(values, c, d)
            both = xor_permute(values, a ^ c, b ^ d)
            values = (values + near) + (far + both)
    return values


def total_carrying(values, rows_extra):
    width, own = values.shape[1], rows_extra.reshape(1, -1)
    slots = {0: own}
    steps = all_bits()
    groups = [steps[:1]] + [steps[k : k + 2] for k in range(1, len(steps), 2)]

    def send(step, current):
        if step[0]:
            return xor_permute(current, *step), {}
        keys = sorted(slots)
        got = xor_permute(jnp.concatenate([current] + [slots[k] for k in keys], axis=1), *step)
        parts = jnp.split(got[:, width:], len(keys), axis=1)
        return got[:, :width], {k ^ step[1]: part for k, part in zip(keys, parts)}

    for group in groups:
        if len(group) == 1:
            other, more = send(group[0], values)
            values = values + other
            slots.update(more)
        else:
            (a, b), (c, d) = group
            near, near_slots = send((a, b), values)
            far, far_slots = send((c, d), values)
            both, both_slots = send((a ^ c, b ^ d), values)
            values = (values + near) + (far + both)
            for more in (near_slots, far_slots, both_slots):
                slots.update(more)
    stacked = jnp.concatenate([slots[k] for k in sorted(slots)], axis=0)
    return values, stacked.reshape(-1, rows_extra.shape[1])


def total_narrow(values):
    count = lax.axis_size("crops") * lax.axis_size("rows")
    copies = jnp.broadcast_to(values[None], (count,) + values.shape)
    return jnp.sum(lax.all_to_all(copies, BOTH, 0, 0, tiled=True), axis=0)


def my_bit(step):
    crop_xor, row_xor = step
    if crop_xor:
        return (lax.axis_index("crops") // crop_xor) % 2
    return (lax.axis_index("rows") // row_xor) % 2


def halve(values, dim, step, narrow):
    bit = my_bit(step)
    kept = lax.dynamic_index_in_dim(values, bit, dim, keepdims=False)
    sent = lax.dynamic_index_in_dim(values, 1 - bit, dim, keepdims=False)
    if narrow:
        sent = sent.astype(BF16)
    return kept.astype(F32) + xor_permute(sent, *step).astype(F32)


def double(values, step):
    other = xor_permute(values, *step)
    low = my_bit(step) == 0
    return jnp.stack([jnp.where(low, values, other), jnp.where(low, other, values)])


def gather_rows(values):
    row_bits = [(0, b) for b in bits_of("rows")]
    count = len(row_bits)
    rows, cols = values.shape
    for step in reversed(row_bits):
        values = double(values, step)
    values = values.transpose(tuple(range(count - 1, -1, -1)) + (count, count + 1))
    return values.reshape(-1, cols)


def row_quarter(weight):
    size = weight.shape[0] // lax.axis_size("rows")
    return lax.dynamic_slice_in_dim(weight, lax.axis_index("rows") * size, size)


def gather_first(weight):
    crop_total = lax.axis_size("crops")
    size, cols = weight.shape[0] // 2, weight.shape[1]
    bit = lax.axis_index("rows") % 2
    mine = lax.dynamic_slice_in_dim(weight, bit * size, size)
    mine = lax.all_to_all(
        jnp.broadcast_to(mine[None], (crop_total, size, cols)), "crops", 0, 0, tiled=True
    )
    other = xor_permute(mine, 0, 1)
    low = bit == 0
    both = jnp.stack([jnp.where(low, mine, other), jnp.where(low, other, mine)], axis=1)
    return both.reshape(2 * crop_total * size, cols)


def gather_pair(first, second):
    quarter_one, quarter_two = row_quarter(first), row_quarter(second)
    cols = first.shape[1]
    blocks = second.shape[1] // cols
    size, short = quarter_one.shape[0], quarter_two.shape[0]
    flat_two = quarter_two.reshape(short, blocks, cols).transpose(1, 0, 2).reshape(-1, cols)
    whole = lax.all_gather(jnp.concatenate([quarter_one, flat_two], axis=0), BOTH, axis=0, tiled=False)
    count = whole.shape[0]
    second_blocks = whole[:, size:].reshape(count, blocks, short, cols).transpose(1, 0, 2, 3)
    if size % 16:
        whole, size = whole[:, :size].reshape(1, -1, cols), count * size
    return (whole, size), second_blocks.reshape(blocks, -1, cols)


def spread_of(sums, count):
    mean = sums[0] / count
    return mean, lax.rsqrt(sums[1] / count - mean * mean + EPS_NORM)


def gelu_both(x, mask=None):
    square = x * x
    half = 0.5 * jnp.tanh(x * (GELU_SCALE + GELU_SCALE * GELU_CUBE * square)) + 0.5
    inner = x * (2.0 * GELU_SCALE + 6.0 * GELU_SCALE * GELU_CUBE * square)
    kept = half if mask is None else half * mask
    return x * kept, kept * (1.0 + (1.0 - half) * inner)


def split_parts(x, parts):
    pieces = []
    for _ in range(parts - 1):
        piece = lax.reduce_precision(x, 8, 7)
        pieces.append(piece.astype(BF16))
        x = x - piece
    pieces.append(x.astype(BF16))
    return jnp.concatenate(pieces, axis=0)


def split_dot(x, matrix, dim, parts):
    count = x.shape[0]
    out = lax.dot_general(
        split_parts(x, parts), matrix, (((1,), (dim,)), ((), ())), preferred_element_type=F32
    )
    total = out[(parts - 1) * count :]
    for k in range(parts - 2, -1, -1):
        total = total + out[k * count : (k + 1) * count]
    return total


TN = (((0,), (0,)), ((), ()))
NT = (((1,), (1,)), ((), ()))
TILE = 16
UNROLL = 16


def kernel_call(body, grid, ins, outs, scratch, args, flops, transcendentals=0, deps=()):
    moved = sum(a.size * a.dtype.itemsize for a in args) + sum(
        math.prod(s.shape) * s.dtype.itemsize for s, _ in outs
    )
    count = len(ins)

    def inner(*refs):
        body(*refs[:count], *refs[count + len(deps) :])

    return pl.pallas_call(
        inner,
        grid=(grid,),
        in_specs=ins + [pl.BlockSpec(memory_space=pl.ANY)] * len(deps),
        out_specs=[spec for _, spec in outs],
        out_shape=[shape for shape, _ in outs],
        scratch_shapes=scratch,
        compiler_params=pltpu.CompilerParams(vmem_limit_bytes=52 * 2**20),
        cost_estimate=pl.CostEstimate(
            flops=flops, bytes_accessed=moved, transcendentals=transcendentals
        ),
    )(*args, *deps)


def whole_block(array):
    zeros = (0,) * array.ndim
    return pl.BlockSpec(array.shape, lambda k: zeros)


def spatial_block(weight):
    array, size = weight
    return pl.BlockSpec((array.shape[0], size, array.shape[2]), lambda k: (0, 0, 0))


def sum_block(width):
    return jax.ShapeDtypeStruct((8, width), F32), pl.BlockSpec((8, width), lambda k: (0, 0))


def tall(row):
    return jnp.broadcast_to(row.reshape(1, -1), (TILE, row.size))


def fold(values):
    return values[:8] + values[8:]


def loop(count, step, start):
    return lax.fori_loop(0, count, step, start, unroll=math.gcd(count, UNROLL))


def clear_first(*refs):
    @pl.when(pl.program_id(0) == 0)
    def _():
        for ref in refs:
            ref[...] = jnp.zeros_like(ref)


def planes_of(height, width, rows):
    return pl.BlockSpec((height, rows, width), lambda k: (0, k, 0))


def rows_block(rows, width):
    return pl.BlockSpec((rows, width), lambda k: (k, 0))


def plane_out(total, width, rows):
    return jax.ShapeDtypeStruct((total, width), BF16), rows_block(rows, width)


def gather_tile(ref, index, height):
    if height == 1:
        return ref[0, pl.ds(pl.multiple_of(index * TILE, TILE), TILE), :]
    return jnp.concatenate(
        [ref[i, pl.ds(pl.multiple_of(index * 8, 8), 8), :] for i in range(height)], axis=0
    )


def store_tile(ref, index, values, height):
    if height == 1:
        ref[0, pl.ds(pl.multiple_of(index * TILE, TILE), TILE), :] = values
    else:
        for i in range(height):
            ref[i, pl.ds(pl.multiple_of(index * 8, 8), 8), :] = values[8 * i : 8 * i + 8]


def tile_rows(index):
    return pl.ds(pl.multiple_of(index * TILE, TILE), TILE)


def merge_body(counts, place_ref, *refs):
    step = pl.program_id(0)
    at, rows, totals = 0, 0, []
    for count in counts:
        total = refs[at][...].astype(F32)
        for ref in refs[at + 1 : at + count]:
            total = total + ref[...].astype(F32)
        lead, _, inner, cols = total.shape
        totals.append((rows, inner, total.astype(BF16).reshape(lead, inner, cols)))
        at, rows = at + count, rows + inner
    for k, out_ref in enumerate(refs[at:]):

        @pl.when(step == k)
        def _(out_ref=out_ref):
            for first, inner, total in totals:
                out_ref[:, first : first + inner, :] = total


def merge_split(groups, place, deps):
    lead, split, _, cols = groups[0][0].shape
    counts = [len(parts) for parts in groups]
    inner = sum(parts[0].shape[2] for parts in groups)
    args = [part for parts in groups for part in parts]

    def body(place_ref, *refs):
        merge_body(counts, place_ref, *refs[: len(args)], *refs[len(args) + len(deps) :])

    return pl.pallas_call(
        body,
        grid_spec=pltpu.PrefetchScalarGridSpec(
            num_scalar_prefetch=1,
            grid=(split,),
            in_specs=[
                pl.BlockSpec(
                    (lead, 1, part.shape[2], cols), lambda k, at: (0, jnp.bitwise_xor(at[0], k), 0, 0)
                )
                for part in args
            ]
            + [pl.BlockSpec(memory_space=pl.ANY)] * len(deps),
            out_specs=[pl.BlockSpec((lead, inner, cols), lambda k, at: (0, 0, 0))] * split,
        ),
        out_shape=[jax.ShapeDtypeStruct((lead, inner, cols), BF16)] * split,
        compiler_params=pltpu.CompilerParams(vmem_limit_bytes=52 * 2**20),
        cost_estimate=pl.CostEstimate(
            flops=sum(a.size for a in args), bytes_accessed=3 * sum(a.size for a in args), transcendentals=0
        ),
    )(jnp.reshape(place, (1,)).astype(jnp.int32), *args, *deps)


def reduce_steps():
    row_bits = [(0, b) for b in reversed(bits_of("rows"))]
    crop_bits = [(b, 0) for b in reversed(bits_of("crops"))]
    return [row_bits[-1:], crop_bits[-1:] + row_bits[:-1], crop_bits[:-1]]


def device_count():
    return lax.axis_size("crops") * lax.axis_size("rows")


def exchange(groups, bits, inner, deps=()):
    split = 2 ** len(bits)
    place = sum(my_bit(step) << k for k, step in enumerate(reversed(bits)))
    groups = [[p.reshape(-1, split, n, p.shape[-1]) for p in parts] for parts, n in zip(groups, inner)]
    pieces = merge_split(groups, place, deps)
    parts = [pieces[0]]
    for flips in range(1, split):
        chosen = [step for k, step in enumerate(reversed(bits)) if flips >> k & 1]
        parts.append(xor_permute(pieces[flips], sum(b for b, _ in chosen), sum(b for _, b in chosen)))
    return parts


def core_exchange(values, deps=()):
    inner = values.shape[0] // device_count()
    return exchange([[values]], reduce_steps()[0], [inner], deps)


def near_exchange(groups, inner, deps=()):
    return exchange(groups, reduce_steps()[1], inner, deps)


def far_exchange(parts, deps=()):
    return exchange([parts], reduce_steps()[2], [parts[0].shape[-2]], deps)


def line_exchange(parts, inner):
    _, near, far = reduce_steps()
    return exchange([parts], far[-1:], [inner * 2 ** len(near)])


def reduce_end(parts, deps=()):
    (total,) = merge_split([[p[:, None] for p in parts]], jnp.int32(0), deps)
    return gather_rows(total.reshape(total.shape[1:])).astype(F32)


def pack_body(centred, *refs):
    *ins, out_ref, rows_ref = refs
    at = 0
    for ref in ins:
        share, width = ref.shape
        cols = slice(at, at + width)
        at += width
        values = ref[...]
        extra = jnp.sum(values, axis=0, keepdims=True)
        if centred:
            extra = extra * (1.0 / share)
            values = values - extra
        high = extra.astype(BF16).astype(F32)
        low = extra - high
        rows_ref[:share, cols] = values
        order = (high, high, low, low) if centred else (high, low, high, low)
        for j, row in enumerate(order):
            rows_ref[share + j : share + j + 1, cols] = row
    out_ref[...] = rows_ref[...].astype(BF16)


def gather_products(arrays, centred, deps):
    widths = [a.shape[1] for a in arrays]
    rows = arrays[0].shape[0] + 4
    (packed,) = kernel_call(
        functools.partial(pack_body, centred),
        1,
        [whole_block(a) for a in arrays],
        [
            (
                jax.ShapeDtypeStruct((rows, sum(widths)), BF16),
                pl.BlockSpec((rows, sum(widths)), lambda k: (0, 0)),
            )
        ],
        [pltpu.VMEM((rows, sum(widths)), F32)],
        tuple(arrays),
        6 * rows * sum(widths),
        deps=deps,
    )
    return lax.all_gather(packed, BOTH, axis=0, tiled=True)


def first_body(height, x_ref, m_ref, c_ref, *refs):
    hidden_refs, (slope_ref, sum_ref) = refs[:height], refs[height:]
    clear_first(sum_ref)
    pairs = x_ref.shape[0] // 2
    width = x_ref.shape[3]
    for i in range(height):

        def step(k, carry):
            x = x_ref[pl.ds(pl.multiple_of(2 * k, 2), 2), i].reshape(TILE, width)
            m = m_ref[i, tile_rows(k), :]
            value, slope = gelu_both(c_ref[:TILE] * x + c_ref[TILE:], m)
            hidden = value.astype(BF16)
            hidden_refs[i][tile_rows(k), :] = hidden
            slope_ref[i, tile_rows(k), :] = slope
            return carry + fold(hidden.astype(F32))

        sum_ref[...] += loop(pairs, step, jnp.zeros(sum_ref.shape, F32))


def first_hidden(pre_one, mask_planes, scale, shift, deps):
    crops, height, breadth, width = pre_one.shape
    tile = 16
    consts = jnp.concatenate([tall(scale), tall(shift)], axis=0)
    planes = planes_of(height, width, tile * 8)
    *hidden, slope, sums = kernel_call(
        functools.partial(first_body, height),
        crops // tile,
        [
            pl.BlockSpec((tile, height, 8, width), lambda k: (k, 0, 0, 0)),
            planes_of(height, 1, tile * 8),
            whole_block(consts),
        ],
        [
            *[plane_out(crops * 8, width, tile * 8)] * height,
            (jax.ShapeDtypeStruct((height, crops * 8, width), F32), planes),
            sum_block(width),
        ],
        [],
        (pre_one, mask_planes, consts),
        40 * pre_one.size,
        pre_one.size,
        deps,
    )
    return hidden, slope, jnp.sum(sums, axis=0)


def shifted(values, back):
    wide = values.astype(F32).reshape(2, 8, values.shape[1])
    place = lax.broadcasted_iota(jnp.int32, wide.shape, 1)
    before = jnp.where(place == 0, 0.0, pltpu.roll(wide, 1, 1)).reshape(values.shape).astype(BF16)
    after = jnp.where(place == 7, 0.0, pltpu.roll(wide, 7, 1)).reshape(values.shape).astype(BF16)
    return (after, before) if back else (before, after)


def fill_taps(read, out_ref, back):
    width = out_ref.shape[1] // 3

    def step(k, carry):
        values = read(k)
        low, high = shifted(values, back)
        out_ref[tile_rows(k), :width] = low
        out_ref[tile_rows(k), width : 2 * width] = values
        out_ref[tile_rows(k), 2 * width :] = high
        return carry

    loop(out_ref.shape[0] // TILE, step, 0)


def tap_dot(taps, w_ref, tap_row, back):
    width = taps.shape[1] // 3
    w_ref = w_ref.reshape(w_ref.shape[0] * w_ref.shape[1], w_ref.shape[2])
    if not back:
        return jnp.dot(
            taps, w_ref[3 * width * tap_row : 3 * width * (tap_row + 1), :], preferred_element_type=F32
        )
    total = None
    for b in range(3):
        at = (3 * tap_row + b) * width
        part = lax.dot_general(
            taps[:, b * width : (b + 1) * width],
            w_ref[at : at + width, :],
            NT,
            preferred_element_type=F32,
        )
        total = part if total is None else total + part
    return total


def local_body(height, back, *refs):
    w_ref, out_ref, taps_ref = refs[height:]
    for p in range(height):
        fill_taps(lambda k, p=p: refs[p][tile_rows(k), :], taps_ref.at[p], back)
    for i in range(height):
        total = None
        for p in range(height):
            tap_row = i - p + 1 if back else p - i + 1
            if 0 <= tap_row <= 2:
                part = tap_dot(taps_ref[p], w_ref, tap_row, back)
                total = part if total is None else total + part
        out_ref[i] = total


def conv_local(planes, weight, back):
    height = len(planes)
    rows, width = planes[0].shape
    parts = 2 if rows % 32 == 0 else 1
    (out,) = kernel_call(
        functools.partial(local_body, height, back),
        parts,
        [rows_block(rows // parts, width)] * height + [spatial_block(weight)],
        [(jax.ShapeDtypeStruct((height, rows, width), F32), planes_of(height, width, rows // parts))],
        [pltpu.VMEM((height, rows // parts, 3 * width), BF16)],
        (*planes, weight[0]),
        2 * rows * (3 * height - 2) * 3 * width * width,
    )
    return out


def add_halo(height, back, part_ref, above_ref, below_ref, w_ref, taps_ref):
    fill_taps(lambda k: above_ref[tile_rows(k), :], taps_ref.at[0], back)
    fill_taps(lambda k: below_ref[tile_rows(k), :], taps_ref.at[1], back)
    upper = tap_dot(taps_ref[0], w_ref, 2 if back else 0, back)
    lower = tap_dot(taps_ref[1], w_ref, 0 if back else 2, back)
    if height == 1:
        return [part_ref[0] + (upper + lower)]
    middle = [part_ref[i] for i in range(1, height - 1)]
    return [part_ref[0] + upper] + middle + [part_ref[height - 1] + lower]


def halo_body(height, part_ref, above_ref, below_ref, w_ref, m_ref, out_ref, sum_ref, square_ref, taps_ref):
    clear_first(sum_ref, square_ref)
    rows = add_halo(height, False, part_ref, above_ref, below_ref, w_ref, taps_ref)
    for i in range(height):
        out_ref[i] = rows[i]
    for i in range(height):

        def step(k, carry):
            x = out_ref[i, tile_rows(k), :]
            first = x * m_ref[i, tile_rows(k), :]
            return carry[0] + fold(first), carry[1] + fold(first * x)

        zero = jnp.zeros(sum_ref.shape, F32)
        first, second = loop(out_ref.shape[1] // TILE, step, (zero, zero))
        sum_ref[...] += first
        square_ref[...] += second


def conv_halo(part, above, below, weight, mask_planes):
    height, rows, width = part.shape
    parts = 2 if rows % 32 == 0 else 1
    size = rows // parts
    block = planes_of(height, width, size)
    edge = pl.BlockSpec((size, width), lambda k: (k, 0))
    out, first, second = kernel_call(
        functools.partial(halo_body, height),
        parts,
        [block, edge, edge, spatial_block(weight), planes_of(height, 1, size)],
        [(jax.ShapeDtypeStruct(part.shape, F32), block), sum_block(width), sum_block(width)],
        [pltpu.VMEM((2, size, 3 * width), BF16)],
        (part, above, below, weight[0], mask_planes),
        2 * rows * 2 * 3 * width * width,
    )
    return out, jnp.sum(first, axis=0), jnp.sum(second, axis=0)


def halo_back_body(
    height, part_ref, above_ref, below_ref, w_ref, slope_ref, x_ref, out_ref, sum_ref, dot_ref, taps_ref
):
    clear_first(sum_ref, dot_ref)
    rows = add_halo(height, True, part_ref, above_ref, below_ref, w_ref, taps_ref)
    for i in range(height):
        out_ref[i] = rows[i]
    width = out_ref.shape[2]
    for i in range(height):

        def step(k, carry):
            g = out_ref[i, tile_rows(k), :] * slope_ref[i, tile_rows(k), :]
            out_ref[i, tile_rows(k), :] = g
            x = x_ref[pl.ds(pl.multiple_of(2 * k, 2), 2), i].reshape(TILE, width)
            return carry[0] + fold(g), carry[1] + fold(g * x)

        zero = jnp.zeros(sum_ref.shape, F32)
        first, second = loop(out_ref.shape[1] // TILE, step, (zero, zero))
        sum_ref[...] += first
        dot_ref[...] += second


def conv_back_halo(part, above, below, weight, slope, pre_one, deps):
    height, rows, width = part.shape
    parts = 2 if rows % 32 == 0 else 1
    size = rows // parts
    block = planes_of(height, width, size)
    edge = pl.BlockSpec((size, width), lambda k: (k, 0))
    out, first, second = kernel_call(
        functools.partial(halo_back_body, height),
        parts,
        [
            block,
            edge,
            edge,
            spatial_block(weight),
            block,
            pl.BlockSpec((size // 8, height, 8, width), lambda k: (k, 0, 0, 0)),
        ],
        [(jax.ShapeDtypeStruct(part.shape, F32), block), sum_block(width), sum_block(width)],
        [pltpu.VMEM((2, size, 3 * width), BF16)],
        (part, above, below, weight[0], slope, pre_one),
        2 * rows * 2 * 3 * width * width,
        deps=deps,
    )
    return out, jnp.sum(first, axis=0), jnp.sum(second, axis=0)


def spatial_grad_body(height, *refs):
    x_refs, (above_ref, below_ref), g_refs = refs[:height], refs[height : height + 2], refs[height + 2 : -4]
    mean_ref, total_ref, out_ref, taps_ref = refs[-4:]
    rows = above_ref.shape[0]
    reads = [lambda k: above_ref[tile_rows(k), :]]
    reads += [lambda k, ref=ref: ref[tile_rows(k), :] for ref in x_refs]
    reads += [lambda k: below_ref[tile_rows(k), :]]
    for b in range(3):

        @pl.when(pl.program_id(0) == b)
        def _(b=b):
            for p in range(height + 2):

                def step(k, carry, p=p):
                    values = reads[p](k)
                    if b != 1:
                        values = shifted(values, False)[b // 2]
                    taps_ref[p, tile_rows(k), :] = values
                    return carry

                loop(rows // TILE, step, 0)

    for a in range(3):
        total = None
        for i in range(height):
            part = lax.dot_general(taps_ref[i + a], g_refs[i][...], TN, preferred_element_type=F32)
            total = part if total is None else total + part
        out_ref[a, 0] = (total - mean_ref[...] * total_ref[...]).astype(BF16)


def spatial_grad(hidden, above, below, grads, hidden_mean, grad_total, deps):
    height = len(hidden)
    rows, width = above.shape
    mean, total = hidden_mean.reshape(width, 1), grad_total.reshape(1, width)
    (out,) = kernel_call(
        functools.partial(spatial_grad_body, height),
        3,
        [whole_block(a) for a in (*hidden, above, below, *grads, mean, total)],
        [
            (
                jax.ShapeDtypeStruct((3, 3, width, width), BF16),
                pl.BlockSpec((3, 1, width, width), lambda k: (0, k, 0, 0)),
            )
        ],
        [pltpu.VMEM((height + 2, rows, width), BF16)],
        (*hidden, above, below, *grads, mean, total),
        2 * 9 * height * rows * width * width,
        deps=deps,
    )
    return out.reshape(9 * width, width)


def second_body(height, x_ref, m_ref, c_ref, w_ref, hidden_ref, slope_ref, sum_ref, square_ref, mean_ref, y_ref):
    clear_first(sum_ref, square_ref, mean_ref)
    tiles = hidden_ref.shape[0] // TILE

    def step(k, carry):
        x = gather_tile(x_ref, k, height)
        m = m_ref[tile_rows(k), :]
        value, slope = gelu_both(c_ref[:TILE] * x + c_ref[TILE:], m)
        hidden = value.astype(BF16)
        hidden_ref[tile_rows(k), :] = hidden
        store_tile(slope_ref, k, slope, height)
        return carry + fold(hidden.astype(F32))

    mean_ref[...] += loop(tiles, step, jnp.zeros(mean_ref.shape, F32))
    half = w_ref.shape[2]
    for part in range(w_ref.shape[0]):
        cols = slice(part * half, (part + 1) * half)
        y_ref[:, cols] = jnp.dot(hidden_ref[...], w_ref[part], preferred_element_type=F32)

        def add(k, carry):
            y = y_ref[tile_rows(k), cols]
            return carry[0] + fold(y), carry[1] + fold(y * y)

        zero = jnp.zeros((8, half), F32)
        first, second = loop(tiles, add, (zero, zero))
        sum_ref[:, cols] += first
        square_ref[:, cols] += second


def second_hidden(pre_two, mask_flat, scale, shift, weight):
    height, rows, width = pre_two.shape
    channels = weight.shape[0] * weight.shape[2]
    crops = rows // 8
    tile = 16
    flat = tile * height * 8
    consts = jnp.concatenate([tall(scale), tall(shift)], axis=0)
    hidden, slope, first, second, mean = kernel_call(
        functools.partial(second_body, height),
        crops // tile,
        [
            planes_of(height, width, tile * 8),
            pl.BlockSpec((flat, 1), lambda k: (k, 0)),
            whole_block(consts),
            whole_block(weight),
        ],
        [
            (jax.ShapeDtypeStruct((height * rows, width), BF16), pl.BlockSpec((flat, width), lambda k: (k, 0))),
            (jax.ShapeDtypeStruct(pre_two.shape, F32), planes_of(height, width, tile * 8)),
            sum_block(channels),
            sum_block(channels),
            sum_block(width),
        ],
        [pltpu.VMEM((flat, channels), F32)],
        (pre_two, mask_flat, consts, weight),
        2 * height * rows * width * channels,
        pre_two.size,
    )
    return hidden, slope, jnp.sum(first, axis=0), jnp.sum(second, axis=0), jnp.sum(mean, axis=0)


def third_body(
    height, share, h_ref, w_ref, f_ref, m_ref, c_ref, slope_ref, pool_ref, sums_ref, y_ref
):
    crops = h_ref.shape[0] // (height * 8)
    channels = y_ref.shape[1]
    start = pl.program_id(0) * crops
    padding = -share % 8
    pixels = height * 8
    step_rows = max(pixels, TILE)
    per_step = step_rows // pixels
    chunk = w_ref.shape[2]
    for part in range(w_ref.shape[0]):
        cols = slice(part * chunk, (part + 1) * chunk)
        y_ref[:, cols] = jnp.dot(h_ref[...], w_ref[part], preferred_element_type=F32)

        def step(k, carry):
            at = pl.ds(pl.multiple_of(k * step_rows, TILE), step_rows)
            y = y_ref[at, cols]
            m = m_ref[at, :]
            s = y.reshape(-1, TILE, chunk) * c_ref[:TILE, cols] + c_ref[TILE:, cols]
            s = s.reshape(step_rows, chunk) + f_ref[at, cols].astype(F32)
            value, slope = gelu_both(s, m)
            slope_ref[at, cols] = slope.astype(BF16)
            for j in range(per_step):
                rows = slice(j * pixels, (j + 1) * pixels)
                pooled_at = start + k * per_step + j
                at_crop = pl.ds(pooled_at + pooled_at // share * padding, 1)
                pool_ref[at_crop, cols] = jnp.sum(value[rows], axis=0, keepdims=True)
                sums_ref[at_crop, cols] = jnp.sum(slope[rows], axis=0, keepdims=True)
                sums_ref[at_crop, slice(cols.start + channels, cols.stop + channels)] = jnp.sum(
                    slope[rows] * y[rows], axis=0, keepdims=True
                )
            return carry

        loop(crops // per_step, step, 0)


def third_output(hidden, weight, features, mask_flat, scale, shift, height, share):
    total, width = hidden.shape
    channels = weight.shape[0] * weight.shape[2]
    tile = 16
    flat = tile * height * 8
    crops = total // (height * 8)
    consts = jnp.concatenate([tall(scale), tall(shift)], axis=0)
    rows_of = lambda n: pl.BlockSpec((flat, n), lambda k: (k, 0))
    padded = crops // share * (share + -share % 8)
    kept = lambda n: (jax.ShapeDtypeStruct((padded, n), F32), pl.BlockSpec((padded, n), lambda k: (0, 0)))
    return kernel_call(
        functools.partial(third_body, height, share),
        crops // tile,
        [rows_of(width), whole_block(weight), rows_of(channels), rows_of(1), whole_block(consts)],
        [
            (jax.ShapeDtypeStruct((total, channels), BF16), rows_of(channels)),
            kept(channels),
            kept(2 * channels),
        ],
        [pltpu.VMEM((flat, channels), F32)],
        (hidden, weight, features, mask_flat, consts),
        2 * total * width * channels + 40 * total * channels,
        total * channels,
    )


def third_back_body(
    height,
    inner,
    h_ref,
    w_ref,
    d_ref,
    m_ref,
    s_ref,
    c_ref,
    slope_ref,
    x_ref,
    mean_ref,
    centred_ref,
    total_ref,
    out_ref,
    sum_ref,
    dot_ref,
    y_ref,
    g_ref,
    back_ref,
    grad_ref,
):
    clear_first(grad_ref, total_ref, sum_ref, dot_ref)
    crops = s_ref.shape[0]
    pixels = height * 8
    step_rows = max(pixels, TILE)
    per_step = step_rows // pixels
    chunk = w_ref.shape[2]
    for part in range(w_ref.shape[0]):
        cols = slice(part * chunk, (part + 1) * chunk)
        y_ref[:, cols] = jnp.dot(h_ref[...], w_ref[part], preferred_element_type=F32)

        def step(k, carry):
            at = pl.ds(pl.multiple_of(k * step_rows, TILE), step_rows)
            scales = [
                jnp.broadcast_to(s_ref[pl.ds(k * per_step + j, 1), cols], (pixels, chunk))
                for j in range(per_step)
            ]
            scale = scales[0] if per_step == 1 else jnp.concatenate(scales, axis=0)
            line = y_ref[at, cols].reshape(-1, TILE, chunk) * c_ref[TILE:, cols] + c_ref[:TILE, cols]
            g = d_ref[at, cols].astype(F32) * scale + m_ref[at, :] * line.reshape(step_rows, chunk)
            g = g.astype(BF16)
            g_ref[at, cols] = g
            g = g.astype(F32)
            return carry + jnp.sum(g.reshape(-1, 8, chunk), axis=0)

        total_ref[:, cols] += loop(crops // per_step, step, jnp.zeros((8, chunk), F32))
    grad_ref[...] += lax.dot_general(h_ref[...], g_ref[...], TN, preferred_element_type=F32)
    back = None
    for part in range(w_ref.shape[0]):
        cols = slice(part * chunk, (part + 1) * chunk)
        term = lax.dot_general(g_ref[:, cols], w_ref[part], NT, preferred_element_type=F32)
        back = term if back is None else back + term
    back_ref[...] = back

    def finish(k, carry):
        g = back_ref[tile_rows(k), :] * gather_tile(slope_ref, k, height)
        store_tile(out_ref, k, g, height)
        return carry[0] + fold(g), carry[1] + fold(g * gather_tile(x_ref, k, height))

    zero = jnp.zeros(sum_ref.shape, F32)
    first, second = loop(h_ref.shape[0] // TILE, finish, (zero, zero))
    sum_ref[...] += first
    dot_ref[...] += second

    @pl.when(pl.program_id(0) == pl.num_programs(0) - 1)
    def _():
        total = jnp.sum(total_ref[...], axis=0, keepdims=True)
        width = centred_ref.shape[1]
        blocks, tiles = grad_ref.shape[1] // width, inner // TILE

        def centre(k, carry):
            at = tile_rows(k)
            centred = (grad_ref[at, :] - mean_ref[at, :] * total).astype(BF16)
            for part in range(centred.shape[1] // width):
                block = (k // tiles * blocks + part) * tiles + k % tiles
                centred_ref[tile_rows(block), :] = centred[:, part * width : (part + 1) * width]
            return carry

        lax.fori_loop(0, grad_ref.shape[0] // TILE, centre, 0, unroll=4)


def third_back(
    hidden, weight, slope_three, mask_flat, scale_rows, beta, gamma, slope_two, pre_two, hidden_mean
):
    height, rows, width = pre_two.shape
    total = height * rows
    channels = weight.shape[0] * weight.shape[2]
    mean = hidden_mean.reshape(width, 1)
    inner = max(TILE, width // device_count())
    tile = 16
    flat = tile * height * 8
    crops = rows // 8
    consts = jnp.concatenate([tall(beta), tall(gamma)], axis=0)
    rows_of = lambda n: pl.BlockSpec((flat, n), lambda k: (k, 0))
    planes = planes_of(height, width, tile * 8)
    grad, sums, out, first, second = kernel_call(
        functools.partial(third_back_body, height, inner),
        crops // tile,
        [
            rows_of(width),
            whole_block(weight),
            rows_of(channels),
            rows_of(1),
            pl.BlockSpec((tile, channels), lambda k: (k, 0)),
            whole_block(consts),
            planes,
            planes,
            whole_block(mean),
        ],
        [
            (jax.ShapeDtypeStruct((channels, width), BF16), pl.BlockSpec((channels, width), lambda k: (0, 0))),
            sum_block(channels),
            (jax.ShapeDtypeStruct(pre_two.shape, F32), planes),
            sum_block(width),
            sum_block(width),
        ],
        [
            pltpu.VMEM((flat, channels), F32),
            pltpu.VMEM((flat, channels), BF16),
            pltpu.VMEM((flat, width), F32),
            pltpu.VMEM((width, channels), F32),
        ],
        (hidden, weight, slope_three, mask_flat, scale_rows, consts, slope_two, pre_two, mean),
        6 * total * width * channels,
    )
    return grad, jnp.sum(sums, axis=0), out, jnp.sum(first, axis=0), jnp.sum(second, axis=0)


def second_back_body(height, g_ref, x_ref, m_ref, c_ref, *refs):
    out_refs, sum_ref = refs[:height], refs[height]
    clear_first(sum_ref)
    for i in range(height):

        def step(k, carry):
            at = tile_rows(k)
            line = c_ref[TILE : 2 * TILE] + c_ref[2 * TILE :] * x_ref[i, at, :]
            g = (c_ref[:TILE] * g_ref[i, at, :] + m_ref[i, at, :] * line).astype(BF16)
            out_refs[i][at, :] = g
            return carry + fold(g.astype(F32))

        sum_ref[...] += loop(g_ref.shape[1] // TILE, step, jnp.zeros(sum_ref.shape, F32))


def second_back(grads, pre_two, mask_planes, alpha, beta, gamma, deps):
    height, rows, width = pre_two.shape
    size = 128
    consts = jnp.concatenate([tall(alpha), tall(beta), tall(gamma)], axis=0)
    block = planes_of(height, width, size)
    *out, sums = kernel_call(
        functools.partial(second_back_body, height),
        rows // size,
        [block, block, planes_of(height, 1, size), whole_block(consts)],
        [plane_out(rows, width, size)] * height + [sum_block(width)],
        [],
        (grads, pre_two, mask_planes, consts),
        10 * pre_two.size,
        deps=deps,
    )
    return out, jnp.sum(sums, axis=0)


def first_back_body(height, g_ref, x_ref, m_ref, c_ref, f_ref, out_ref, grad_ref, total_ref):
    clear_first(total_ref)
    width = out_ref.shape[1]
    per_step = max(1, 2 // height)

    def step(k, carry):
        g = gather_tile(g_ref, k, height)
        x = x_ref[pl.ds(k * per_step, per_step)].reshape(-1, width)
        line = c_ref[TILE : 2 * TILE] + c_ref[2 * TILE :] * x
        out_ref[tile_rows(k), :] = (c_ref[:TILE] * g + m_ref[tile_rows(k), :] * line).astype(BF16)
        return carry

    loop(out_ref.shape[0] // TILE, step, 0)
    last = pl.program_id(0) == pl.num_programs(0) - 1
    for at in range(0, f_ref.shape[1], width):
        part = slice(at, at + width)
        total_ref[part, :] += lax.dot_general(
            f_ref[:, part], out_ref[...], TN, preferred_element_type=F32
        )

    @pl.when(last)
    def _():
        grad_ref[...] = total_ref[...].astype(BF16)


def first_back(grads, pre_one, mask_flat, alpha, beta, gamma, features, deps):
    crops, height, breadth, width = pre_one.shape
    channels = features.shape[1]
    tile = crops // 2
    flat = tile * height * 8
    consts = jnp.concatenate([tall(alpha), tall(beta), tall(gamma)], axis=0)
    return kernel_call(
        functools.partial(first_back_body, height),
        crops // tile,
        [
            planes_of(height, width, tile * 8),
            pl.BlockSpec((tile, height, 8, width), lambda k: (k, 0, 0, 0)),
            rows_block(flat, 1),
            whole_block(consts),
            rows_block(flat, channels),
        ],
        [
            plane_out(crops * height * 8, width, flat),
            (jax.ShapeDtypeStruct((channels, width), BF16), pl.BlockSpec((channels, width), lambda k: (0, 0))),
        ],
        [pltpu.VMEM((channels, width), F32)],
        (grads, pre_one, mask_flat, consts, features),
        2 * crops * height * 8 * width * channels,
        deps=deps,
    )


def last_body(height, g_ref, w_ref, d_ref, s_ref, out_ref, y_ref):
    y_ref[...] = lax.dot_general(g_ref[...], w_ref[...], NT, preferred_element_type=F32)
    pixels = height * 8
    step_rows = max(pixels, TILE)
    per_step = step_rows // pixels
    chunk = 1024
    for part in range(y_ref.shape[1] // chunk):
        cols = slice(part * chunk, (part + 1) * chunk)

        def step(k, carry):
            at = pl.ds(pl.multiple_of(k * step_rows, TILE), step_rows)
            scales = [
                jnp.broadcast_to(s_ref[pl.ds(k * per_step + j, 1), cols], (pixels, chunk))
                for j in range(per_step)
            ]
            scale = scales[0] if per_step == 1 else jnp.concatenate(scales, axis=0)
            out_ref[at, cols] = (y_ref[at, cols] + d_ref[at, cols].astype(F32) * scale).astype(BF16)
            return carry

        loop(s_ref.shape[0] // per_step, step, 0)


def last_grads(grads, weight, slope_three, scale_rows, height, deps):
    total, width = grads.shape
    channels = weight.shape[0]
    tile = 16
    flat = tile * height * 8
    crops = total // (height * 8)
    rows_of = lambda n: pl.BlockSpec((flat, n), lambda k: (k, 0))
    (out,) = kernel_call(
        functools.partial(last_body, height),
        crops // tile,
        [
            rows_of(width),
            whole_block(weight),
            rows_of(channels),
            pl.BlockSpec((tile, channels), lambda k: (k, 0)),
        ],
        [(jax.ShapeDtypeStruct((total, channels), BF16), rows_of(channels))],
        [pltpu.VMEM((flat, channels), F32)],
        (grads, weight, slope_three, scale_rows),
        2 * total * width * channels,
        deps=deps,
    )
    return out


def edge_rows(planes):
    ends = lax.axis_size("rows") - 1
    above = lax.ppermute(planes[-1], "rows", [(i, i + 1) for i in range(ends)])
    below = lax.ppermute(planes[0], "rows", [(i + 1, i) for i in range(ends)])
    return above, below


def back_consts(gain, mean, spread, count, grad_sum, grad_dot):
    grad_gain = spread * (grad_dot - mean * grad_sum)
    alpha = gain * spread
    gamma = -alpha * spread * grad_gain / count
    beta = -alpha * grad_sum / count - gamma * mean
    return alpha, beta, gamma, grad_gain


def shards(
    features,
    pixel_mask,
    partners,
    queued,
    w_reduce,
    w_spatial,
    w_expand,
    w_hidden,
    w_embed,
    prototypes,
    gain_one,
    bias_one,
    gain_two,
    bias_two,
    gain_three,
    bias_three,
    gain_head,
    bias_head,
):
    local_crops, height, breadth, channels = features.shape
    pixels = height * breadth
    narrow = w_reduce.shape[1]
    row_count = lax.axis_size("rows")
    share = local_crops // row_count
    total_crops = local_crops * lax.axis_size("crops")
    full_reduce = gather_first(w_reduce)
    full_spatial, full_expand = gather_pair(w_spatial, w_expand)
    head_whole = lax.all_gather(
        jnp.concatenate([row_quarter(w_hidden), row_quarter(w_embed)], axis=1), BOTH, axis=0, tiled=True
    )
    hidden_cols = w_hidden.shape[1]
    full_hidden, full_embed = head_whole[:, :hidden_cols], head_whole[:, hidden_cols:]

    row_bits = [(0, b) for b in bits_of("rows")]
    crop_count = jnp.sum(pixel_mask.reshape(local_crops, -1), axis=1).astype(F32)
    crop_count = jnp.broadcast_to(crop_count[:, None], (local_crops, 128))
    crop_count = crop_count.reshape((2,) * len(row_bits) + (share, 128))
    for k, step in enumerate(row_bits):
        crop_count = halve(crop_count, len(row_bits) - 1 - k, step, False)
    crop_count = crop_count[:, :1]

    flat_in = features.reshape(-1, channels)
    weight_col = pixel_mask.reshape(-1, 1).astype(F32)
    mask_planes = (
        pixel_mask.transpose(1, 0, 2).reshape(height, local_crops * breadth, 1).astype(F32)
    )

    queue_unit = queued * lax.rsqrt(jnp.sum(queued * queued, axis=1, keepdims=True) + EPS_UNIT)
    queue_scores = jnp.dot(queue_unit, prototypes, precision=PRECISE)
    pre_one = jnp.dot(flat_in, full_reduce, preferred_element_type=F32)
    masked_one = pre_one * weight_col
    sums_one = total_narrow(
        jnp.stack(
            [
                jnp.sum(masked_one, axis=0),
                jnp.sum(masked_one * pre_one, axis=0),
                jnp.full((narrow,), jnp.sum(weight_col)),
            ]
        )
    )
    valid_count = sums_one[2, :1]
    mean_one, spread_one = spread_of(sums_one, valid_count)
    pre_one = pre_one.reshape(local_crops, height, breadth, narrow)
    scale_one = gain_one * spread_one
    hidden_one, slope_one, hidden_sum_one = first_hidden(
        pre_one, mask_planes, scale_one, bias_one - mean_one * scale_one, (queue_scores,)
    )
    above_one, below_one = edge_rows(hidden_one)
    part_two = conv_local(hidden_one, full_spatial, False)
    pre_two, sum_two, square_two = conv_halo(part_two, above_one, below_one, full_spatial, mask_planes)
    sums_two = total_narrow(jnp.stack([sum_two, square_two, hidden_sum_one]))
    mean_two, spread_two = spread_of(sums_two, valid_count)
    hidden_mean_one = sums_two[2] / valid_count
    scale_two = gain_two * spread_two
    hidden_two, slope_two, sum_three, square_three, hidden_sum_two = second_hidden(
        pre_two, weight_col, scale_two, bias_two - mean_two * scale_two, full_expand
    )
    sums_three = total_wide(jnp.concatenate([sum_three, square_three, hidden_sum_two])[None])[0]
    hidden_mean_two = sums_three[2 * channels :] / valid_count
    mean_three, spread_three = spread_of(sums_three[: 2 * channels].reshape(2, -1), valid_count)
    scale_three = gain_three * spread_three
    slope_three, crop_sums, slope_sums = third_output(
        hidden_two, full_expand, flat_in, weight_col, scale_three, bias_three - mean_three * scale_three, height, share
    )
    pooled = crop_sums.reshape((2,) * len(row_bits) + (-1, channels))
    for k, step in enumerate(row_bits):
        pooled = halve(pooled, len(row_bits) - 1 - k, step, False)
    pooled = pooled[:share] / crop_count
    slope_sums = slope_sums.reshape((2,) * len(row_bits) + (-1, 2 * channels))
    for k, step in enumerate(row_bits):
        slope_sums = halve(slope_sums, len(row_bits) - 1 - k, step, False)
    slope_sums = slope_sums[:share]

    pre_head = split_dot(pooled, full_hidden, 0, 3)
    sums_head = total_wide(jnp.stack([jnp.sum(pre_head, axis=0), jnp.sum(pre_head * pre_head, axis=0)]))
    mean_head, spread_head = spread_of(sums_head, F32(total_crops))
    norm_head = (pre_head - mean_head) * spread_head
    hidden_head, slope_head = gelu_both(gain_head * norm_head + bias_head)
    embedding = split_dot(hidden_head, full_embed, 0, 3)
    inverse = lax.rsqrt(jnp.sum(embedding * embedding, axis=1, keepdims=True) + EPS_UNIT)
    unit_embed = embedding * inverse

    partner_rows = (
        lax.dynamic_slice_in_dim(partners, lax.axis_index("rows") * share, share)
        - lax.axis_index("crops") * local_crops
    )
    partner_at = (partner_rows // share ^ lax.axis_index("rows")) * share + partner_rows % share
    row_total = total_crops + queued.shape[0] * lax.axis_size("crops") * row_count
    proto_total = prototypes.shape[1]
    scores = jnp.dot(unit_embed, prototypes, precision=PRECISE)
    plan_mass = jnp.exp(scores / SHARPNESS)
    queue_mass = jnp.exp(queue_scores / SHARPNESS)
    for iteration in range(3):
        column = jnp.sum(plan_mass, axis=0, keepdims=True) + jnp.sum(queue_mass, axis=0, keepdims=True)
        if iteration == 0:
            column, everyone = total_carrying(column, unit_embed)
            partner_embed = jnp.take(everyone, partner_at, axis=0)
            partner_scores = jnp.dot(partner_embed, prototypes, precision=PRECISE)
            partner_mass = jnp.exp(partner_scores / SHARPNESS)
        else:
            column = total_wide(column)
        scale = 1.0 / (proto_total * column)
        partner_mass = partner_mass * scale
        partner_mass = partner_mass / (row_total * jnp.sum(partner_mass, axis=1, keepdims=True))
        if iteration < 2:
            plan_mass = plan_mass * scale
            queue_mass = queue_mass * scale
            plan_mass = plan_mass / (row_total * jnp.sum(plan_mass, axis=1, keepdims=True))
            queue_mass = queue_mass / (row_total * jnp.sum(queue_mass, axis=1, keepdims=True))
    target = row_total * partner_mass
    log_probability = jax.nn.log_softmax(scores / SOFTMAX_TEMPER, axis=1)
    loss_part = -jnp.sum(target * log_probability) / total_crops
    grad_scores = (
        jnp.exp(log_probability) * jnp.sum(target, axis=1, keepdims=True) - target
    ) / (SOFTMAX_TEMPER * total_crops)
    grad_unit = jnp.dot(grad_scores, prototypes.T, precision=PRECISE)
    grad_embedding = inverse * (
        grad_unit - unit_embed * jnp.sum(unit_embed * grad_unit, axis=1, keepdims=True)
    )
    grad_hidden_head = split_dot(grad_embedding, full_embed, 1, 3)
    grad_act_head = grad_hidden_head * slope_head
    sums_back = total_wide(
        jnp.stack(
            [
                jnp.sum(grad_act_head * norm_head, axis=0),
                jnp.sum(grad_act_head, axis=0),
                jnp.full((channels,), loss_part),
            ]
        )
    )
    grad_gain_head, grad_bias_head, swav_loss = sums_back[0], sums_back[1], sums_back[2, 0]
    grad_pre_head = (
        gain_head
        * spread_head
        * (grad_act_head - (grad_bias_head + norm_head * grad_gain_head) / total_crops)
    )
    grad_pooled = split_dot(grad_pre_head, full_hidden, 1, 2)
    per_pixel = grad_pooled / crop_count
    scale_rows = gather_rows(per_pixel)

    crop_index = lax.axis_index("crops")
    proto_pad = -proto_total % 128
    forward_all = gather_products([pooled, hidden_head, unit_embed], True, ())
    backward_all = gather_products(
        [grad_pre_head, grad_embedding, jnp.pad(grad_scores, ((0, 0), (0, proto_pad)))],
        False,
        (slope_sums, forward_all),
    )
    shard_hidden, shard_embed, width = w_hidden.shape[0], w_embed.shape[0], w_embed.shape[1]

    def product_of(at, size, to, count):
        return lax.dot_general(
            lax.dynamic_slice_in_dim(forward_all, at, size, 1),
            lax.slice_in_dim(backward_all, to, to + count, axis=1),
            TN,
            preferred_element_type=F32,
        )

    out_hidden = product_of(crop_index * shard_hidden, shard_hidden, 0, hidden_cols)
    out_embed = product_of(channels + crop_index * shard_embed, shard_embed, hidden_cols, width)
    grad_prototypes = product_of(channels + hidden_cols, width, hidden_cols + width, proto_total)

    sums_three_back = jnp.sum(jnp.concatenate([per_pixel, per_pixel], axis=1) * slope_sums, axis=0)
    sums_three_back = total_wide(sums_three_back[None])[0]
    grad_bias_three = sums_three_back[:channels]
    alpha, beta, gamma, grad_gain_three = back_consts(
        gain_three, mean_three, spread_three, valid_count, grad_bias_three, sums_three_back[channels:]
    )
    grad_w_expand, total_three, grad_act_two, sum_back, dot_back = third_back(
        hidden_two,
        full_expand,
        slope_three,
        weight_col,
        scale_rows * alpha,
        beta,
        gamma,
        slope_two,
        pre_two,
        hidden_mean_two,
    )
    sums_two_back = total_narrow(jnp.stack([sum_back, dot_back]))
    grad_bias_two = sums_two_back[0]
    alpha, beta, gamma, grad_gain_two = back_consts(
        gain_two, mean_two, spread_two, valid_count, grad_bias_two, sums_two_back[1]
    )
    grad_pre_two, total_two = second_back(
        grad_act_two, pre_two, mask_planes, alpha, beta, gamma, ()
    )
    above_two, below_two = edge_rows(grad_pre_two)
    part_one = conv_local(grad_pre_two, full_spatial, True)
    grad_act_one, sum_back, dot_back = conv_back_halo(
        part_one, above_two, below_two, full_spatial, slope_one, pre_one, ()
    )
    sums_one_back = total_narrow(
        jnp.concatenate([sum_back, dot_back, total_two, total_three]).reshape(-1, narrow)
    )
    grad_w_spatial = spatial_grad(
        hidden_one,
        above_one,
        below_one,
        grad_pre_two,
        hidden_mean_one,
        total_two,
        (grad_act_one,),
    )
    grad_bias_one = sums_one_back[0]
    alpha, beta, gamma, grad_gain_one = back_consts(
        gain_one, mean_one, spread_one, valid_count, grad_bias_one, sums_one_back[1]
    )
    spatial_core = core_exchange(grad_w_spatial, (alpha,))
    blocks = channels // narrow
    spatial_rows, *lane_rows = [
        n // row_count for n in (w_spatial.shape[0], w_reduce.shape[0], blocks * w_expand.shape[0])
    ]
    grad_pre_one, grad_w_reduce = first_back(
        grad_act_one, pre_one, weight_col, alpha, beta, gamma, flat_in, (spatial_core[0],)
    )
    near = near_exchange([spatial_core], [spatial_rows])
    lines = [
        line_exchange(core_exchange(g), n) for g, n in zip((grad_w_reduce, grad_w_expand), lane_rows)
    ]
    grad_features = last_grads(
        grad_pre_one,
        full_reduce,
        slope_three,
        scale_rows,
        height,
        (out_hidden, out_embed, grad_prototypes, near[0], *[parts[0] for parts in lines]),
    )
    far = far_exchange(near, (grad_features,))
    lane = near_exchange(lines, lane_rows, (grad_features,))
    lane = exchange([lane], reduce_steps()[2][:-1], [sum(lane_rows)])
    out_spatial = reduce_end(far).reshape(w_spatial.shape)
    sums = reduce_end(lane).reshape(row_count, -1, narrow)
    out_reduce = sums[:, : lane_rows[0]].reshape(w_reduce.shape)
    out_expand = sums[:, lane_rows[0] :].reshape(row_count, blocks, -1, narrow)
    out_expand = out_expand.transpose(0, 2, 1, 3).reshape(w_expand.shape)
    grad_features = grad_features.reshape(features.shape)

    grad_totals = sums_one_back[2:].reshape(-1)
    tap_means = jnp.tile(hidden_mean_one, 9)
    shard_expand, shard_spatial = w_expand.shape[0], w_spatial.shape[0]
    means = lax.dynamic_slice_in_dim(hidden_mean_two, crop_index * shard_expand, shard_expand)
    out_expand = out_expand + means[:, None] * grad_totals[narrow:]
    means = lax.dynamic_slice_in_dim(tap_means, crop_index * shard_spatial, shard_spatial)
    out_spatial = out_spatial + means[:, None] * grad_totals[:narrow]
    return (
        swav_loss,
        grad_features,
        out_reduce,
        out_spatial,
        out_expand,
        out_hidden,
        out_embed,
        grad_prototypes,
        grad_gain_one,
        grad_bias_one,
        grad_gain_two,
        grad_bias_two,
        grad_gain_three,
        grad_bias_three,
        grad_gain_head,
        grad_bias_head,
    )


def solution(mesh):
    split = P("crops", None)
    map_spec = P("crops", "rows", None, None)
    in_specs = (
        (map_spec, P("crops", "rows", None), P("crops"), P(BOTH, None)) + (split,) * 5 + (P(),) * 9
    )
    out_specs = (P(), map_spec) + (split,) * 5 + (P(),) * 9
    return jax.shard_map(shards, mesh=mesh, in_specs=in_specs, out_specs=out_specs, check_vma=False)
```

```python
import functools
import itertools
import math

import jax
import jax.numpy as jnp
from jax import lax
from jax.experimental import pallas as pl
from jax.experimental.pallas import tpu as pltpu
from jax.sharding import PartitionSpec as P

EPS_NORM = 1e-05
EPS_UNIT = 1e-06
SHARPNESS = 0.05
SOFTMAX_TEMPER = 0.1
PRECISE = lax.Precision.HIGHEST
BOTH = ("crops", "rows")
GELU_SCALE = 0.7978845608028654
GELU_CUBE = 0.044715
F32 = jnp.float32
BF16 = jnp.bfloat16


def bits_of(axis):
    return [1 << k for k in range(lax.axis_size(axis).bit_length() - 1)]


def xor_permute(values, crop_xor, row_xor):
    crop_total, row_total = lax.axis_size("crops"), lax.axis_size("rows")
    pairs = [
        (c * row_total + r, (c ^ crop_xor) * row_total + (r ^ row_xor))
        for c in range(crop_total)
        for r in range(row_total)
    ]
    return lax.ppermute(values, BOTH, pairs)


def all_bits():
    return [(0, b) for b in bits_of("rows")] + [(b, 0) for b in bits_of("crops")]


def total_wide(values):
    steps = all_bits()
    groups = [steps[:1]] + [steps[k : k + 2] for k in range(1, len(steps), 2)]
    for group in groups:
        if len(group) == 1:
            values = values + xor_permute(values, *group[0])
        else:
            (a, b), (c, d) = group
            near = xor_permute(values, a, b)
            far = xor_permute(values, c, d)
            both = xor_permute(values, a ^ c, b ^ d)
            values = (values + near) + (far + both)
    return values


def total_carrying(values, rows_extra):
    width, own = values.shape[1], rows_extra.reshape(1, -1)
    slots = {0: own}
    steps = all_bits()
    groups = [steps[:1]] + [steps[k : k + 2] for k in range(1, len(steps), 2)]

    def send(step, current):
        if step[0]:
            return xor_permute(current, *step), {}
        keys = sorted(slots)
        got = xor_permute(jnp.concatenate([current] + [slots[k] for k in keys], axis=1), *step)
        parts = jnp.split(got[:, width:], len(keys), axis=1)
        return got[:, :width], {k ^ step[1]: part for k, part in zip(keys, parts)}

    for group in groups:
        if len(group) == 1:
            other, more = send(group[0], values)
            values = values + other
            slots.update(more)
        else:
            (a, b), (c, d) = group
            near, near_slots = send((a, b), values)
            far, far_slots = send((c, d), values)
            both, both_slots = send((a ^ c, b ^ d), values)
            values = (values + near) + (far + both)
            for more in (near_slots, far_slots, both_slots):
                slots.update(more)
    stacked = jnp.concatenate([slots[k] for k in sorted(slots)], axis=0)
    return values, stacked.reshape(-1, rows_extra.shape[1])


def total_narrow(values):
    count = lax.axis_size("crops") * lax.axis_size("rows")
    copies = jnp.broadcast_to(values[None], (count,) + values.shape)
    return jnp.sum(lax.all_to_all(copies, BOTH, 0, 0, tiled=True), axis=0)


def my_bit(step):
    crop_xor, row_xor = step
    if crop_xor:
        return (lax.axis_index("crops") // crop_xor) % 2
    return (lax.axis_index("rows") // row_xor) % 2


def halve(values, dim, step, narrow):
    bit = my_bit(step)
    kept = lax.dynamic_index_in_dim(values, bit, dim, keepdims=False)
    sent = lax.dynamic_index_in_dim(values, 1 - bit, dim, keepdims=False)
    if narrow:
        sent = sent.astype(BF16)
    return kept.astype(F32) + xor_permute(sent, *step).astype(F32)


def double(values, step):
    other = xor_permute(values, *step)
    low = my_bit(step) == 0
    return jnp.stack([jnp.where(low, values, other), jnp.where(low, other, values)])


def gather_rows(values):
    row_bits = [(0, b) for b in bits_of("rows")]
    count = len(row_bits)
    rows, cols = values.shape
    for step in reversed(row_bits):
        values = double(values, step)
    values = values.transpose(tuple(range(count - 1, -1, -1)) + (count, count + 1))
    return values.reshape(-1, cols)


def row_quarter(weight):
    size = weight.shape[0] // lax.axis_size("rows")
    return lax.dynamic_slice_in_dim(weight, lax.axis_index("rows") * size, size)


def gather_first(weight):
    crop_total = lax.axis_size("crops")
    size, cols = weight.shape[0] // 2, weight.shape[1]
    bit = lax.axis_index("rows") % 2
    mine = lax.dynamic_slice_in_dim(weight, bit * size, size)
    mine = lax.all_to_all(
        jnp.broadcast_to(mine[None], (crop_total, size, cols)), "crops", 0, 0, tiled=True
    )
    other = xor_permute(mine, 0, 1)
    low = bit == 0
    both = jnp.stack([jnp.where(low, mine, other), jnp.where(low, other, mine)], axis=1)
    return both.reshape(2 * crop_total * size, cols)


def gather_pair(first, second):
    quarter_one, quarter_two = row_quarter(first), row_quarter(second)
    cols = first.shape[1]
    blocks = second.shape[1] // cols
    size, short = quarter_one.shape[0], quarter_two.shape[0]
    flat_two = quarter_two.reshape(short, blocks, cols).transpose(1, 0, 2).reshape(-1, cols)
    whole = lax.all_gather(jnp.concatenate([quarter_one, flat_two], axis=0), BOTH, axis=0, tiled=False)
    count = whole.shape[0]
    second_blocks = whole[:, size:].reshape(count, blocks, short, cols).transpose(1, 0, 2, 3)
    if size % 16:
        whole, size = whole[:, :size].reshape(1, -1, cols), count * size
    return (whole, size), second_blocks.reshape(blocks, -1, cols)


def spread_of(sums, count):
    mean = sums[0] / count
    return mean, lax.rsqrt(sums[1] / count - mean * mean + EPS_NORM)


def gelu_both(x, mask=None):
    square = x * x
    half = 0.5 * jnp.tanh(x * (GELU_SCALE + GELU_SCALE * GELU_CUBE * square)) + 0.5
    inner = x * (2.0 * GELU_SCALE + 6.0 * GELU_SCALE * GELU_CUBE * square)
    kept = half if mask is None else half * mask
    return x * kept, kept * (1.0 + (1.0 - half) * inner)


def split_parts(x, parts):
    pieces = []
    for _ in range(parts - 1):
        piece = lax.reduce_precision(x, 8, 7)
        pieces.append(piece.astype(BF16))
        x = x - piece
    pieces.append(x.astype(BF16))
    return jnp.concatenate(pieces, axis=0)


def split_dot(x, matrix, dim, parts):
    count = x.shape[0]
    out = lax.dot_general(
        split_parts(x, parts), matrix, (((1,), (dim,)), ((), ())), preferred_element_type=F32
    )
    total = out[(parts - 1) * count :]
    for k in range(parts - 2, -1, -1):
        total = total + out[k * count : (k + 1) * count]
    return total


TN = (((0,), (0,)), ((), ()))
NT = (((1,), (1,)), ((), ()))
TILE = 16
UNROLL = 16


def kernel_call(body, grid, ins, outs, scratch, args, flops, transcendentals=0, deps=()):
    moved = sum(a.size * a.dtype.itemsize for a in args) + sum(
        math.prod(s.shape) * s.dtype.itemsize for s, _ in outs
    )
    count = len(ins)

    def inner(*refs):
        body(*refs[:count], *refs[count + len(deps) :])

    return pl.pallas_call(
        inner,
        grid=(grid,),
        in_specs=ins + [pl.BlockSpec(memory_space=pl.ANY)] * len(deps),
        out_specs=[spec for _, spec in outs],
        out_shape=[shape for shape, _ in outs],
        scratch_shapes=scratch,
        compiler_params=pltpu.CompilerParams(vmem_limit_bytes=52 * 2**20),
        cost_estimate=pl.CostEstimate(
            flops=flops, bytes_accessed=moved, transcendentals=transcendentals
        ),
    )(*args, *deps)


def whole_block(array):
    zeros = (0,) * array.ndim
    return pl.BlockSpec(array.shape, lambda k: zeros)


def spatial_block(weight):
    array, size = weight
    return pl.BlockSpec((array.shape[0], size, array.shape[2]), lambda k: (0, 0, 0))


def sum_block(width):
    return jax.ShapeDtypeStruct((8, width), F32), pl.BlockSpec((8, width), lambda k: (0, 0))


def tall(row):
    return jnp.broadcast_to(row.reshape(1, -1), (TILE, row.size))


def fold(values):
    return values[:8] + values[8:]


def loop(count, step, start):
    return lax.fori_loop(0, count, step, start, unroll=math.gcd(count, UNROLL))


def clear_first(*refs):
    @pl.when(pl.program_id(0) == 0)
    def _():
        for ref in refs:
            ref[...] = jnp.zeros_like(ref)


def planes_of(height, width, rows):
    return pl.BlockSpec((height, rows, width), lambda k: (0, k, 0))


def rows_block(rows, width):
    return pl.BlockSpec((rows, width), lambda k: (k, 0))


def plane_out(total, width, rows):
    return jax.ShapeDtypeStruct((total, width), BF16), rows_block(rows, width)


def gather_tile(ref, index, height):
    if height == 1:
        return ref[0, pl.ds(pl.multiple_of(index * TILE, TILE), TILE), :]
    return jnp.concatenate(
        [ref[i, pl.ds(pl.multiple_of(index * 8, 8), 8), :] for i in range(height)], axis=0
    )


def store_tile(ref, index, values, height):
    if height == 1:
        ref[0, pl.ds(pl.multiple_of(index * TILE, TILE), TILE), :] = values
    else:
        for i in range(height):
            ref[i, pl.ds(pl.multiple_of(index * 8, 8), 8), :] = values[8 * i : 8 * i + 8]


def tile_rows(index):
    return pl.ds(pl.multiple_of(index * TILE, TILE), TILE)


def merge_body(counts, place_ref, *refs):
    step = pl.program_id(0)
    at, rows, totals = 0, 0, []
    for count in counts:
        total = refs[at][...].astype(F32)
        for ref in refs[at + 1 : at + count]:
            total = total + ref[...].astype(F32)
        lead, _, inner, cols = total.shape
        totals.append((rows, inner, total.astype(BF16).reshape(lead, inner, cols)))
        at, rows = at + count, rows + inner
    for k, out_ref in enumerate(refs[at:]):

        @pl.when(step == k)
        def _(out_ref=out_ref):
            for first, inner, total in totals:
                out_ref[:, first : first + inner, :] = total


def merge_split(groups, place, deps):
    lead, split, _, cols = groups[0][0].shape
    counts = [len(parts) for parts in groups]
    inner = sum(parts[0].shape[2] for parts in groups)
    args = [part for parts in groups for part in parts]

    def body(place_ref, *refs):
        merge_body(counts, place_ref, *refs[: len(args)], *refs[len(args) + len(deps) :])

    return pl.pallas_call(
        body,
        grid_spec=pltpu.PrefetchScalarGridSpec(
            num_scalar_prefetch=1,
            grid=(split,),
            in_specs=[
                pl.BlockSpec(
                    (lead, 1, part.shape[2], cols), lambda k, at: (0, jnp.bitwise_xor(at[0], k), 0, 0)
                )
                for part in args
            ]
            + [pl.BlockSpec(memory_space=pl.ANY)] * len(deps),
            out_specs=[pl.BlockSpec((lead, inner, cols), lambda k, at: (0, 0, 0))] * split,
        ),
        out_shape=[jax.ShapeDtypeStruct((lead, inner, cols), BF16)] * split,
        compiler_params=pltpu.CompilerParams(vmem_limit_bytes=52 * 2**20),
        cost_estimate=pl.CostEstimate(
            flops=sum(a.size for a in args), bytes_accessed=3 * sum(a.size for a in args), transcendentals=0
        ),
    )(jnp.reshape(place, (1,)).astype(jnp.int32), *args, *deps)


def reduce_steps():
    row_bits = [(0, b) for b in reversed(bits_of("rows"))]
    crop_bits = [(b, 0) for b in reversed(bits_of("crops"))]
    return [row_bits[-1:], crop_bits[-1:] + row_bits[:-1], crop_bits[:-1]]


def device_count():
    return lax.axis_size("crops") * lax.axis_size("rows")


def exchange(groups, bits, inner, deps=()):
    split = 2 ** len(bits)
    place = sum(my_bit(step) << k for k, step in enumerate(reversed(bits)))
    groups = [[p.reshape(-1, split, n, p.shape[-1]) for p in parts] for parts, n in zip(groups, inner)]
    pieces = merge_split(groups, place, deps)
    parts = [pieces[0]]
    for flips in range(1, split):
        chosen = [step for k, step in enumerate(reversed(bits)) if flips >> k & 1]
        parts.append(xor_permute(pieces[flips], sum(b for b, _ in chosen), sum(b for _, b in chosen)))
    return parts


def core_exchange(values, deps=()):
    inner = values.shape[0] // device_count()
    return exchange([[values]], reduce_steps()[0], [inner], deps)


def near_exchange(groups, inner, deps=()):
    return exchange(groups, reduce_steps()[1], inner, deps)


def far_exchange(parts, deps=()):
    return exchange([parts], reduce_steps()[2], [parts[0].shape[-2]], deps)


def line_exchange(parts, inner):
    _, near, far = reduce_steps()
    return exchange([parts], far[-1:], [inner * 2 ** len(near)])


def reduce_end(parts, deps=()):
    (total,) = merge_split([[p[:, None] for p in parts]], jnp.int32(0), deps)
    return gather_rows(total.reshape(total.shape[1:])).astype(F32)


def pack_body(centred, *refs):
    *ins, out_ref, rows_ref = refs
    at = 0
    for ref in ins:
        share, width = ref.shape
        cols = slice(at, at + width)
        at += width
        values = ref[...]
        extra = jnp.sum(values, axis=0, keepdims=True)
        if centred:
            extra = extra * (1.0 / share)
            values = values - extra
        high = extra.astype(BF16).astype(F32)
        low = extra - high
        rows_ref[:share, cols] = values
        order = (high, high, low, low) if centred else (high, low, high, low)
        for j, row in enumerate(order):
            rows_ref[share + j : share + j + 1, cols] = row
    out_ref[...] = rows_ref[...].astype(BF16)


def gather_products(arrays, centred, deps):
    widths = [a.shape[1] for a in arrays]
    rows = arrays[0].shape[0] + 4
    (packed,) = kernel_call(
        functools.partial(pack_body, centred),
        1,
        [whole_block(a) for a in arrays],
        [
            (
                jax.ShapeDtypeStruct((rows, sum(widths)), BF16),
                pl.BlockSpec((rows, sum(widths)), lambda k: (0, 0)),
            )
        ],
        [pltpu.VMEM((rows, sum(widths)), F32)],
        tuple(arrays),
        6 * rows * sum(widths),
        deps=deps,
    )
    return lax.all_gather(packed, BOTH, axis=0, tiled=True)


def first_body(height, x_ref, m_ref, c_ref, *refs):
    hidden_refs, (slope_ref, sum_ref) = refs[:height], refs[height:]
    clear_first(sum_ref)
    pairs = x_ref.shape[0] // 2
    width = x_ref.shape[3]
    for i in range(height):

        def step(k, carry):
            x = x_ref[pl.ds(pl.multiple_of(2 * k, 2), 2), i].reshape(TILE, width)
            m = m_ref[i, tile_rows(k), :]
            value, slope = gelu_both(c_ref[:TILE] * x + c_ref[TILE:], m)
            hidden = value.astype(BF16)
            hidden_refs[i][tile_rows(k), :] = hidden
            slope_ref[i, tile_rows(k), :] = slope
            return carry + fold(hidden.astype(F32))

        sum_ref[...] += loop(pairs, step, jnp.zeros(sum_ref.shape, F32))


def first_hidden(pre_one, mask_planes, scale, shift, deps):
    crops, height, breadth, width = pre_one.shape
    tile = 16
    consts = jnp.concatenate([tall(scale), tall(shift)], axis=0)
    planes = planes_of(height, width, tile * 8)
    *hidden, slope, sums = kernel_call(
        functools.partial(first_body, height),
        crops // tile,
        [
            pl.BlockSpec((tile, height, 8, width), lambda k: (k, 0, 0, 0)),
            planes_of(height, 1, tile * 8),
            whole_block(consts),
        ],
        [
            *[plane_out(crops * 8, width, tile * 8)] * height,
            (jax.ShapeDtypeStruct((height, crops * 8, width), F32), planes),
            sum_block(width),
        ],
        [],
        (pre_one, mask_planes, consts),
        40 * pre_one.size,
        pre_one.size,
        deps,
    )
    return hidden, slope, jnp.sum(sums, axis=0)


def shifted(values, back):
    wide = values.astype(F32).reshape(2, 8, values.shape[1])
    place = lax.broadcasted_iota(jnp.int32, wide.shape, 1)
    before = jnp.where(place == 0, 0.0, pltpu.roll(wide, 1, 1)).reshape(values.shape).astype(BF16)
    after = jnp.where(place == 7, 0.0, pltpu.roll(wide, 7, 1)).reshape(values.shape).astype(BF16)
    return (after, before) if back else (before, after)


def fill_taps(read, out_ref, back):
    width = out_ref.shape[1] // 3

    def step(k, carry):
        values = read(k)
        low, high = shifted(values, back)
        out_ref[tile_rows(k), :width] = low
        out_ref[tile_rows(k), width : 2 * width] = values
        out_ref[tile_rows(k), 2 * width :] = high
        return carry

    loop(out_ref.shape[0] // TILE, step, 0)


def tap_dot(taps, w_ref, tap_row, back):
    width = taps.shape[1] // 3
    w_ref = w_ref.reshape(w_ref.shape[0] * w_ref.shape[1], w_ref.shape[2])
    if not back:
        return jnp.dot(
            taps, w_ref[3 * width * tap_row : 3 * width * (tap_row + 1), :], preferred_element_type=F32
        )
    total = None
    for b in range(3):
        at = (3 * tap_row + b) * width
        part = lax.dot_general(
            taps[:, b * width : (b + 1) * width],
            w_ref[at : at + width, :],
            NT,
            preferred_element_type=F32,
        )
        total = part if total is None else total + part
    return total


def local_body(height, back, *refs):
    w_ref, out_ref, taps_ref = refs[height:]
    for p in range(height):
        fill_taps(lambda k, p=p: refs[p][tile_rows(k), :], taps_ref.at[p], back)
    for i in range(height):
        total = None
        for p in range(height):
            tap_row = i - p + 1 if back else p - i + 1
            if 0 <= tap_row <= 2:
                part = tap_dot(taps_ref[p], w_ref, tap_row, back)
                total = part if total is None else total + part
        out_ref[i] = total


def conv_local(planes, weight, back):
    height = len(planes)
    rows, width = planes[0].shape
    parts = 2 if rows % 32 == 0 else 1
    (out,) = kernel_call(
        functools.partial(local_body, height, back),
        parts,
        [rows_block(rows // parts, width)] * height + [spatial_block(weight)],
        [(jax.ShapeDtypeStruct((height, rows, width), F32), planes_of(height, width, rows // parts))],
        [pltpu.VMEM((height, rows // parts, 3 * width), BF16)],
        (*planes, weight[0]),
        2 * rows * (3 * height - 2) * 3 * width * width,
    )
    return out


def add_halo(height, back, part_ref, above_ref, below_ref, w_ref, taps_ref):
    fill_taps(lambda k: above_ref[tile_rows(k), :], taps_ref.at[0], back)
    fill_taps(lambda k: below_ref[tile_rows(k), :], taps_ref.at[1], back)
    upper = tap_dot(taps_ref[0], w_ref, 2 if back else 0, back)
    lower = tap_dot(taps_ref[1], w_ref, 0 if back else 2, back)
    if height == 1:
        return [part_ref[0] + (upper + lower)]
    middle = [part_ref[i] for i in range(1, height - 1)]
    return [part_ref[0] + upper] + middle + [part_ref[height - 1] + lower]


def halo_body(height, part_ref, above_ref, below_ref, w_ref, m_ref, out_ref, sum_ref, square_ref, taps_ref):
    clear_first(sum_ref, square_ref)
    rows = add_halo(height, False, part_ref, above_ref, below_ref, w_ref, taps_ref)
    for i in range(height):
        out_ref[i] = rows[i]
    for i in range(height):

        def step(k, carry):
            x = out_ref[i, tile_rows(k), :]
            first = x * m_ref[i, tile_rows(k), :]
            return carry[0] + fold(first), carry[1] + fold(first * x)

        zero = jnp.zeros(sum_ref.shape, F32)
        first, second = loop(out_ref.shape[1] // TILE, step, (zero, zero))
        sum_ref[...] += first
        square_ref[...] += second


def conv_halo(part, above, below, weight, mask_planes):
    height, rows, width = part.shape
    parts = 2 if rows % 32 == 0 else 1
    size = rows // parts
    block = planes_of(height, width, size)
    edge = pl.BlockSpec((size, width), lambda k: (k, 0))
    out, first, second = kernel_call(
        functools.partial(halo_body, height),
        parts,
        [block, edge, edge, spatial_block(weight), planes_of(height, 1, size)],
        [(jax.ShapeDtypeStruct(part.shape, F32), block), sum_block(width), sum_block(width)],
        [pltpu.VMEM((2, size, 3 * width), BF16)],
        (part, above, below, weight[0], mask_planes),
        2 * rows * 2 * 3 * width * width,
    )
    return out, jnp.sum(first, axis=0), jnp.sum(second, axis=0)


def halo_back_body(
    height, part_ref, above_ref, below_ref, w_ref, slope_ref, x_ref, out_ref, sum_ref, dot_ref, taps_ref
):
    clear_first(sum_ref, dot_ref)
    rows = add_halo(height, True, part_ref, above_ref, below_ref, w_ref, taps_ref)
    for i in range(height):
        out_ref[i] = rows[i]
    width = out_ref.shape[2]
    for i in range(height):

        def step(k, carry):
            g = out_ref[i, tile_rows(k), :] * slope_ref[i, tile_rows(k), :]
            out_ref[i, tile_rows(k), :] = g
            x = x_ref[pl.ds(pl.multiple_of(2 * k, 2), 2), i].reshape(TILE, width)
            return carry[0] + fold(g), carry[1] + fold(g * x)

        zero = jnp.zeros(sum_ref.shape, F32)
        first, second = loop(out_ref.shape[1] // TILE, step, (zero, zero))
        sum_ref[...] += first
        dot_ref[...] += second


def conv_back_halo(part, above, below, weight, slope, pre_one, deps):
    height, rows, width = part.shape
    parts = 2 if rows % 32 == 0 else 1
    size = rows // parts
    block = planes_of(height, width, size)
    edge = pl.BlockSpec((size, width), lambda k: (k, 0))
    out, first, second = kernel_call(
        functools.partial(halo_back_body, height),
        parts,
        [
            block,
            edge,
            edge,
            spatial_block(weight),
            block,
            pl.BlockSpec((size // 8, height, 8, width), lambda k: (k, 0, 0, 0)),
        ],
        [(jax.ShapeDtypeStruct(part.shape, F32), block), sum_block(width), sum_block(width)],
        [pltpu.VMEM((2, size, 3 * width), BF16)],
        (part, above, below, weight[0], slope, pre_one),
        2 * rows * 2 * 3 * width * width,
        deps=deps,
    )
    return out, jnp.sum(first, axis=0), jnp.sum(second, axis=0)


def spatial_grad_body(height, *refs):
    x_refs, (above_ref, below_ref), g_refs = refs[:height], refs[height : height + 2], refs[height + 2 : -4]
    mean_ref, total_ref, out_ref, taps_ref = refs[-4:]
    rows = above_ref.shape[0]
    reads = [lambda k: above_ref[tile_rows(k), :]]
    reads += [lambda k, ref=ref: ref[tile_rows(k), :] for ref in x_refs]
    reads += [lambda k: below_ref[tile_rows(k), :]]
    for b in range(3):

        @pl.when(pl.program_id(0) == b)
        def _(b=b):
            for p in range(height + 2):

                def step(k, carry, p=p):
                    values = reads[p](k)
                    if b != 1:
                        values = shifted(values, False)[b // 2]
                    taps_ref[p, tile_rows(k), :] = values
                    return carry

                loop(rows // TILE, step, 0)

    for a in range(3):
        total = None
        for i in range(height):
            part = lax.dot_general(taps_ref[i + a], g_refs[i][...], TN, preferred_element_type=F32)
            total = part if total is None else total + part
        out_ref[a, 0] = (total - mean_ref[...] * total_ref[...]).astype(BF16)


def spatial_grad(hidden, above, below, grads, hidden_mean, grad_total, deps):
    height = len(hidden)
    rows, width = above.shape
    mean, total = hidden_mean.reshape(width, 1), grad_total.reshape(1, width)
    (out,) = kernel_call(
        functools.partial(spatial_grad_body, height),
        3,
        [whole_block(a) for a in (*hidden, above, below, *grads, mean, total)],
        [
            (
                jax.ShapeDtypeStruct((3, 3, width, width), BF16),
                pl.BlockSpec((3, 1, width, width), lambda k: (0, k, 0, 0)),
            )
        ],
        [pltpu.VMEM((height + 2, rows, width), BF16)],
        (*hidden, above, below, *grads, mean, total),
        2 * 9 * height * rows * width * width,
        deps=deps,
    )
    return out.reshape(9 * width, width)


def second_body(height, x_ref, m_ref, c_ref, w_ref, hidden_ref, slope_ref, sum_ref, square_ref, mean_ref, y_ref):
    clear_first(sum_ref, square_ref, mean_ref)
    tiles = hidden_ref.shape[0] // TILE

    def step(k, carry):
        x = gather_tile(x_ref, k, height)
        m = m_ref[tile_rows(k), :]
        value, slope = gelu_both(c_ref[:TILE] * x + c_ref[TILE:], m)
        hidden = value.astype(BF16)
        hidden_ref[tile_rows(k), :] = hidden
        store_tile(slope_ref, k, slope, height)
        return carry + fold(hidden.astype(F32))

    mean_ref[...] += loop(tiles, step, jnp.zeros(mean_ref.shape, F32))
    half = w_ref.shape[2]
    for part in range(w_ref.shape[0]):
        cols = slice(part * half, (part + 1) * half)
        y_ref[:, cols] = jnp.dot(hidden_ref[...], w_ref[part], preferred_element_type=F32)

        def add(k, carry):
            y = y_ref[tile_rows(k), cols]
            return carry[0] + fold(y), carry[1] + fold(y * y)

        zero = jnp.zeros((8, half), F32)
        first, second = loop(tiles, add, (zero, zero))
        sum_ref[:, cols] += first
        square_ref[:, cols] += second


def second_hidden(pre_two, mask_flat, scale, shift, weight):
    height, rows, width = pre_two.shape
    channels = weight.shape[0] * weight.shape[2]
    crops = rows // 8
    tile = 16
    flat = tile * height * 8
    consts = jnp.concatenate([tall(scale), tall(shift)], axis=0)
    hidden, slope, first, second, mean = kernel_call(
        functools.partial(second_body, height),
        crops // tile,
        [
            planes_of(height, width, tile * 8),
            pl.BlockSpec((flat, 1), lambda k: (k, 0)),
            whole_block(consts),
            whole_block(weight),
        ],
        [
            (jax.ShapeDtypeStruct((height * rows, width), BF16), pl.BlockSpec((flat, width), lambda k: (k, 0))),
            (jax.ShapeDtypeStruct(pre_two.shape, F32), planes_of(height, width, tile * 8)),
            sum_block(channels),
            sum_block(channels),
            sum_block(width),
        ],
        [pltpu.VMEM((flat, channels), F32)],
        (pre_two, mask_flat, consts, weight),
        2 * height * rows * width * channels,
        pre_two.size,
    )
    return hidden, slope, jnp.sum(first, axis=0), jnp.sum(second, axis=0), jnp.sum(mean, axis=0)


def third_body(
    height, share, h_ref, w_ref, f_ref, m_ref, c_ref, slope_ref, pool_ref, sums_ref, y_ref
):
    crops = h_ref.shape[0] // (height * 8)
    channels = y_ref.shape[1]
    start = pl.program_id(0) * crops
    padding = -share % 8
    pixels = height * 8
    step_rows = max(pixels, TILE)
    per_step = step_rows // pixels
    chunk = w_ref.shape[2]
    for part in range(w_ref.shape[0]):
        cols = slice(part * chunk, (part + 1) * chunk)
        y_ref[:, cols] = jnp.dot(h_ref[...], w_ref[part], preferred_element_type=F32)

        def step(k, carry):
            at = pl.ds(pl.multiple_of(k * step_rows, TILE), step_rows)
            y = y_ref[at, cols]
            m = m_ref[at, :]
            s = y.reshape(-1, TILE, chunk) * c_ref[:TILE, cols] + c_ref[TILE:, cols]
            s = s.reshape(step_rows, chunk) + f_ref[at, cols].astype(F32)
            value, slope = gelu_both(s, m)
            slope_ref[at, cols] = slope.astype(BF16)
            for j in range(per_step):
                rows = slice(j * pixels, (j + 1) * pixels)
                pooled_at = start + k * per_step + j
                at_crop = pl.ds(pooled_at + pooled_at // share * padding, 1)
                pool_ref[at_crop, cols] = jnp.sum(value[rows], axis=0, keepdims=True)
                sums_ref[at_crop, cols] = jnp.sum(slope[rows], axis=0, keepdims=True)
                sums_ref[at_crop, slice(cols.start + channels, cols.stop + channels)] = jnp.sum(
                    slope[rows] * y[rows], axis=0, keepdims=True
                )
            return carry

        loop(crops // per_step, step, 0)


def third_output(hidden, weight, features, mask_flat, scale, shift, height, share):
    total, width = hidden.shape
    channels = weight.shape[0] * weight.shape[2]
    tile = 16
    flat = tile * height * 8
    crops = total // (height * 8)
    consts = jnp.concatenate([tall(scale), tall(shift)], axis=0)
    rows_of = lambda n: pl.BlockSpec((flat, n), lambda k: (k, 0))
    padded = crops // share * (share + -share % 8)
    kept = lambda n: (jax.ShapeDtypeStruct((padded, n), F32), pl.BlockSpec((padded, n), lambda k: (0, 0)))
    return kernel_call(
        functools.partial(third_body, height, share),
        crops // tile,
        [rows_of(width), whole_block(weight), rows_of(channels), rows_of(1), whole_block(consts)],
        [
            (jax.ShapeDtypeStruct((total, channels), BF16), rows_of(channels)),
            kept(channels),
            kept(2 * channels),
        ],
        [pltpu.VMEM((flat, channels), F32)],
        (hidden, weight, features, mask_flat, consts),
        2 * total * width * channels + 40 * total * channels,
        total * channels,
    )


def third_back_body(
    height,
    inner,
    h_ref,
    w_ref,
    d_ref,
    m_ref,
    s_ref,
    c_ref,
    slope_ref,
    x_ref,
    mean_ref,
    centred_ref,
    total_ref,
    out_ref,
    sum_ref,
    dot_ref,
    y_ref,
    g_ref,
    back_ref,
    grad_ref,
):
    clear_first(grad_ref, total_ref, sum_ref, dot_ref)
    crops = s_ref.shape[0]
    pixels = height * 8
    step_rows = max(pixels, TILE)
    per_step = step_rows // pixels
    chunk = w_ref.shape[2]
    for part in range(w_ref.shape[0]):
        cols = slice(part * chunk, (part + 1) * chunk)
        y_ref[:, cols] = jnp.dot(h_ref[...], w_ref[part], preferred_element_type=F32)

        def step(k, carry):
            at = pl.ds(pl.multiple_of(k * step_rows, TILE), step_rows)
            scales = [
                jnp.broadcast_to(s_ref[pl.ds(k * per_step + j, 1), cols], (pixels, chunk))
                for j in range(per_step)
            ]
            scale = scales[0] if per_step == 1 else jnp.concatenate(scales, axis=0)
            line = y_ref[at, cols].reshape(-1, TILE, chunk) * c_ref[TILE:, cols] + c_ref[:TILE, cols]
            g = d_ref[at, cols].astype(F32) * scale + m_ref[at, :] * line.reshape(step_rows, chunk)
            g = g.astype(BF16)
            g_ref[at, cols] = g
            g = g.astype(F32)
            return carry + jnp.sum(g.reshape(-1, 8, chunk), axis=0)

        total_ref[:, cols] += loop(crops // per_step, step, jnp.zeros((8, chunk), F32))
    grad_ref[...] += lax.dot_general(h_ref[...], g_ref[...], TN, preferred_element_type=F32)
    back = None
    for part in range(w_ref.shape[0]):
        cols = slice(part * chunk, (part + 1) * chunk)
        term = lax.dot_general(g_ref[:, cols], w_ref[part], NT, preferred_element_type=F32)
        back = term if back is None else back + term
    back_ref[...] = back

    def finish(k, carry):
        g = back_ref[tile_rows(k), :] * gather_tile(slope_ref, k, height)
        store_tile(out_ref, k, g, height)
        return carry[0] + fold(g), carry[1] + fold(g * gather_tile(x_ref, k, height))

    zero = jnp.zeros(sum_ref.shape, F32)
    first, second = loop(h_ref.shape[0] // TILE, finish, (zero, zero))
    sum_ref[...] += first
    dot_ref[...] += second

    @pl.when(pl.program_id(0) == pl.num_programs(0) - 1)
    def _():
        total = jnp.sum(total_ref[...], axis=0, keepdims=True)
        width = centred_ref.shape[1]
        blocks, tiles = grad_ref.shape[1] // width, inner // TILE

        def centre(k, carry):
            at = tile_rows(k)
            centred = (grad_ref[at, :] - mean_ref[at, :] * total).astype(BF16)
            for part in range(centred.shape[1] // width):
                block = (k // tiles * blocks + part) * tiles + k % tiles
                centred_ref[tile_rows(block), :] = centred[:, part * width : (part + 1) * width]
            return carry

        lax.fori_loop(0, grad_ref.shape[0] // TILE, centre, 0, unroll=4)


def third_back(
    hidden, weight, slope_three, mask_flat, scale_rows, beta, gamma, slope_two, pre_two, hidden_mean
):
    height, rows, width = pre_two.shape
    total = height * rows
    channels = weight.shape[0] * weight.shape[2]
    mean = hidden_mean.reshape(width, 1)
    inner = max(TILE, width // device_count())
    tile = 16
    flat = tile * height * 8
    crops = rows // 8
    consts = jnp.concatenate([tall(beta), tall(gamma)], axis=0)
    rows_of = lambda n: pl.BlockSpec((flat, n), lambda k: (k, 0))
    planes = planes_of(height, width, tile * 8)
    grad, sums, out, first, second = kernel_call(
        functools.partial(third_back_body, height, inner),
        crops // tile,
        [
            rows_of(width),
            whole_block(weight),
            rows_of(channels),
            rows_of(1),
            pl.BlockSpec((tile, channels), lambda k: (k, 0)),
            whole_block(consts),
            planes,
            planes,
            whole_block(mean),
        ],
        [
            (jax.ShapeDtypeStruct((channels, width), BF16), pl.BlockSpec((channels, width), lambda k: (0, 0))),
            sum_block(channels),
            (jax.ShapeDtypeStruct(pre_two.shape, F32), planes),
            sum_block(width),
            sum_block(width),
        ],
        [
            pltpu.VMEM((flat, channels), F32),
            pltpu.VMEM((flat, channels), BF16),
            pltpu.VMEM((flat, width), F32),
            pltpu.VMEM((width, channels), F32),
        ],
        (hidden, weight, slope_three, mask_flat, scale_rows, consts, slope_two, pre_two, mean),
        6 * total * width * channels,
    )
    return grad, jnp.sum(sums, axis=0), out, jnp.sum(first, axis=0), jnp.sum(second, axis=0)


def second_back_body(height, g_ref, x_ref, m_ref, c_ref, *refs):
    out_refs, sum_ref = refs[:height], refs[height]
    clear_first(sum_ref)
    for i in range(height):

        def step(k, carry):
            at = tile_rows(k)
            line = c_ref[TILE : 2 * TILE] + c_ref[2 * TILE :] * x_ref[i, at, :]
            g = (c_ref[:TILE] * g_ref[i, at, :] + m_ref[i, at, :] * line).astype(BF16)
            out_refs[i][at, :] = g
            return carry + fold(g.astype(F32))

        sum_ref[...] += loop(g_ref.shape[1] // TILE, step, jnp.zeros(sum_ref.shape, F32))


def second_back(grads, pre_two, mask_planes, alpha, beta, gamma, deps):
    height, rows, width = pre_two.shape
    size = 128
    consts = jnp.concatenate([tall(alpha), tall(beta), tall(gamma)], axis=0)
    block = planes_of(height, width, size)
    *out, sums = kernel_call(
        functools.partial(second_back_body, height),
        rows // size,
        [block, block, planes_of(height, 1, size), whole_block(consts)],
        [plane_out(rows, width, size)] * height + [sum_block(width)],
        [],
        (grads, pre_two, mask_planes, consts),
        10 * pre_two.size,
        deps=deps,
    )
    return out, jnp.sum(sums, axis=0)


def first_back_body(height, g_ref, x_ref, m_ref, c_ref, f_ref, out_ref, grad_ref, total_ref):
    clear_first(total_ref)
    width = out_ref.shape[1]
    per_step = max(1, 2 // height)

    def step(k, carry):
        g = gather_tile(g_ref, k, height)
        x = x_ref[pl.ds(k * per_step, per_step)].reshape(-1, width)
        line = c_ref[TILE : 2 * TILE] + c_ref[2 * TILE :] * x
        out_ref[tile_rows(k), :] = (c_ref[:TILE] * g + m_ref[tile_rows(k), :] * line).astype(BF16)
        return carry

    loop(out_ref.shape[0] // TILE, step, 0)
    last = pl.program_id(0) == pl.num_programs(0) - 1
    for at in range(0, f_ref.shape[1], width):
        part = slice(at, at + width)
        total_ref[part, :] += lax.dot_general(
            f_ref[:, part], out_ref[...], TN, preferred_element_type=F32
        )

    @pl.when(last)
    def _():
        grad_ref[...] = total_ref[...].astype(BF16)


def first_back(grads, pre_one, mask_flat, alpha, beta, gamma, features, deps):
    crops, height, breadth, width = pre_one.shape
    channels = features.shape[1]
    tile = crops // 2
    flat = tile * height * 8
    consts = jnp.concatenate([tall(alpha), tall(beta), tall(gamma)], axis=0)
    return kernel_call(
        functools.partial(first_back_body, height),
        crops // tile,
        [
            planes_of(height, width, tile * 8),
            pl.BlockSpec((tile, height, 8, width), lambda k: (k, 0, 0, 0)),
            rows_block(flat, 1),
            whole_block(consts),
            rows_block(flat, channels),
        ],
        [
            plane_out(crops * height * 8, width, flat),
            (jax.ShapeDtypeStruct((channels, width), BF16), pl.BlockSpec((channels, width), lambda k: (0, 0))),
        ],
        [pltpu.VMEM((channels, width), F32)],
        (grads, pre_one, mask_flat, consts, features),
        2 * crops * height * 8 * width * channels,
        deps=deps,
    )


def last_body(height, g_ref, w_ref, d_ref, s_ref, out_ref, y_ref):
    y_ref[...] = lax.dot_general(g_ref[...], w_ref[...], NT, preferred_element_type=F32)
    pixels = height * 8
    step_rows = max(pixels, TILE)
    per_step = step_rows // pixels
    chunk = 1024
    for part in range(y_ref.shape[1] // chunk):
        cols = slice(part * chunk, (part + 1) * chunk)

        def step(k, carry):
            at = pl.ds(pl.multiple_of(k * step_rows, TILE), step_rows)
            scales = [
                jnp.broadcast_to(s_ref[pl.ds(k * per_step + j, 1), cols], (pixels, chunk))
                for j in range(per_step)
            ]
            scale = scales[0] if per_step == 1 else jnp.concatenate(scales, axis=0)
            out_ref[at, cols] = (y_ref[at, cols] + d_ref[at, cols].astype(F32) * scale).astype(BF16)
            return carry

        loop(s_ref.shape[0] // per_step, step, 0)


def last_grads(grads, weight, slope_three, scale_rows, height, deps):
    total, width = grads.shape
    channels = weight.shape[0]
    tile = 16
    flat = tile * height * 8
    crops = total // (height * 8)
    rows_of = lambda n: pl.BlockSpec((flat, n), lambda k: (k, 0))
    (out,) = kernel_call(
        functools.partial(last_body, height),
        crops // tile,
        [
            rows_of(width),
            whole_block(weight),
            rows_of(channels),
            pl.BlockSpec((tile, channels), lambda k: (k, 0)),
        ],
        [(jax.ShapeDtypeStruct((total, channels), BF16), rows_of(channels))],
        [pltpu.VMEM((flat, channels), F32)],
        (grads, weight, slope_three, scale_rows),
        2 * total * width * channels,
        deps=deps,
    )
    return out


def edge_rows(planes):
    ends = lax.axis_size("rows") - 1
    above = lax.ppermute(planes[-1], "rows", [(i, i + 1) for i in range(ends)])
    below = lax.ppermute(planes[0], "rows", [(i + 1, i) for i in range(ends)])
    return above, below


def back_consts(gain, mean, spread, count, grad_sum, grad_dot):
    grad_gain = spread * (grad_dot - mean * grad_sum)
    alpha = gain * spread
    gamma = -alpha * spread * grad_gain / count
    beta = -alpha * grad_sum / count - gamma * mean
    return alpha, beta, gamma, grad_gain


def shards(
    features,
    pixel_mask,
    partners,
    queued,
    w_reduce,
    w_spatial,
    w_expand,
    w_hidden,
    w_embed,
    prototypes,
    gain_one,
    bias_one,
    gain_two,
    bias_two,
    gain_three,
    bias_three,
    gain_head,
    bias_head,
):
    local_crops, height, breadth, channels = features.shape
    pixels = height * breadth
    narrow = w_reduce.shape[1]
    row_count = lax.axis_size("rows")
    share = local_crops // row_count
    total_crops = local_crops * lax.axis_size("crops")
    full_reduce = gather_first(w_reduce)
    full_spatial, full_expand = gather_pair(w_spatial, w_expand)
    head_whole = lax.all_gather(
        jnp.concatenate([row_quarter(w_hidden), row_quarter(w_embed)], axis=1), BOTH, axis=0, tiled=True
    )
    hidden_cols = w_hidden.shape[1]
    full_hidden, full_embed = head_whole[:, :hidden_cols], head_whole[:, hidden_cols:]

    row_bits = [(0, b) for b in bits_of("rows")]
    crop_count = jnp.sum(pixel_mask.reshape(local_crops, -1), axis=1).astype(F32)
    crop_count = jnp.broadcast_to(crop_count[:, None], (local_crops, 128))
    crop_count = crop_count.reshape((2,) * len(row_bits) + (share, 128))
    for k, step in enumerate(row_bits):
        crop_count = halve(crop_count, len(row_bits) - 1 - k, step, False)
    crop_count = crop_count[:, :1]

    flat_in = features.reshape(-1, channels)
    weight_col = pixel_mask.reshape(-1, 1).astype(F32)
    mask_planes = (
        pixel_mask.transpose(1, 0, 2).reshape(height, local_crops * breadth, 1).astype(F32)
    )

    queue_unit = queued * lax.rsqrt(jnp.sum(queued * queued, axis=1, keepdims=True) + EPS_UNIT)
    queue_scores = jnp.dot(queue_unit, prototypes, precision=PRECISE)
    pre_one = jnp.dot(flat_in, full_reduce, preferred_element_type=F32)
    masked_one = pre_one * weight_col
    sums_one = total_narrow(
        jnp.stack(
            [
                jnp.sum(masked_one, axis=0),
                jnp.sum(masked_one * pre_one, axis=0),
                jnp.full((narrow,), jnp.sum(weight_col)),
            ]
        )
    )
    valid_count = sums_one[2, :1]
    mean_one, spread_one = spread_of(sums_one, valid_count)
    pre_one = pre_one.reshape(local_crops, height, breadth, narrow)
    scale_one = gain_one * spread_one
    hidden_one, slope_one, hidden_sum_one = first_hidden(
        pre_one, mask_planes, scale_one, bias_one - mean_one * scale_one, (queue_scores,)
    )
    above_one, below_one = edge_rows(hidden_one)
    part_two = conv_local(hidden_one, full_spatial, False)
    pre_two, sum_two, square_two = conv_halo(part_two, above_one, below_one, full_spatial, mask_planes)
    sums_two = total_narrow(jnp.stack([sum_two, square_two, hidden_sum_one]))
    mean_two, spread_two = spread_of(sums_two, valid_count)
    hidden_mean_one = sums_two[2] / valid_count
    scale_two = gain_two * spread_two
    hidden_two, slope_two, sum_three, square_three, hidden_sum_two = second_hidden(
        pre_two, weight_col, scale_two, bias_two - mean_two * scale_two, full_expand
    )
    sums_three = total_wide(jnp.concatenate([sum_three, square_three, hidden_sum_two])[None])[0]
    hidden_mean_two = sums_three[2 * channels :] / valid_count
    mean_three, spread_three = spread_of(sums_three[: 2 * channels].reshape(2, -1), valid_count)
    scale_three = gain_three * spread_three
    slope_three, crop_sums, slope_sums = third_output(
        hidden_two, full_expand, flat_in, weight_col, scale_three, bias_three - mean_three * scale_three, height, share
    )
    pooled = crop_sums.reshape((2,) * len(row_bits) + (-1, channels))
    for k, step in enumerate(row_bits):
        pooled = halve(pooled, len(row_bits) - 1 - k, step, False)
    pooled = pooled[:share] / crop_count
    slope_sums = slope_sums.reshape((2,) * len(row_bits) + (-1, 2 * channels))
    for k, step in enumerate(row_bits):
        slope_sums = halve(slope_sums, len(row_bits) - 1 - k, step, False)
    slope_sums = slope_sums[:share]

    pre_head = split_dot(pooled, full_hidden, 0, 3)
    sums_head = total_wide(jnp.stack([jnp.sum(pre_head, axis=0), jnp.sum(pre_head * pre_head, axis=0)]))
    mean_head, spread_head = spread_of(sums_head, F32(total_crops))
    norm_head = (pre_head - mean_head) * spread_head
    hidden_head, slope_head = gelu_both(gain_head * norm_head + bias_head)
    embedding = split_dot(hidden_head, full_embed, 0, 3)
    inverse = lax.rsqrt(jnp.sum(embedding * embedding, axis=1, keepdims=True) + EPS_UNIT)
    unit_embed = embedding * inverse

    partner_rows = (
        lax.dynamic_slice_in_dim(partners, lax.axis_index("rows") * share, share)
        - lax.axis_index("crops") * local_crops
    )
    partner_at = (partner_rows // share ^ lax.axis_index("rows")) * share + partner_rows % share
    row_total = total_crops + queued.shape[0] * lax.axis_size("crops") * row_count
    proto_total = prototypes.shape[1]
    scores = jnp.dot(unit_embed, prototypes, precision=PRECISE)
    plan_mass = jnp.exp(scores / SHARPNESS)
    queue_mass = jnp.exp(queue_scores / SHARPNESS)
    for iteration in range(3):
        column = jnp.sum(plan_mass, axis=0, keepdims=True) + jnp.sum(queue_mass, axis=0, keepdims=True)
        if iteration == 0:
            column, everyone = total_carrying(column, unit_embed)
            partner_embed = jnp.take(everyone, partner_at, axis=0)
            partner_scores = jnp.dot(partner_embed, prototypes, precision=PRECISE)
            partner_mass = jnp.exp(partner_scores / SHARPNESS)
        else:
            column = total_wide(column)
        scale = 1.0 / (proto_total * column)
        partner_mass = partner_mass * scale
        partner_mass = partner_mass / (row_total * jnp.sum(partner_mass, axis=1, keepdims=True))
        if iteration < 2:
            plan_mass = plan_mass * scale
            queue_mass = queue_mass * scale
            plan_mass = plan_mass / (row_total * jnp.sum(plan_mass, axis=1, keepdims=True))
            queue_mass = queue_mass / (row_total * jnp.sum(queue_mass, axis=1, keepdims=True))
    target = row_total * partner_mass
    log_probability = jax.nn.log_softmax(scores / SOFTMAX_TEMPER, axis=1)
    loss_part = -jnp.sum(target * log_probability) / total_crops
    grad_scores = (
        jnp.exp(log_probability) * jnp.sum(target, axis=1, keepdims=True) - target
    ) / (SOFTMAX_TEMPER * total_crops)
    grad_unit = jnp.dot(grad_scores, prototypes.T, precision=PRECISE)
    grad_embedding = inverse * (
        grad_unit - unit_embed * jnp.sum(unit_embed * grad_unit, axis=1, keepdims=True)
    )
    grad_hidden_head = split_dot(grad_embedding, full_embed, 1, 3)
    grad_act_head = grad_hidden_head * slope_head
    sums_back = total_wide(
        jnp.stack(
            [
                jnp.sum(grad_act_head * norm_head, axis=0),
                jnp.sum(grad_act_head, axis=0),
                jnp.full((channels,), loss_part),
            ]
        )
    )
    grad_gain_head, grad_bias_head, swav_loss = sums_back[0], sums_back[1], sums_back[2, 0]
    grad_pre_head = (
        gain_head
        * spread_head
        * (grad_act_head - (grad_bias_head + norm_head * grad_gain_head) / total_crops)
    )
    grad_pooled = split_dot(grad_pre_head, full_hidden, 1, 2)
    per_pixel = grad_pooled / crop_count
    scale_rows = gather_rows(per_pixel)

    crop_index = lax.axis_index("crops")
    proto_pad = -proto_total % 128
    forward_all = gather_products([pooled, hidden_head, unit_embed], True, ())
    backward_all = gather_products(
        [grad_pre_head, grad_embedding, jnp.pad(grad_scores, ((0, 0), (0, proto_pad)))],
        False,
        (slope_sums, forward_all),
    )
    shard_hidden, shard_embed, width = w_hidden.shape[0], w_embed.shape[0], w_embed.shape[1]

    def product_of(at, size, to, count):
        return lax.dot_general(
            lax.dynamic_slice_in_dim(forward_all, at, size, 1),
            lax.slice_in_dim(backward_all, to, to + count, axis=1),
            TN,
            preferred_element_type=F32,
        )

    out_hidden = product_of(crop_index * shard_hidden, shard_hidden, 0, hidden_cols)
    out_embed = product_of(channels + crop_index * shard_embed, shard_embed, hidden_cols, width)
    grad_prototypes = product_of(channels + hidden_cols, width, hidden_cols + width, proto_total)

    sums_three_back = jnp.sum(jnp.concatenate([per_pixel, per_pixel], axis=1) * slope_sums, axis=0)
    sums_three_back = total_wide(sums_three_back[None])[0]
    grad_bias_three = sums_three_back[:channels]
    alpha, beta, gamma, grad_gain_three = back_consts(
        gain_three, mean_three, spread_three, valid_count, grad_bias_three, sums_three_back[channels:]
    )
    grad_w_expand, total_three, grad_act_two, sum_back, dot_back = third_back(
        hidden_two,
        full_expand,
        slope_three,
        weight_col,
        scale_rows * alpha,
        beta,
        gamma,
        slope_two,
        pre_two,
        hidden_mean_two,
    )
    sums_two_back = total_narrow(jnp.stack([sum_back, dot_back]))
    grad_bias_two = sums_two_back[0]
    alpha, beta, gamma, grad_gain_two = back_consts(
        gain_two, mean_two, spread_two, valid_count, grad_bias_two, sums_two_back[1]
    )
    expand_core = core_exchange(grad_w_expand)
    grad_pre_two, total_two = second_back(
        grad_act_two, pre_two, mask_planes, alpha, beta, gamma, (expand_core[0],)
    )
    above_two, below_two = edge_rows(grad_pre_two)
    part_one = conv_local(grad_pre_two, full_spatial, True)
    grad_act_one, sum_back, dot_back = conv_back_halo(
        part_one, above_two, below_two, full_spatial, slope_one, pre_one, ()
    )
    sums_one_back = total_narrow(
        jnp.concatenate([sum_back, dot_back, total_two, total_three]).reshape(-1, narrow)
    )
    grad_w_spatial = spatial_grad(
        hidden_one,
        above_one,
        below_one,
        grad_pre_two,
        hidden_mean_one,
        total_two,
        (grad_act_one,),
    )
    grad_bias_one = sums_one_back[0]
    alpha, beta, gamma, grad_gain_one = back_consts(
        gain_one, mean_one, spread_one, valid_count, grad_bias_one, sums_one_back[1]
    )
    spatial_core = core_exchange(grad_w_spatial, (alpha,))
    blocks = channels // narrow
    spatial_rows, *lane_rows = [
        n // row_count for n in (w_spatial.shape[0], w_reduce.shape[0], blocks * w_expand.shape[0])
    ]
    grad_pre_one, grad_w_reduce = first_back(
        grad_act_one, pre_one, weight_col, alpha, beta, gamma, flat_in, (spatial_core[0],)
    )
    near = near_exchange([spatial_core], [spatial_rows])
    lines = [
        line_exchange(parts, n)
        for parts, n in zip((core_exchange(grad_w_reduce), expand_core), lane_rows)
    ]
    grad_features = last_grads(
        grad_pre_one,
        full_reduce,
        slope_three,
        scale_rows,
        height,
        (out_hidden, out_embed, grad_prototypes, near[0], *[parts[0] for parts in lines]),
    )
    far = far_exchange(near, (grad_features,))
    lane = near_exchange(lines, lane_rows, (grad_features,))
    lane = exchange([lane], reduce_steps()[2][:-1], [sum(lane_rows)])
    out_spatial = reduce_end(far).reshape(w_spatial.shape)
    sums = reduce_end(lane).reshape(row_count, -1, narrow)
    out_reduce = sums[:, : lane_rows[0]].reshape(w_reduce.shape)
    out_expand = sums[:, lane_rows[0] :].reshape(row_count, blocks, -1, narrow)
    out_expand = out_expand.transpose(0, 2, 1, 3).reshape(w_expand.shape)
    grad_features = grad_features.reshape(features.shape)

    grad_totals = sums_one_back[2:].reshape(-1)
    tap_means = jnp.tile(hidden_mean_one, 9)
    shard_expand, shard_spatial = w_expand.shape[0], w_spatial.shape[0]
    means = lax.dynamic_slice_in_dim(hidden_mean_two, crop_index * shard_expand, shard_expand)
    out_expand = out_expand + means[:, None] * grad_totals[narrow:]
    means = lax.dynamic_slice_in_dim(tap_means, crop_index * shard_spatial, shard_spatial)
    out_spatial = out_spatial + means[:, None] * grad_totals[:narrow]
    return (
        swav_loss,
        grad_features,
        out_reduce,
        out_spatial,
        out_expand,
        out_hidden,
        out_embed,
        grad_prototypes,
        grad_gain_one,
        grad_bias_one,
        grad_gain_two,
        grad_bias_two,
        grad_gain_three,
        grad_bias_three,
        grad_gain_head,
        grad_bias_head,
    )


def solution(mesh):
    split = P("crops", None)
    map_spec = P("crops", "rows", None, None)
    in_specs = (
        (map_spec, P("crops", "rows", None), P("crops"), P(BOTH, None)) + (split,) * 5 + (P(),) * 9
    )
    out_specs = (P(), map_spec) + (split,) * 5 + (P(),) * 9
    return jax.shard_map(shards, mesh=mesh, in_specs=in_specs, out_specs=out_specs, check_vma=False)
```
